32 devices in a mesh: ctx: 8 (over z, x), grp: 4 (over y, core).
Axes of the slice: x: 2, y: 2, z: 4, core: 2. Of those that a mesh axis runs over, the one named last changes fastest.
Arguments:
- query: bfloat16 [1024, 8192], P('ctx', 'grp'), may hold values from -6 to 6
- keys: bfloat16 [1024, 8192], P('ctx', 'grp'), may hold values from -6 to 6
- values: bfloat16 [1024, 8192], P('ctx', 'grp'), may hold values from -6 to 6
- cotangent: bfloat16 [1024, 8192], P('ctx', 'grp'), may hold values from -6 to 6
- filter_taps: bfloat16 [64, 384], P('grp'), may hold values from -5 to 5, as said below
Outputs:
- gated: bfloat16 [1024, 8192], P('ctx', 'grp')
- key_grad: bfloat16 [1024, 8192], P('ctx', 'grp')
- value_grad: bfloat16 [1024, 8192], P('ctx', 'grp')
- filter_grad: float32 [64, 384], P('grp')
The draws below stay inside these ranges and needn't reach their ends.
Inputs may be any that keep to these rules, and one draw needn't show every extreme that they name: `filter_taps`: each tap is a random value times a decay along the taps whose length differs from group to group.
All inputs are finite; a program needn't handle non-finite values.
Results may differ from the reference program's by a relative error of at most 0.005.
Values may be sent and summed in bfloat16 or wider, within the bound.
No kernel may reach another device: no remote copies, remote signals or barrier semaphores. Data moves between devices by JAX's collectives and lax.ppermute only.
A program may use at most 64 MiB of HBM per device.

```python
import math
import jax
import jax.numpy as jnp
from jax import lax

D = 8192
GROUP_CH = 128
C = 128
REACH = 3
TOKENS = 1024
GROUPS = 64
TAPS = 384


def draw_filter_taps(key, part):
    first, second = jax.random.split(key)
    spans = jax.random.uniform(first, (GROUPS, 1), jnp.float32, math.log(40.0), math.log(8.0 * TAPS))
    decay = jnp.exp(spans)
    steps = jnp.arange(TAPS).astype(jnp.float32)[None, :]
    total = (1.0 - jnp.exp(-2.0 * TAPS / decay)) / (1.0 - jnp.exp(-2.0 / decay))
    noise = jnp.clip(jax.random.normal(second, (GROUPS, TAPS), jnp.float32), -5.0, 5.0)
    return (noise * jnp.exp(-steps / decay) / jnp.sqrt(total)).astype(jnp.bfloat16)


def block_levels(key, extent, pieces, low, high):
    def one(position, blocks):
        draws = jax.random.uniform(jax.random.fold_in(jax.random.fold_in(key, 6), position), (blocks,), jnp.float32, low / len(pieces), high / len(pieces))
        return jnp.repeat(jnp.exp(draws), extent[position] // blocks).reshape((-1,) + (1,) * (len(extent) - position - 1))

    loudness = one(*pieces[0])
    for cut in pieces[1:]:
        loudness = loudness * one(*cut)
    return loudness


def centred(own_key, extent, scale, limit, pieces=(), kind=jnp.bfloat16):
    drawn = jax.random.normal(own_key, extent, jnp.float32) * scale
    if len(pieces) > 0:
        drawn = block_levels(own_key, extent, pieces, -0.22, 0.18) * drawn
    return jnp.clip(drawn, min=-limit, max=limit).astype(kind)


def setup_inputs(seed: int = 0) -> dict:
    streams_of = jax.random.split(jax.random.key(seed), 6)
    query = centred(streams_of[0], (TOKENS, D), 1.0, 6.0, ((0, 8), (1, 4)))
    keys = centred(streams_of[1], (TOKENS, D), 1.0, 6.0, ((0, 8), (1, 4)))
    values = centred(streams_of[2], (TOKENS, D), 1.0, 6.0, ((0, 8), (1, 4)))
    cotangent = centred(streams_of[3], (TOKENS, D), 1.0, 6.0, ((0, 8), (1, 4)))
    filter_taps = draw_filter_taps(jax.random.fold_in(streams_of[5], 71), 0)
    return dict(query=query, keys=keys, values=values, cotangent=cotangent, filter_taps=filter_taps)


def reference(query, keys, values, cotangent, filter_taps):
    blocks = TOKENS // C
    fsize = 4 * C
    prod = (keys.astype(jnp.float32) * values.astype(jnp.float32)).astype(jnp.bfloat16)
    grad_gate = (cotangent.astype(jnp.float32) * query.astype(jnp.float32)).astype(jnp.bfloat16)

    def grouped(array):
        return array.astype(jnp.float32).reshape(blocks, C, GROUPS, GROUP_CH).transpose(2, 0, 1, 3)

    def ungrouped(array):
        return array.transpose(1, 2, 0, 3).reshape(TOKENS, D)

    def one_group(items):
        source, grads, taps = items
        padded = jnp.concatenate([jnp.zeros((C,), jnp.float32), taps])
        forward_sum = jnp.zeros_like(source)
        backward_sum = jnp.zeros_like(source)
        filter_acc = jnp.zeros(((REACH + 1) * C,), jnp.float32)
        grad_spec = jnp.fft.rfft(grads, fsize, axis=1)
        for distance in range(min(REACH, blocks)):
            kernel = padded[distance * C:(distance + 2) * C]
            kspec = jnp.fft.rfft(kernel, fsize)[None, :, None]
            early = jnp.concatenate([jnp.zeros((distance, C, GROUP_CH), jnp.float32), source[:blocks - distance]], axis=0)
            late = jnp.concatenate([grads[distance:], jnp.zeros((distance, C, GROUP_CH), jnp.float32)], axis=0)
            early_spec = jnp.fft.rfft(early, fsize, axis=1)
            forward_sum = forward_sum + jnp.fft.irfft(kspec * early_spec, fsize, axis=1)[:, C:2 * C]
            mirrored = jnp.fft.rfft(late[:, ::-1], fsize, axis=1)
            backward_sum = backward_sum + jnp.fft.irfft(kspec * mirrored, fsize, axis=1)[:, C:2 * C][:, ::-1]
            cross = lax.optimization_barrier(jnp.sum(grad_spec * jnp.conj(early_spec), axis=(0, 2)))
            corr = jnp.fft.irfft(cross, fsize)
            diagonal = jnp.concatenate([corr[fsize - C:], corr[:C]])
            filter_acc = filter_acc.at[distance * C:(distance + 2) * C].add(diagonal)
        return (forward_sum, backward_sum, filter_acc[C:])
    convolved, backward, filter_sum = lax.map(one_group, (grouped(prod), grouped(grad_gate), filter_taps.astype(jnp.float32)))
    convolved = ungrouped(convolved)
    backward = ungrouped(backward)
    gated = (query.astype(jnp.float32) * convolved).astype(jnp.bfloat16)
    key_grad = (backward * values.astype(jnp.float32)).astype(jnp.bfloat16)
    value_grad = (backward * keys.astype(jnp.float32)).astype(jnp.bfloat16)
    filter_grad = filter_sum / jnp.sqrt(jnp.float32(TOKENS * GROUP_CH))
    return (gated, key_grad, value_grad, filter_grad)
```

```python
import functools
import math

import jax
import jax.numpy as jnp
from jax import lax
from jax.experimental import pallas as pl
from jax.experimental.pallas import tpu as pltpu
from jax.sharding import PartitionSpec as P

SUBLANES = 8
VMEM_LIMIT = 32 * 1024 * 1024


def shifted(block, axis, distance):
    devices = range(lax.axis_size(axis))
    route = [(i - distance, i) for i in devices if i - distance in devices]
    return lax.ppermute(block, axis, route)


def summed(partial, axis):
    size = lax.axis_size(axis)
    if size & (size - 1):
        return lax.psum(partial, axis)
    stride = 1
    while stride < size:
        route = [(i, i ^ stride) for i in range(size)]
        partial = partial + lax.ppermute(partial, axis, route)
        stride *= 2
    return partial


def tiles_kernel(rows, reach, taps_ref, back_ref, conv_ref):
    width = reach * rows
    for group in range(taps_ref.shape[0]):
        row = taps_ref[group : group + 1, :].astype(jnp.float32)
        spread = jnp.concatenate(
            [jnp.zeros((SUBLANES, rows), jnp.float32), jnp.broadcast_to(row, (SUBLANES, width))],
            axis=1,
        )
        spread = pltpu.roll(spread, 0, 1, stride=1, stride_axis=0)
        bands = [
            pltpu.roll(spread, start, 1)[:, rows:] if start else spread[:, rows:]
            for start in range(0, rows, SUBLANES)
        ]
        band = jnp.concatenate(bands, axis=0)
        back_ref[group] = band.astype(jnp.bfloat16)
        turned = [band[:, d * rows : (d + 1) * rows].T for d in range(reach)]
        conv_ref[group] = jnp.concatenate(turned, axis=1).astype(jnp.bfloat16)


def taps_kernel(rows, reach, factor, prod_ref, early_ref, grad_ref, late_ref, out_ref):
    width = reach * rows
    contract = (((1,), (1,)), ((), ()))
    group_count = out_ref.shape[0]
    group_width = prod_ref.shape[1] // group_count
    sums = []
    for group in range(group_count):
        columns = slice(group * group_width, (group + 1) * group_width)
        prod = prod_ref[:, columns]
        grad = grad_ref[:, columns]
        dot = functools.partial(
            lax.dot_general, dimension_numbers=contract, preferred_element_type=jnp.float32
        )
        near = dot(prod, grad)
        middle = dot(early_ref[:, columns], grad)
        far = dot(prod, late_ref[:, columns])
        outer = jnp.concatenate([near, middle, far, jnp.zeros((rows, rows), jnp.float32)], axis=1)
        total = outer[:SUBLANES]
        for start in range(SUBLANES, rows, SUBLANES):
            total = total + pltpu.roll(
                outer[start : start + SUBLANES], width + rows - start, 1
            )
        total = jnp.concatenate(
            [pltpu.roll(total[s : s + 1], (width + rows - s) % (width + rows), 1) for s in range(SUBLANES)],
            axis=0,
        )
        sums.append(jnp.sum(total, axis=0, keepdims=True)[:, :width])
    out_ref[...] = jnp.concatenate(sums, axis=0) * factor


def outputs_kernel(
    rows, group_width, conv_ref, back_ref, p0, p1, p2, g0, g1, g2, query, keys, values, gated, key_grad, value_grad
):
    for group in range(conv_ref.shape[0]):
        columns = slice(group * group_width, (group + 1) * group_width)
        early = jnp.concatenate([ref[:, columns] for ref in (p0, p1, p2)], axis=0)
        late = jnp.concatenate([ref[:, columns] for ref in (g0, g1, g2)], axis=0)
        convolved = jnp.dot(conv_ref[group], early, preferred_element_type=jnp.float32)
        backward = jnp.dot(back_ref[group], late, preferred_element_type=jnp.float32)
        gated[:, columns] = (query[:, columns].astype(jnp.float32) * convolved).astype(gated.dtype)
        key_grad[:, columns] = (backward * values[:, columns].astype(jnp.float32)).astype(key_grad.dtype)
        value_grad[:, columns] = (backward * keys[:, columns].astype(jnp.float32)).astype(value_grad.dtype)


def shards(query, keys, values, cotangent, filter_taps):
    rows, local_width = query.shape
    group_count, taps = filter_taps.shape
    group_width = local_width // group_count
    reach = taps // rows
    params = pltpu.CompilerParams(vmem_limit_bytes=VMEM_LIMIT)
    step = min(group_count, 8)
    grid = (group_count // step,)

    prod = (keys.astype(jnp.float32) * values.astype(jnp.float32)).astype(jnp.bfloat16)
    p1 = shifted(prod, "ctx", 1)
    grad_gate = (cotangent.astype(jnp.float32) * query.astype(jnp.float32)).astype(jnp.bfloat16)
    g2 = shifted(grad_gate, "ctx", -2)

    tile_shape = jax.ShapeDtypeStruct((group_count, rows, taps), jnp.bfloat16)
    tile_spec = pl.BlockSpec((step, rows, taps), lambda i: (i, 0, 0))
    taps_spec = pl.BlockSpec((step, taps), lambda i: (i, 0))
    block_spec = pl.BlockSpec((rows, step * group_width), lambda i: (0, i))
    back_tiles, conv_tiles = pl.pallas_call(
        functools.partial(tiles_kernel, rows, reach),
        grid=grid,
        in_specs=[taps_spec],
        out_specs=[tile_spec, tile_spec],
        out_shape=[tile_shape, tile_shape],
        compiler_params=params,
        cost_estimate=pl.CostEstimate(flops=10**9, bytes_accessed=10**7, transcendentals=0),
        name="tiles",
    )(filter_taps)

    p1, g2, late_p, late_g = lax.optimization_barrier((p1, g2, prod, grad_gate))
    p2 = shifted(late_p, "ctx", 2)
    g1 = shifted(late_g, "ctx", -1)

    factor = 1.0 / math.sqrt(rows * lax.axis_size("ctx") * group_width)
    partial = pl.pallas_call(
        functools.partial(taps_kernel, rows, reach, factor),
        grid=grid,
        in_specs=[block_spec] * 4,
        out_specs=taps_spec,
        out_shape=jax.ShapeDtypeStruct((group_count, taps), jnp.float32),
        compiler_params=params,
        cost_estimate=pl.CostEstimate(flops=10**9, bytes_accessed=10**7, transcendentals=0),
        name="taps",
    )(prod, p1, grad_gate, g2)
    filter_grad = summed(partial, "ctx")

    out_shape = jax.ShapeDtypeStruct((rows, local_width), jnp.bfloat16)
    gated, key_grad, value_grad = pl.pallas_call(
        functools.partial(outputs_kernel, rows, group_width),
        grid=grid,
        in_specs=[tile_spec, tile_spec] + [block_spec] * 9,
        out_specs=[block_spec] * 3,
        out_shape=[out_shape] * 3,
        compiler_params=params,
        cost_estimate=pl.CostEstimate(flops=10**9, bytes_accessed=10**7, transcendentals=0),
        name="outputs",
    )(conv_tiles, back_tiles, prod, p1, p2, grad_gate, g1, g2, query, keys, values)
    return (gated, key_grad, value_grad, filter_grad)


def solution(mesh):
    in_specs = (P("ctx", "grp"), P("ctx", "grp"), P("ctx", "grp"), P("ctx", "grp"), P("grp", None))
    out_specs = (P("ctx", "grp"), P("ctx", "grp"), P("ctx", "grp"), P("grp", None))
    return jax.shard_map(shards, mesh=mesh, in_specs=in_specs, out_specs=out_specs, check_vma=False)
```

```python
import functools
import math

import jax
import jax.numpy as jnp
from jax import lax
from jax.experimental import pallas as pl
from jax.experimental.pallas import tpu as pltpu
from jax.sharding import PartitionSpec as P

SUBLANES = 8
VMEM_LIMIT = 32 * 1024 * 1024


def shifted(block, axis, distance):
    devices = range(lax.axis_size(axis))
    route = [(i - distance, i) for i in devices if i - distance in devices]
    return lax.ppermute(block, axis, route)


def summed(partial, axis):
    return jnp.sum(lax.all_gather(partial, axis), axis=0)


def tiles_kernel(rows, reach, taps_ref, back_ref, conv_ref):
    width = reach * rows
    for group in range(taps_ref.shape[0]):
        row = taps_ref[group : group + 1, :].astype(jnp.float32)
        spread = jnp.concatenate(
            [jnp.zeros((SUBLANES, rows), jnp.float32), jnp.broadcast_to(row, (SUBLANES, width))],
            axis=1,
        )
        spread = pltpu.roll(spread, 0, 1, stride=1, stride_axis=0)
        bands = [
            pltpu.roll(spread, start, 1)[:, rows:] if start else spread[:, rows:]
            for start in range(0, rows, SUBLANES)
        ]
        band = jnp.concatenate(bands, axis=0)
        back_ref[group] = band.astype(jnp.bfloat16)
        turned = [band[:, d * rows : (d + 1) * rows].T for d in range(reach)]
        conv_ref[group] = jnp.concatenate(turned, axis=1).astype(jnp.bfloat16)


def taps_kernel(rows, reach, factor, prod_ref, early_ref, grad_ref, late_ref, out_ref):
    width = reach * rows
    contract = (((1,), (1,)), ((), ()))
    group_count = out_ref.shape[0]
    group_width = prod_ref.shape[1] // group_count
    sums = []
    for group in range(group_count):
        columns = slice(group * group_width, (group + 1) * group_width)
        prod = prod_ref[:, columns]
        grad = grad_ref[:, columns]
        dot = functools.partial(
            lax.dot_general, dimension_numbers=contract, preferred_element_type=jnp.float32
        )
        near = dot(prod, grad)
        middle = dot(early_ref[:, columns], grad)
        far = dot(prod, late_ref[:, columns])
        outer = jnp.concatenate([near, middle, far, jnp.zeros((rows, rows), jnp.float32)], axis=1)
        total = outer[:SUBLANES]
        for start in range(SUBLANES, rows, SUBLANES):
            total = total + pltpu.roll(
                outer[start : start + SUBLANES], width + rows - start, 1
            )
        total = jnp.concatenate(
            [pltpu.roll(total[s : s + 1], (width + rows - s) % (width + rows), 1) for s in range(SUBLANES)],
            axis=0,
        )
        sums.append(jnp.sum(total, axis=0, keepdims=True)[:, :width])
    out_ref[...] = jnp.concatenate(sums, axis=0) * factor


def outputs_kernel(
    rows, group_width, conv_ref, back_ref, p0, p1, p2, g0, g1, g2, query, keys, values, gated, key_grad, value_grad
):
    for group in range(conv_ref.shape[0]):
        columns = slice(group * group_width, (group + 1) * group_width)
        early = jnp.concatenate([ref[:, columns] for ref in (p0, p1, p2)], axis=0)
        late = jnp.concatenate([ref[:, columns] for ref in (g0, g1, g2)], axis=0)
        convolved = jnp.dot(conv_ref[group], early, preferred_element_type=jnp.float32)
        backward = jnp.dot(back_ref[group], late, preferred_element_type=jnp.float32)
        gated[:, columns] = (query[:, columns].astype(jnp.float32) * convolved).astype(gated.dtype)
        key_grad[:, columns] = (backward * values[:, columns].astype(jnp.float32)).astype(key_grad.dtype)
        value_grad[:, columns] = (backward * keys[:, columns].astype(jnp.float32)).astype(value_grad.dtype)


def shards(query, keys, values, cotangent, filter_taps):
    rows, local_width = query.shape
    group_count, taps = filter_taps.shape
    group_width = local_width // group_count
    reach = taps // rows
    params = pltpu.CompilerParams(vmem_limit_bytes=VMEM_LIMIT)
    step = min(group_count, 8)
    grid = (group_count // step,)

    prod = (keys.astype(jnp.float32) * values.astype(jnp.float32)).astype(jnp.bfloat16)
    p1 = shifted(prod, "ctx", 1)
    grad_gate = (cotangent.astype(jnp.float32) * query.astype(jnp.float32)).astype(jnp.bfloat16)
    g2 = shifted(grad_gate, "ctx", -2)

    tile_shape = jax.ShapeDtypeStruct((group_count, rows, taps), jnp.bfloat16)
    tile_spec = pl.BlockSpec((step, rows, taps), lambda i: (i, 0, 0))
    taps_spec = pl.BlockSpec((step, taps), lambda i: (i, 0))
    block_spec = pl.BlockSpec((rows, step * group_width), lambda i: (0, i))
    back_tiles, conv_tiles = pl.pallas_call(
        functools.partial(tiles_kernel, rows, reach),
        grid=grid,
        in_specs=[taps_spec],
        out_specs=[tile_spec, tile_spec],
        out_shape=[tile_shape, tile_shape],
        compiler_params=params,
        cost_estimate=pl.CostEstimate(flops=10**9, bytes_accessed=10**7, transcendentals=0),
        name="tiles",
    )(filter_taps)

    g1 = shifted(grad_gate, "ctx", -1)
    p2 = shifted(prod, "ctx", 2)

    back_tiles, conv_tiles, ready = lax.optimization_barrier((back_tiles, conv_tiles, grad_gate))
    factor = 1.0 / math.sqrt(rows * lax.axis_size("ctx") * group_width)
    partial = pl.pallas_call(
        functools.partial(taps_kernel, rows, reach, factor),
        grid=grid,
        in_specs=[block_spec] * 4,
        out_specs=taps_spec,
        out_shape=jax.ShapeDtypeStruct((group_count, taps), jnp.float32),
        compiler_params=params,
        cost_estimate=pl.CostEstimate(flops=10**9, bytes_accessed=10**7, transcendentals=0),
        name="taps",
    )(prod, p1, ready, g2)
    filter_grad = summed(partial, "ctx")

    out_shape = jax.ShapeDtypeStruct((rows, local_width), jnp.bfloat16)
    gated, key_grad, value_grad = pl.pallas_call(
        functools.partial(outputs_kernel, rows, group_width),
        grid=grid,
        in_specs=[tile_spec, tile_spec] + [block_spec] * 9,
        out_specs=[block_spec] * 3,
        out_shape=[out_shape] * 3,
        compiler_params=params,
        cost_estimate=pl.CostEstimate(flops=10**9, bytes_accessed=10**7, transcendentals=0),
        name="outputs",
    )(conv_tiles, back_tiles, prod, p1, p2, grad_gate, g1, g2, query, keys, values)
    return (gated, key_grad, value_grad, filter_grad)


def solution(mesh):
    in_specs = (P("ctx", "grp"), P("ctx", "grp"), P("ctx", "grp"), P("ctx", "grp"), P("grp", None))
    out_specs = (P("ctx", "grp"), P("ctx", "grp"), P("ctx", "grp"), P("grp", None))
    return jax.shard_map(shards, mesh=mesh, in_specs=in_specs, out_specs=out_specs, check_vma=False)
```

```python
import functools
import math

import jax
import jax.numpy as jnp
from jax import lax
from jax.experimental import pallas as pl
from jax.experimental.pallas import tpu as pltpu
from jax.sharding import PartitionSpec as P

SUBLANES = 8
VMEM_LIMIT = 32 * 1024 * 1024


def shifted(block, axis, distance):
    devices = range(lax.axis_size(axis))
    route = [(i - distance, i) for i in devices if i - distance in devices]
    return lax.ppermute(block, axis, route)


def summed(partial, axis):
    copies = jnp.broadcast_to(partial[None], (lax.axis_size(axis), *partial.shape))
    return jnp.sum(lax.all_to_all(copies, axis, 0, 0), axis=0)


def tiles_kernel(rows, reach, taps_ref, back_ref, conv_ref):
    width = reach * rows
    for group in range(taps_ref.shape[0]):
        row = taps_ref[group : group + 1, :].astype(jnp.float32)
        spread = jnp.concatenate(
            [jnp.zeros((SUBLANES, rows), jnp.float32), jnp.broadcast_to(row, (SUBLANES, width))],
            axis=1,
        )
        spread = pltpu.roll(spread, 0, 1, stride=1, stride_axis=0)
        bands = [
            pltpu.roll(spread, start, 1)[:, rows:] if start else spread[:, rows:]
            for start in range(0, rows, SUBLANES)
        ]
        band = jnp.concatenate(bands, axis=0)
        back_ref[group] = band.astype(jnp.bfloat16)
        turned = [band[:, d * rows : (d + 1) * rows].T for d in range(reach)]
        conv_ref[group] = jnp.concatenate(turned, axis=1).astype(jnp.bfloat16)


def taps_kernel(rows, reach, factor, prod_ref, early_ref, grad_ref, late_ref, out_ref):
    width = reach * rows
    contract = (((1,), (1,)), ((), ()))
    group_count = out_ref.shape[0]
    group_width = prod_ref.shape[1] // group_count
    sums = []
    for group in range(group_count):
        columns = slice(group * group_width, (group + 1) * group_width)
        prod = prod_ref[:, columns]
        grad = grad_ref[:, columns]
        dot = functools.partial(
            lax.dot_general, dimension_numbers=contract, preferred_element_type=jnp.float32
        )
        near = dot(prod, grad)
        middle = dot(early_ref[:, columns], grad)
        far = dot(prod, late_ref[:, columns])
        outer = jnp.concatenate([near, middle, far, jnp.zeros((rows, rows), jnp.float32)], axis=1)
        total = outer[:SUBLANES]
        for start in range(SUBLANES, rows, SUBLANES):
            total = total + pltpu.roll(
                outer[start : start + SUBLANES], width + rows - start, 1
            )
        total = jnp.concatenate(
            [pltpu.roll(total[s : s + 1], (width + rows - s) % (width + rows), 1) for s in range(SUBLANES)],
            axis=0,
        )
        sums.append(jnp.sum(total, axis=0, keepdims=True)[:, :width])
    out_ref[...] = jnp.concatenate(sums, axis=0) * factor


def outputs_kernel(
    rows, group_width, conv_ref, back_ref, p0, p1, p2, g0, g1, g2, query, keys, values, gated, key_grad, value_grad
):
    for group in range(conv_ref.shape[0]):
        columns = slice(group * group_width, (group + 1) * group_width)
        early = jnp.concatenate([ref[:, columns] for ref in (p0, p1, p2)], axis=0)
        late = jnp.concatenate([ref[:, columns] for ref in (g0, g1, g2)], axis=0)
        convolved = jnp.dot(conv_ref[group], early, preferred_element_type=jnp.float32)
        backward = jnp.dot(back_ref[group], late, preferred_element_type=jnp.float32)
        gated[:, columns] = (query[:, columns].astype(jnp.float32) * convolved).astype(gated.dtype)
        key_grad[:, columns] = (backward * values[:, columns].astype(jnp.float32)).astype(key_grad.dtype)
        value_grad[:, columns] = (backward * keys[:, columns].astype(jnp.float32)).astype(value_grad.dtype)


def shards(query, keys, values, cotangent, filter_taps):
    rows, local_width = query.shape
    group_count, taps = filter_taps.shape
    group_width = local_width // group_count
    reach = taps // rows
    params = pltpu.CompilerParams(vmem_limit_bytes=VMEM_LIMIT)
    step = min(group_count, 8)
    grid = (group_count // step,)

    prod = (keys.astype(jnp.float32) * values.astype(jnp.float32)).astype(jnp.bfloat16)
    p1 = shifted(prod, "ctx", 1)
    grad_gate = (cotangent.astype(jnp.float32) * query.astype(jnp.float32)).astype(jnp.bfloat16)
    g2 = shifted(grad_gate, "ctx", -2)

    tile_shape = jax.ShapeDtypeStruct((group_count, rows, taps), jnp.bfloat16)
    tile_spec = pl.BlockSpec((step, rows, taps), lambda i: (i, 0, 0))
    taps_spec = pl.BlockSpec((step, taps), lambda i: (i, 0))
    block_spec = pl.BlockSpec((rows, step * group_width), lambda i: (0, i))
    back_tiles, conv_tiles = pl.pallas_call(
        functools.partial(tiles_kernel, rows, reach),
        grid=grid,
        in_specs=[taps_spec],
        out_specs=[tile_spec, tile_spec],
        out_shape=[tile_shape, tile_shape],
        compiler_params=params,
        cost_estimate=pl.CostEstimate(flops=10**9, bytes_accessed=10**7, transcendentals=0),
        name="tiles",
    )(filter_taps)

    g1 = shifted(grad_gate, "ctx", -1)
    p2 = shifted(prod, "ctx", 2)

    factor = 1.0 / math.sqrt(rows * lax.axis_size("ctx") * group_width)
    partial = pl.pallas_call(
        functools.partial(taps_kernel, rows, reach, factor),
        grid=grid,
        in_specs=[block_spec] * 4,
        out_specs=taps_spec,
        out_shape=jax.ShapeDtypeStruct((group_count, taps), jnp.float32),
        compiler_params=params,
        cost_estimate=pl.CostEstimate(flops=10**9, bytes_accessed=10**7, transcendentals=0),
        name="taps",
    )(prod, p1, grad_gate, g2)
    filter_grad = summed(partial, "ctx")

    out_shape = jax.ShapeDtypeStruct((rows, local_width), jnp.bfloat16)
    gated, key_grad, value_grad = pl.pallas_call(
        functools.partial(outputs_kernel, rows, group_width),
        grid=grid,
        in_specs=[tile_spec, tile_spec] + [block_spec] * 9,
        out_specs=[block_spec] * 3,
        out_shape=[out_shape] * 3,
        compiler_params=params,
        cost_estimate=pl.CostEstimate(flops=10**9, bytes_accessed=10**7, transcendentals=0),
        name="outputs",
    )(conv_tiles, back_tiles, prod, p1, p2, grad_gate, g1, g2, query, keys, values)
    return (gated, key_grad, value_grad, filter_grad)


def solution(mesh):
    in_specs = (P("ctx", "grp"), P("ctx", "grp"), P("ctx", "grp"), P("ctx", "grp"), P("grp", None))
    out_specs = (P("ctx", "grp"), P("ctx", "grp"), P("ctx", "grp"), P("grp", None))
    return jax.shard_map(shards, mesh=mesh, in_specs=in_specs, out_specs=out_specs, check_vma=False)
```

```python
import functools
import math

import jax
import jax.numpy as jnp
from jax import lax
from jax.experimental import pallas as pl
from jax.experimental.pallas import tpu as pltpu
from jax.sharding import PartitionSpec as P

SUBLANES = 8
VMEM_LIMIT = 32 * 1024 * 1024
WHOLE = pl.BlockSpec(memory_space=pltpu.VMEM)


def moved(block, axis, distances):
    size = lax.axis_size(axis)
    route = [(i, i + distances[i % 2]) for i in range(size)]
    return lax.ppermute(block, axis, [pair for pair in route if 0 <= pair[1] < size])


def tiles_kernel(rows, reach, taps_ref, back_ref, conv_ref):
    width = reach * rows
    for group in range(taps_ref.shape[0]):
        row = taps_ref[group : group + 1, :].astype(jnp.float32)
        spread = jnp.concatenate(
            [jnp.zeros((SUBLANES, rows), jnp.float32), jnp.broadcast_to(row, (SUBLANES, width))],
            axis=1,
        )
        spread = pltpu.roll(spread, 0, 1, stride=1, stride_axis=0)
        bands = [
            pltpu.roll(spread, start, 1)[:, rows:] if start else spread[:, rows:]
            for start in range(0, rows, SUBLANES)
        ]
        band = jnp.concatenate(bands, axis=0)
        back_ref[group] = band.astype(jnp.bfloat16)
        turned = [band[:, d * rows : (d + 1) * rows].T for d in range(reach)]
        conv_ref[group] = jnp.concatenate(turned, axis=1).astype(jnp.bfloat16)


def skewed_sum(outer, rows):
    width = outer.shape[1]
    total = outer[:SUBLANES]
    for start in range(SUBLANES, rows, SUBLANES):
        total = total + pltpu.roll(outer[start : start + SUBLANES], width - start, 1)
    lines = [total[:1]] + [pltpu.roll(total[s : s + 1], width - s, 1) for s in range(1, SUBLANES)]
    return functools.reduce(jnp.add, lines)


DOT_ROWS = functools.partial(
    lax.dot_general,
    dimension_numbers=(((1,), (1,)), ((), ())),
    preferred_element_type=jnp.float32,
)


def most_taps_kernel(rows, even_ref, odd_ref, diagonal_ref, two_ref, out_ref):
    odd = lax.rem(lax.axis_index("ctx"), 2) == 1
    group_count, width = out_ref.shape
    group_width = even_ref.shape[1] // group_count
    half = group_count // 2

    def columns(group):
        return slice(group * group_width, (group + 1) * group_width)

    def held(ref, group):
        return ref[:, columns(group)]

    middles = []
    for group in range(half):
        across = lax.select(odd, held(diagonal_ref, group + half), held(diagonal_ref, group))
        own = lax.select(odd, held(odd_ref, group + half), held(odd_ref, group))
        middles.append(DOT_ROWS(lax.select(odd, own, across), lax.select(odd, across, own)))
    blank = jnp.zeros((rows, rows), jnp.float32)
    sums = []
    for group in range(group_count):
        near = DOT_ROWS(
            lax.select(odd, held(odd_ref, group), held(even_ref, group)),
            lax.select(odd, held(even_ref, group), held(odd_ref, group)),
        )
        far = DOT_ROWS(
            lax.select(odd, held(odd_ref, group), held(two_ref, group)),
            lax.select(odd, held(two_ref, group), held(odd_ref, group)),
        )
        if group < half:
            middle = lax.select(odd, blank, middles[group])
        else:
            middle = lax.select(odd, middles[group - half], blank)
        outer = jnp.concatenate([near, middle, far, blank], axis=1)
        sums.append(skewed_sum(outer, rows)[:, :width])
    out_ref[...] = jnp.concatenate(sums, axis=0)


def last_taps_kernel(rows, factor, partial_ref, even_ref, first_ref, out_ref):
    odd = lax.rem(lax.axis_index("ctx"), 2) == 1
    copies, group_count, width = out_ref.shape
    group_width = even_ref.shape[1] // group_count
    half = group_count // 2
    blank = jnp.zeros((rows, rows), jnp.float32)
    sums = []
    for group in range(half):
        columns = slice(group * group_width, (group + 1) * group_width)
        other = slice((group + half) * group_width, (group + half + 1) * group_width)
        own = lax.select(odd, even_ref[:, columns], even_ref[:, other])
        across = first_ref[:, columns]
        outer = DOT_ROWS(lax.select(odd, across, own), lax.select(odd, own, across))
        sums.append(skewed_sum(jnp.concatenate([blank, outer], axis=1), rows))
    rest = jnp.concatenate(
        [jnp.concatenate(sums, axis=0), jnp.zeros((half, width - 2 * rows), jnp.float32)], axis=1
    )
    low = partial_ref[:half] + lax.select(odd, rest, jnp.zeros_like(rest))
    high = partial_ref[half:] + lax.select(odd, jnp.zeros_like(rest), rest)
    for copy in range(copies):
        out_ref[copy, :half] = low * factor
        out_ref[copy, half:] = high * factor


def outputs_kernel(
    conv_ref, back_ref, even_ref, odd_ref, diagonal_ref, two_ref, first_ref, far_ref, last_ref,
    query_ref, keys_ref, values_ref, gated_out, key_out, value_out, gated, key_grad, value_grad, sems,
):
    odd = lax.rem(lax.axis_index("ctx"), 2) == 1
    group_count = conv_ref.shape[0]
    group_width = even_ref.shape[1] // group_count
    half = group_count // 2
    step = max(1, group_count // 4)
    copies = []
    for group in range(group_count):
        columns = slice(group * group_width, (group + 1) * group_width)
        inner = slice((group % half) * group_width, (group % half + 1) * group_width)
        diagonal = diagonal_ref[:, columns]
        first = first_ref[:, inner]
        last = last_ref[:, inner]
        even_kept, odd_kept = even_ref[:, columns], odd_ref[:, columns]
        two, far = two_ref[:, columns], far_ref[:, columns]
        low = group < half
        early = [
            lax.select(odd, odd_kept, even_kept),
            lax.select(odd, first if low else last, diagonal),
            lax.select(odd, far, two),
        ]
        late = [
            lax.select(odd, even_kept, odd_kept),
            lax.select(odd, diagonal, last if low else first),
            lax.select(odd, two, far),
        ]
        convolved = jnp.dot(
            conv_ref[group], jnp.concatenate(early, axis=0), preferred_element_type=jnp.float32
        )
        backward = jnp.dot(
            back_ref[group], jnp.concatenate(late, axis=0), preferred_element_type=jnp.float32
        )
        gated[:, columns] = (query_ref[:, columns].astype(jnp.float32) * convolved).astype(gated.dtype)
        key_grad[:, columns] = (backward * values_ref[:, columns].astype(jnp.float32)).astype(key_grad.dtype)
        value_grad[:, columns] = (backward * keys_ref[:, columns].astype(jnp.float32)).astype(value_grad.dtype)
        if (group + 1) % step == 0:
            part = pl.ds((group + 1 - step) * group_width, step * group_width)
            for kept, out in ((gated, gated_out), (key_grad, key_out), (value_grad, value_out)):
                copy = pltpu.make_async_copy(kept.at[:, part], out.at[:, part], sems.at[len(copies)])
                copy.start()
                copies.append(copy)
    for copy in copies:
        copy.wait()


def shards(query, keys, values, cotangent, filter_taps):
    rows, local_width = query.shape
    group_count, taps = filter_taps.shape
    group_width = local_width // group_count
    reach = taps // rows
    size = lax.axis_size("ctx")
    odd = lax.axis_index("ctx") % 2 == 1
    half = local_width // 2
    params = pltpu.CompilerParams(vmem_limit_bytes=VMEM_LIMIT)
    cost = pl.CostEstimate(flops=5 * 10**8, bytes_accessed=8 * 10**6, transcendentals=0)

    prod = (keys.astype(jnp.float32) * values.astype(jnp.float32)).astype(jnp.bfloat16)
    grad = (cotangent.astype(jnp.float32) * query.astype(jnp.float32)).astype(jnp.bfloat16)
    odd_kept = jnp.where(odd, prod, grad)
    diagonal = moved(odd_kept, "ctx", (-1, 1))
    even_kept = jnp.where(odd, grad, prod)
    two = moved(even_kept, "ctx", (2, -2))
    first = moved(jnp.where(odd, grad[:, half:], prod[:, :half]), "ctx", (1, -1))
    far = moved(odd_kept, "ctx", (-2, 2))
    last = moved(jnp.where(odd, grad[:, :half], prod[:, half:]), "ctx", (1, -1))

    step = min(group_count, 8)
    tile_shape = jax.ShapeDtypeStruct((group_count, rows, taps), jnp.bfloat16)
    tile_spec = pl.BlockSpec((step, rows, taps), lambda i: (i, 0, 0))
    back_tiles, conv_tiles = pl.pallas_call(
        functools.partial(tiles_kernel, rows, reach),
        grid=(group_count // step,),
        in_specs=[pl.BlockSpec((step, taps), lambda i: (i, 0))],
        out_specs=[tile_spec, tile_spec],
        out_shape=[tile_shape, tile_shape],
        compiler_params=params,
        cost_estimate=cost,
        name="tiles",
    )(filter_taps)

    factor = 1.0 / math.sqrt(rows * size * group_width)
    most = pl.pallas_call(
        functools.partial(most_taps_kernel, rows),
        in_specs=[WHOLE] * 4,
        out_specs=WHOLE,
        out_shape=jax.ShapeDtypeStruct((group_count, taps), jnp.float32),
        compiler_params=params,
        cost_estimate=cost,
        name="most_taps",
    )(even_kept, odd_kept, diagonal, two)
    partial = pl.pallas_call(
        functools.partial(last_taps_kernel, rows, factor),
        in_specs=[WHOLE] * 3,
        out_specs=WHOLE,
        out_shape=jax.ShapeDtypeStruct((size, group_count, taps), jnp.float32),
        compiler_params=params,
        cost_estimate=cost,
        name="last_taps",
    )(most, even_kept, first)
    filter_grad = jnp.sum(lax.all_to_all(partial, "ctx", 0, 0), axis=0)

    out_shape = jax.ShapeDtypeStruct((rows, local_width), jnp.bfloat16)
    gated, key_grad, value_grad = pl.pallas_call(
        outputs_kernel,
        in_specs=[WHOLE] * 12,
        out_specs=[pl.BlockSpec(memory_space=pl.ANY)] * 3,
        out_shape=[out_shape] * 3,
        scratch_shapes=[pltpu.VMEM((rows, local_width), jnp.bfloat16)] * 3 + [pltpu.SemaphoreType.DMA((12,))],
        compiler_params=params,
        cost_estimate=cost,
        name="outputs",
    )(
        conv_tiles, back_tiles, even_kept, odd_kept, diagonal, two, first, far, last, query, keys, values
    )
    return (gated, key_grad, value_grad, filter_grad)


def solution(mesh):
    in_specs = (P("ctx", "grp"), P("ctx", "grp"), P("ctx", "grp"), P("ctx", "grp"), P("grp", None))
    out_specs = (P("ctx", "grp"), P("ctx", "grp"), P("ctx", "grp"), P("grp", None))
    return jax.shard_map(shards, mesh=mesh, in_specs=in_specs, out_specs=out_specs, check_vma=False)
```

```python
import functools
import math

import jax
import jax.numpy as jnp
from jax import lax
from jax.experimental import pallas as pl
from jax.experimental.pallas import tpu as pltpu
from jax.sharding import PartitionSpec as P

SUBLANES = 8
PARTS = 4
VMEM_LIMIT = 16 * 1024 * 1024
WHOLE = pl.BlockSpec(memory_space=pltpu.VMEM)


def moved(block, axis, distances):
    size = lax.axis_size(axis)
    route = [(i, i + distances[i % 2]) for i in range(size)]
    return lax.ppermute(block, axis, [pair for pair in route if 0 <= pair[1] < size])


def tiles_kernel(rows, reach, taps_ref, ready_ref, late_ref):
    odd = lax.rem(lax.axis_index("ctx"), 2) == 1
    width = reach * rows
    for group in range(taps_ref.shape[0]):
        row = taps_ref[group : group + 1, :].astype(jnp.float32)
        spread = jnp.concatenate(
            [jnp.zeros((SUBLANES, rows), jnp.float32), jnp.broadcast_to(row, (SUBLANES, width))],
            axis=1,
        )
        spread = pltpu.roll(spread, 0, 1, stride=1, stride_axis=0)
        bands = [
            pltpu.roll(spread, start, 1)[:, rows:] if start else spread[:, rows:]
            for start in range(0, rows, SUBLANES)
        ]
        band = jnp.concatenate(bands, axis=0)
        turned = [band[:, d * rows : (d + 1) * rows].T for d in range(reach)]
        turned = jnp.concatenate(turned, axis=1)
        ready_ref[group] = lax.select(odd, band, turned).astype(jnp.bfloat16)
        late_ref[group] = lax.select(odd, turned, band).astype(jnp.bfloat16)


def skewed_sum(outer, rows):
    width = outer.shape[1]
    total = outer[:SUBLANES]
    for start in range(SUBLANES, rows, SUBLANES):
        total = total + pltpu.roll(outer[start : start + SUBLANES], width - start, 1)
    lines = [total[:1]] + [pltpu.roll(total[s : s + 1], width - s, 1) for s in range(1, SUBLANES)]
    return functools.reduce(jnp.add, lines)


DOT_ROWS = functools.partial(
    lax.dot_general,
    dimension_numbers=(((1,), (1,)), ((), ())),
    preferred_element_type=jnp.float32,
)


def write_out(odd, held, outs, part, sems, place):
    copies = []
    for block, places in zip(held, outs):
        for parity, out in enumerate(places):
            if out is not None:
                copies.append((parity, block.at[:, part], out.at[:, part], sems.at[place + len(copies)]))
    for parity, source, target, sem in copies:
        @pl.when(odd == (parity == 1))
        def _():
            pltpu.make_async_copy(source, target, sem).start()
    return copies


def wait_out(odd, copies):
    for parity, source, target, sem in copies:
        @pl.when(odd == (parity == 1))
        def _():
            pltpu.make_async_copy(source, target, sem).wait()


def ready_kernel(
    rows, tile_ref, even_ref, odd_ref, diagonal_ref, two_ref, query_ref, keys_ref, values_ref,
    sum_ref, gated_out, key_out, value_out, one, other, sems,
):
    odd = lax.rem(lax.axis_index("ctx"), 2) == 1
    group_count, width = sum_ref.shape
    group_width = even_ref.shape[1] // group_count
    half = group_count // 2
    step = max(1, group_count // PARTS)

    def columns(group):
        return slice(group * group_width, (group + 1) * group_width)

    def held(ref, group):
        return ref[:, columns(group)]

    copies = []
    for group in range(group_count):
        ready = jnp.dot(
            tile_ref[group],
            jnp.concatenate([held(ref, group) for ref in (even_ref, diagonal_ref, two_ref)], axis=0),
            preferred_element_type=jnp.float32,
        )
        factor = lax.select(odd, held(values_ref, group), held(query_ref, group))
        one[:, columns(group)] = (ready * factor.astype(jnp.float32)).astype(one.dtype)
        other[:, columns(group)] = (ready * held(keys_ref, group).astype(jnp.float32)).astype(other.dtype)
        if (group + 1) % step == 0:
            part = pl.ds((group + 1 - step) * group_width, step * group_width)
            copies += write_out(
                odd, (one, other), ((gated_out, key_out), (None, value_out)), part, sems, len(copies)
            )

    middles = []
    for group in range(half):
        across = lax.select(odd, held(diagonal_ref, group + half), held(diagonal_ref, group))
        own = lax.select(odd, held(odd_ref, group + half), held(odd_ref, group))
        middles.append(DOT_ROWS(lax.select(odd, own, across), lax.select(odd, across, own)))
    blank = jnp.zeros((rows, rows), jnp.float32)
    sums = []
    for group in range(group_count):
        near = DOT_ROWS(
            lax.select(odd, held(odd_ref, group), held(even_ref, group)),
            lax.select(odd, held(even_ref, group), held(odd_ref, group)),
        )
        far = DOT_ROWS(
            lax.select(odd, held(odd_ref, group), held(two_ref, group)),
            lax.select(odd, held(two_ref, group), held(odd_ref, group)),
        )
        if group < half:
            middle = lax.select(odd, blank, middles[group])
        else:
            middle = lax.select(odd, middles[group - half], blank)
        outer = jnp.concatenate([near, middle, far, blank], axis=1)
        sums.append(skewed_sum(outer, rows)[:, :width])
    sum_ref[...] = jnp.concatenate(sums, axis=0)
    wait_out(odd, copies)


def first_kernel(rows, factor, sum_ref, tile_ref, even_ref, odd_ref, first_ref, out_ref, late_ref):
    odd = lax.rem(lax.axis_index("ctx"), 2) == 1
    copies, group_count, width = out_ref.shape
    group_width = even_ref.shape[1] // group_count
    half = group_count // 2
    blank = jnp.zeros((rows, rows), jnp.float32)
    sums = []
    for group in range(half):
        columns = slice(group * group_width, (group + 1) * group_width)
        other = slice((group + half) * group_width, (group + half + 1) * group_width)
        own = lax.select(odd, even_ref[:, columns], even_ref[:, other])
        across = first_ref[:, columns]
        outer = DOT_ROWS(lax.select(odd, across, own), lax.select(odd, own, across))
        sums.append(skewed_sum(jnp.concatenate([blank, outer], axis=1), rows))
        low = jnp.dot(tile_ref[group, :, :rows], odd_ref[:, columns], preferred_element_type=jnp.float32)
        high = jnp.dot(tile_ref[group + half, :, :rows], odd_ref[:, other], preferred_element_type=jnp.float32)
        tile = lax.select(
            odd, tile_ref[group, :, rows : 2 * rows], tile_ref[group + half, :, rows : 2 * rows]
        )
        more = jnp.dot(tile, across, preferred_element_type=jnp.float32)
        late_ref[:, columns] = low + lax.select(odd, more, blank)
        late_ref[:, other] = high + lax.select(odd, blank, more)
    rest = jnp.concatenate(
        [jnp.concatenate(sums, axis=0), jnp.zeros((half, width - 2 * rows), jnp.float32)], axis=1
    )
    low = (sum_ref[:half] + lax.select(odd, rest, jnp.zeros_like(rest))) * factor
    high = (sum_ref[half:] + lax.select(odd, jnp.zeros_like(rest), rest)) * factor
    for copy in range(copies):
        out_ref[copy, :half] = low
        out_ref[copy, half:] = high


def late_kernel(
    tile_ref, late_ref, far_ref, last_ref, query_ref, keys_ref, values_ref, gated_in, key_in, value_in,
    gated_out, key_out, value_out, one, other, sems,
):
    odd = lax.rem(lax.axis_index("ctx"), 2) == 1
    group_count, rows, _ = tile_ref.shape
    group_width = far_ref.shape[1] // group_count
    half = group_count // 2
    step = max(1, group_count // PARTS)
    blank = jnp.zeros((rows, group_width), jnp.float32)
    copies = []
    for group in range(group_count):
        columns = slice(group * group_width, (group + 1) * group_width)
        inner = slice((group % half) * group_width, (group % half + 1) * group_width)
        late = late_ref[:, columns] + jnp.dot(
            tile_ref[group, :, 2 * rows :], far_ref[:, columns], preferred_element_type=jnp.float32
        )
        more = jnp.dot(
            tile_ref[group, :, rows : 2 * rows], last_ref[:, inner], preferred_element_type=jnp.float32
        )
        late = late + (lax.select(odd, blank, more) if group < half else lax.select(odd, more, blank))
        factor = lax.select(odd, query_ref[:, columns], values_ref[:, columns])
        one[:, columns] = (late * factor.astype(jnp.float32)).astype(one.dtype)
        other[:, columns] = (late * keys_ref[:, columns].astype(jnp.float32)).astype(other.dtype)
        if (group + 1) % step == 0:
            part = pl.ds((group + 1 - step) * group_width, step * group_width)
            copies += write_out(
                odd, (one, other), ((key_out, gated_out), (value_out, None)), part, sems, len(copies)
            )
    wait_out(odd, copies)


def shards(query, keys, values, cotangent, filter_taps):
    rows, local_width = query.shape
    group_count, taps = filter_taps.shape
    group_width = local_width // group_count
    reach = taps // rows
    size = lax.axis_size("ctx")
    odd = lax.axis_index("ctx") % 2 == 1
    half = local_width // 2
    params = pltpu.CompilerParams(vmem_limit_bytes=VMEM_LIMIT)
    cost = pl.CostEstimate(flops=5 * 10**8, bytes_accessed=8 * 10**6, transcendentals=0)

    prod = (keys.astype(jnp.float32) * values.astype(jnp.float32)).astype(jnp.bfloat16)
    grad = (cotangent.astype(jnp.float32) * query.astype(jnp.float32)).astype(jnp.bfloat16)
    odd_kept = jnp.where(odd, prod, grad)
    diagonal = moved(odd_kept, "ctx", (-1, 1))
    even_kept = jnp.where(odd, grad, prod)
    two = moved(even_kept, "ctx", (2, -2))
    first = moved(jnp.where(odd, grad[:, half:], prod[:, :half]), "ctx", (1, -1))
    far = moved(odd_kept, "ctx", (-2, 2))
    rest = jnp.where(odd, grad[:, :half], prod[:, half:])
    rest, diagonal = lax.optimization_barrier((rest, diagonal))
    last = moved(rest, "ctx", (1, -1))

    step = min(group_count, 8)
    tile_shape = jax.ShapeDtypeStruct((group_count, rows, taps), jnp.bfloat16)
    tile_spec = pl.BlockSpec((step, rows, taps), lambda i: (i, 0, 0))
    ready_tiles, late_tiles = pl.pallas_call(
        functools.partial(tiles_kernel, rows, reach),
        grid=(group_count // step,),
        in_specs=[pl.BlockSpec((step, taps), lambda i: (i, 0))],
        out_specs=[tile_spec, tile_spec],
        out_shape=[tile_shape, tile_shape],
        compiler_params=params,
        cost_estimate=cost,
        name="tiles",
    )(filter_taps)

    out_shape = jax.ShapeDtypeStruct((rows, local_width), jnp.bfloat16)
    out_scratch = [pltpu.VMEM((rows, local_width), jnp.bfloat16)] * 2 + [pltpu.SemaphoreType.DMA((3 * PARTS,))]
    anywhere = pl.BlockSpec(memory_space=pl.ANY)
    sums, gated, key_grad, value_grad = pl.pallas_call(
        functools.partial(ready_kernel, rows),
        in_specs=[WHOLE] * 8,
        out_specs=[WHOLE] + [anywhere] * 3,
        out_shape=[jax.ShapeDtypeStruct((group_count, taps), jnp.float32)] + [out_shape] * 3,
        scratch_shapes=out_scratch,
        compiler_params=params,
        cost_estimate=cost,
        name="ready",
    )(ready_tiles, even_kept, odd_kept, diagonal, two, query, keys, values)

    factor = 1.0 / math.sqrt(rows * size * group_width)
    partial, late = pl.pallas_call(
        functools.partial(first_kernel, rows, factor),
        in_specs=[WHOLE] * 5,
        out_specs=[WHOLE] * 2,
        out_shape=[
            jax.ShapeDtypeStruct((size, group_count, taps), jnp.float32),
            jax.ShapeDtypeStruct((rows, local_width), jnp.float32),
        ],
        compiler_params=params,
        cost_estimate=cost,
        name="first",
    )(sums, late_tiles, even_kept, odd_kept, first)
    filter_grad = jnp.sum(lax.all_to_all(partial, "ctx", 0, 0), axis=0)

    gated, key_grad, value_grad = pl.pallas_call(
        late_kernel,
        in_specs=[WHOLE] * 7 + [anywhere] * 3,
        out_specs=[anywhere] * 3,
        out_shape=[out_shape] * 3,
        input_output_aliases={7: 0, 8: 1, 9: 2},
        scratch_shapes=out_scratch,
        compiler_params=params,
        cost_estimate=cost,
        name="late",
    )(late_tiles, late, far, last, query, keys, values, gated, key_grad, value_grad)
    return (gated, key_grad, value_grad, filter_grad)


def solution(mesh):
    in_specs = (P("ctx", "grp"), P("ctx", "grp"), P("ctx", "grp"), P("ctx", "grp"), P("grp", None))
    out_specs = (P("ctx", "grp"), P("ctx", "grp"), P("ctx", "grp"), P("grp", None))
    return jax.shard_map(shards, mesh=mesh, in_specs=in_specs, out_specs=out_specs, check_vma=False)
```

```python
import functools
import math

import jax
import jax.numpy as jnp
from jax import lax
from jax.experimental import pallas as pl
from jax.experimental.pallas import tpu as pltpu
from jax.sharding import PartitionSpec as P

SUBLANES = 8
PARTS = 4
VMEM_LIMIT = 16 * 1024 * 1024
WHOLE = pl.BlockSpec(memory_space=pltpu.VMEM)


def in_vmem(*arrays):
    return [pltpu.with_memory_space_constraint(array, pltpu.VMEM) for array in arrays]


def moved(block, axis, distances):
    size = lax.axis_size(axis)
    route = [(i, i + distances[i % 2]) for i in range(size)]
    return lax.ppermute(block, axis, [pair for pair in route if 0 <= pair[1] < size])


def tiles_kernel(rows, reach, taps_ref, ready_ref, late_ref):
    odd = lax.rem(lax.axis_index("ctx"), 2) == 1
    width = reach * rows
    for group in range(taps_ref.shape[0]):
        row = taps_ref[group : group + 1, :].astype(jnp.float32)
        spread = jnp.concatenate(
            [jnp.zeros((SUBLANES, rows), jnp.float32), jnp.broadcast_to(row, (SUBLANES, width))],
            axis=1,
        )
        spread = pltpu.roll(spread, 0, 1, stride=1, stride_axis=0)
        bands = [
            pltpu.roll(spread, start, 1)[:, rows:] if start else spread[:, rows:]
            for start in range(0, rows, SUBLANES)
        ]
        band = jnp.concatenate(bands, axis=0)
        turned = [band[:, d * rows : (d + 1) * rows].T for d in range(reach)]
        turned = jnp.concatenate(turned, axis=1)
        ready_ref[group] = lax.select(odd, band, turned).astype(jnp.bfloat16)
        late_ref[group] = lax.select(odd, turned, band).astype(jnp.bfloat16)


def skewed_sum(outer, rows):
    width = outer.shape[1]
    total = outer[:SUBLANES]
    for start in range(SUBLANES, rows, SUBLANES):
        total = total + pltpu.roll(outer[start : start + SUBLANES], width - start, 1)
    lines = [total[:1]] + [pltpu.roll(total[s : s + 1], width - s, 1) for s in range(1, SUBLANES)]
    return functools.reduce(jnp.add, lines)


DOT_ROWS = functools.partial(
    lax.dot_general,
    dimension_numbers=(((1,), (1,)), ((), ())),
    preferred_element_type=jnp.float32,
)


def write_out(odd, held, outs, part, sems, place):
    copies = []
    for block, places in zip(held, outs):
        for parity, out in enumerate(places):
            if out is not None:
                copies.append((parity, block.at[:, part], out.at[:, part], sems.at[place + len(copies)]))
    for parity, source, target, sem in copies:
        @pl.when(odd == (parity == 1))
        def _():
            pltpu.make_async_copy(source, target, sem).start()
    return copies


def wait_out(odd, copies):
    for parity, source, target, sem in copies:
        @pl.when(odd == (parity == 1))
        def _():
            pltpu.make_async_copy(source, target, sem).wait()


def ready_kernel(
    rows, tile_ref, even_ref, odd_ref, diagonal_ref, two_ref, query_ref, keys_ref, values_ref,
    sum_ref, gated_out, key_out, value_out, one, other, sems,
):
    odd = lax.rem(lax.axis_index("ctx"), 2) == 1
    group_count, width = sum_ref.shape
    group_width = even_ref.shape[1] // group_count
    half = group_count // 2
    step = max(1, group_count // PARTS)

    def columns(group):
        return slice(group * group_width, (group + 1) * group_width)

    def held(ref, group):
        return ref[:, columns(group)]

    copies = []
    for group in range(group_count):
        ready = jnp.dot(
            tile_ref[group],
            jnp.concatenate([held(ref, group) for ref in (even_ref, diagonal_ref, two_ref)], axis=0),
            preferred_element_type=jnp.float32,
        )
        factor = lax.select(odd, held(values_ref, group), held(query_ref, group))
        one[:, columns(group)] = (ready * factor.astype(jnp.float32)).astype(one.dtype)
        other[:, columns(group)] = (ready * held(keys_ref, group).astype(jnp.float32)).astype(other.dtype)
        if (group + 1) % step == 0:
            part = pl.ds((group + 1 - step) * group_width, step * group_width)
            copies += write_out(
                odd, (one, other), ((gated_out, key_out), (None, value_out)), part, sems, len(copies)
            )

    middles = []
    for group in range(half):
        across = lax.select(odd, held(diagonal_ref, group + half), held(diagonal_ref, group))
        own = lax.select(odd, held(odd_ref, group + half), held(odd_ref, group))
        middles.append(DOT_ROWS(lax.select(odd, own, across), lax.select(odd, across, own)))
    blank = jnp.zeros((rows, rows), jnp.float32)
    sums = []
    for group in range(group_count):
        near = DOT_ROWS(
            lax.select(odd, held(odd_ref, group), held(even_ref, group)),
            lax.select(odd, held(even_ref, group), held(odd_ref, group)),
        )
        far = DOT_ROWS(
            lax.select(odd, held(odd_ref, group), held(two_ref, group)),
            lax.select(odd, held(two_ref, group), held(odd_ref, group)),
        )
        if group < half:
            middle = lax.select(odd, blank, middles[group])
        else:
            middle = lax.select(odd, middles[group - half], blank)
        outer = jnp.concatenate([near, middle, far, blank], axis=1)
        sums.append(skewed_sum(outer, rows)[:, :width])
    sum_ref[...] = jnp.concatenate(sums, axis=0)
    wait_out(odd, copies)


def first_kernel(rows, factor, sum_ref, tile_ref, even_ref, odd_ref, first_ref, out_ref, late_ref):
    odd = lax.rem(lax.axis_index("ctx"), 2) == 1
    copies, group_count, width = out_ref.shape
    group_width = even_ref.shape[1] // group_count
    half = group_count // 2
    blank = jnp.zeros((rows, rows), jnp.float32)
    sums = []
    for group in range(half):
        columns = slice(group * group_width, (group + 1) * group_width)
        other = slice((group + half) * group_width, (group + half + 1) * group_width)
        own = lax.select(odd, even_ref[:, columns], even_ref[:, other])
        across = first_ref[:, columns]
        outer = DOT_ROWS(lax.select(odd, across, own), lax.select(odd, own, across))
        sums.append(skewed_sum(jnp.concatenate([blank, outer], axis=1), rows))
        low = jnp.dot(tile_ref[group, :, :rows], odd_ref[:, columns], preferred_element_type=jnp.float32)
        high = jnp.dot(tile_ref[group + half, :, :rows], odd_ref[:, other], preferred_element_type=jnp.float32)
        tile = lax.select(
            odd, tile_ref[group, :, rows : 2 * rows], tile_ref[group + half, :, rows : 2 * rows]
        )
        more = jnp.dot(tile, across, preferred_element_type=jnp.float32)
        late_ref[:, columns] = low + lax.select(odd, more, blank)
        late_ref[:, other] = high + lax.select(odd, blank, more)
    rest = jnp.concatenate(
        [jnp.concatenate(sums, axis=0), jnp.zeros((half, width - 2 * rows), jnp.float32)], axis=1
    )
    low = (sum_ref[:half] + lax.select(odd, rest, jnp.zeros_like(rest))) * factor
    high = (sum_ref[half:] + lax.select(odd, jnp.zeros_like(rest), rest)) * factor
    for copy in range(copies):
        out_ref[copy, :half] = low
        out_ref[copy, half:] = high


def late_kernel(
    tile_ref, late_ref, far_ref, last_ref, query_ref, keys_ref, values_ref, gated_in, key_in, value_in,
    gated_out, key_out, value_out, one, other, sems,
):
    odd = lax.rem(lax.axis_index("ctx"), 2) == 1
    group_count, rows, _ = tile_ref.shape
    group_width = far_ref.shape[1] // group_count
    half = group_count // 2
    step = max(1, group_count // PARTS)
    blank = jnp.zeros((rows, group_width), jnp.float32)
    copies = []
    for group in range(group_count):
        columns = slice(group * group_width, (group + 1) * group_width)
        inner = slice((group % half) * group_width, (group % half + 1) * group_width)
        late = late_ref[:, columns] + jnp.dot(
            tile_ref[group, :, 2 * rows :], far_ref[:, columns], preferred_element_type=jnp.float32
        )
        more = jnp.dot(
            tile_ref[group, :, rows : 2 * rows], last_ref[:, inner], preferred_element_type=jnp.float32
        )
        late = late + (lax.select(odd, blank, more) if group < half else lax.select(odd, more, blank))
        factor = lax.select(odd, query_ref[:, columns], values_ref[:, columns])
        one[:, columns] = (late * factor.astype(jnp.float32)).astype(one.dtype)
        other[:, columns] = (late * keys_ref[:, columns].astype(jnp.float32)).astype(other.dtype)
        if (group + 1) % step == 0:
            part = pl.ds((group + 1 - step) * group_width, step * group_width)
            copies += write_out(
                odd, (one, other), ((key_out, gated_out), (value_out, None)), part, sems, len(copies)
            )
    wait_out(odd, copies)


def shards(query, keys, values, cotangent, filter_taps):
    rows, local_width = query.shape
    group_count, taps = filter_taps.shape
    group_width = local_width // group_count
    reach = taps // rows
    size = lax.axis_size("ctx")
    odd = lax.axis_index("ctx") % 2 == 1
    half = local_width // 2
    params = pltpu.CompilerParams(vmem_limit_bytes=VMEM_LIMIT)
    small = pl.CostEstimate(flops=10**6, bytes_accessed=10**5, transcendentals=0)
    large = pl.CostEstimate(flops=10**11, bytes_accessed=10**8, transcendentals=0)

    prod = (keys.astype(jnp.float32) * values.astype(jnp.float32)).astype(jnp.bfloat16)
    grad = (cotangent.astype(jnp.float32) * query.astype(jnp.float32)).astype(jnp.bfloat16)
    odd_kept = jnp.where(odd, prod, grad)
    diagonal = moved(odd_kept, "ctx", (-1, 1))
    even_kept = jnp.where(odd, grad, prod)
    two = moved(even_kept, "ctx", (2, -2))
    first = moved(jnp.where(odd, grad[:, half:], prod[:, :half]), "ctx", (1, -1))
    far = moved(odd_kept, "ctx", (-2, 2))
    rest = jnp.where(odd, grad[:, :half], prod[:, half:])
    rest, diagonal = lax.optimization_barrier((rest, diagonal))
    last = moved(rest, "ctx", (1, -1))

    ready_tiles, late_tiles = pl.pallas_call(
        functools.partial(tiles_kernel, rows, reach),
        in_specs=[WHOLE],
        out_specs=[WHOLE] * 2,
        out_shape=[pltpu.VMEM((group_count, rows, taps), jnp.bfloat16)] * 2,
        compiler_params=params,
        cost_estimate=small,
        name="tiles",
    )(filter_taps)

    out_shape = jax.ShapeDtypeStruct((rows, local_width), jnp.bfloat16)
    out_scratch = [pltpu.VMEM((rows, local_width), jnp.bfloat16)] * 2 + [pltpu.SemaphoreType.DMA((3 * PARTS,))]
    anywhere = pl.BlockSpec(memory_space=pl.ANY)
    sums, gated, key_grad, value_grad = pl.pallas_call(
        functools.partial(ready_kernel, rows),
        in_specs=[WHOLE] * 8,
        out_specs=[WHOLE] + [anywhere] * 3,
        out_shape=[pltpu.VMEM((group_count, taps), jnp.float32)] + [out_shape] * 3,
        scratch_shapes=out_scratch,
        compiler_params=params,
        cost_estimate=small,
        name="ready",
    )(*in_vmem(ready_tiles, even_kept, odd_kept, diagonal, two, query, keys, values))

    factor = 1.0 / math.sqrt(rows * size * group_width)
    partial, late = pl.pallas_call(
        functools.partial(first_kernel, rows, factor),
        in_specs=[WHOLE] * 5,
        out_specs=[WHOLE] * 2,
        out_shape=[
            jax.ShapeDtypeStruct((size, group_count, taps), jnp.float32),
            pltpu.VMEM((rows, local_width), jnp.float32),
        ],
        compiler_params=params,
        cost_estimate=small,
        name="first",
    )(*in_vmem(sums, late_tiles, even_kept, odd_kept, first))
    filter_grad = jnp.sum(lax.all_to_all(partial, "ctx", 0, 0), axis=0)

    gated, key_grad, value_grad = pl.pallas_call(
        late_kernel,
        in_specs=[WHOLE] * 7 + [anywhere] * 3,
        out_specs=[anywhere] * 3,
        out_shape=[out_shape] * 3,
        input_output_aliases={7: 0, 8: 1, 9: 2},
        scratch_shapes=out_scratch,
        compiler_params=params,
        cost_estimate=large,
        name="late",
    )(*in_vmem(late_tiles, late, far, last, query, keys, values), gated, key_grad, value_grad)
    return (gated, key_grad, value_grad, filter_grad)


def solution(mesh):
    in_specs = (P("ctx", "grp"), P("ctx", "grp"), P("ctx", "grp"), P("ctx", "grp"), P("grp", None))
    out_specs = (P("ctx", "grp"), P("ctx", "grp"), P("ctx", "grp"), P("grp", None))
    return jax.shard_map(shards, mesh=mesh, in_specs=in_specs, out_specs=out_specs, check_vma=False)
```

```python
import functools
import math

import jax
import jax.numpy as jnp
from jax import lax
from jax.experimental import pallas as pl
from jax.experimental.pallas import tpu as pltpu
from jax.sharding import PartitionSpec as P

SUBLANES = 8
PARTS = 4
VMEM_LIMIT = 16 * 1024 * 1024
WHOLE = pl.BlockSpec(memory_space=pltpu.VMEM)
ANYWHERE = pl.BlockSpec(memory_space=pl.ANY)
DOT_ROWS = functools.partial(
    lax.dot_general,
    dimension_numbers=(((1,), (1,)), ((), ())),
    preferred_element_type=jnp.float32,
)
DOT = functools.partial(jnp.dot, preferred_element_type=jnp.float32)


def in_vmem(*arrays):
    return [pltpu.with_memory_space_constraint(array, pltpu.VMEM) for array in arrays]


def in_hbm(*arrays):
    return [pltpu.with_memory_space_constraint(array, pltpu.HBM) for array in arrays]


def moved(block, axis, distances):
    size = lax.axis_size(axis)
    route = [(i, i + distances[i % 2]) for i in range(size)]
    return lax.ppermute(block, axis, [pair for pair in route if 0 <= pair[1] < size])


def summed(pair_sum, axis, add, add_last):
    size = lax.axis_size(axis)
    if size & (size - 1):
        even = lax.axis_index(axis) % 2 == 0
        return lax.psum(jnp.where(even, pair_sum, 0.0), axis)
    stride = 2
    while stride < size:
        route = [(i, i ^ stride) for i in range(size)]
        arrived = lax.ppermute(pair_sum, axis, route)
        stride *= 2
        pair_sum = (add if stride < size else add_last)(pair_sum, arrived)
    return pair_sum


def is_odd():
    return lax.rem(lax.axis_index("ctx"), 2) == 1


def product(left, right):
    return (left.astype(jnp.float32) * right.astype(jnp.float32)).astype(jnp.bfloat16)


def scaled(value, factor):
    return (value * factor.astype(jnp.float32)).astype(jnp.bfloat16)


def columns_of(group, width):
    return slice(group * width, (group + 1) * width)


def launch(odd, moves, sems, used):
    copies = [(*move, sems.at[used + place]) for place, move in enumerate(moves)]
    for parity, source, target, sem in copies:
        @pl.when(odd if parity else jnp.logical_not(odd))
        def _():
            pltpu.make_async_copy(source, target, sem).start()
    return copies


def finish(odd, copies):
    for parity, source, target, sem in copies:
        @pl.when(odd if parity else jnp.logical_not(odd))
        def _():
            pltpu.make_async_copy(source, target, sem).wait()


def skewed_sum(outer, rows):
    width = outer.shape[1]
    total = outer[:SUBLANES]
    for start in range(SUBLANES, rows, SUBLANES):
        total = total + pltpu.roll(outer[start : start + SUBLANES], width - start, 1)
    lines = [total[:1]] + [pltpu.roll(total[s : s + 1], width - s, 1) for s in range(1, SUBLANES)]
    return functools.reduce(jnp.add, lines)


def diagonal_kernel(query_hbm, keys_hbm, values_hbm, cotangent_hbm, out_ref, left, right, sems):
    odd = is_odd()
    half = out_ref.shape[1]
    low, high = pl.ds(0, half), pl.ds(half, half)
    copies = launch(
        odd,
        [
            (1, keys_hbm.at[:, low], left),
            (1, values_hbm.at[:, low], right),
            (0, cotangent_hbm.at[:, high], left),
            (0, query_hbm.at[:, high], right),
        ],
        sems,
        0,
    )
    finish(odd, copies)
    out_ref[...] = product(left[...], right[...])


def products_kernel(query_ref, keys_ref, values_ref, cotangent_ref, sent_ref, near_ref, across_ref):
    odd = is_odd()
    prod = product(keys_ref[...], values_ref[...])
    grad = product(cotangent_ref[...], query_ref[...])
    near_ref[...] = lax.select(odd, prod, grad)
    across_ref[...] = lax.select(odd, grad, prod)


def tiles_kernel(rows, taps_ref, ready_tiles, late_tiles):
    odd = is_odd()
    group_count, width = taps_ref.shape
    for group in range(group_count):
        row = taps_ref[group : group + 1, :].astype(jnp.float32)
        spread = jnp.concatenate(
            [jnp.zeros((SUBLANES, rows), jnp.float32), jnp.broadcast_to(row, (SUBLANES, width))],
            axis=1,
        )
        spread = pltpu.roll(spread, 0, 1, stride=1, stride_axis=0)
        bands = [
            pltpu.roll(spread, start, 1)[:, rows:] if start else spread[:, rows:]
            for start in range(0, rows, SUBLANES)
        ]
        band = jnp.concatenate(bands, axis=0)
        turned = [band[:, start : start + rows].T for start in range(0, width, rows)]
        turned = jnp.concatenate(turned, axis=1)
        ready_tiles[group] = lax.select(odd, band, turned).astype(jnp.bfloat16)
        late_tiles[group] = lax.select(odd, turned, band).astype(jnp.bfloat16)


def own_kernel(
    rows, ready_tiles, late_tiles, near_ref, across_ref, diagonal_ref, sum_ref, late_ref, ready_ref
):
    odd = is_odd()
    group_count, width = sum_ref.shape
    group_width = near_ref.shape[1] // group_count
    half = group_count // 2
    blank = jnp.zeros((rows, rows), jnp.float32)
    for group in range(group_count):
        columns = columns_of(group, group_width)
        late_ref[:, columns] = DOT(late_tiles[group, :, :rows], near_ref[:, columns])
        ready_ref[:, columns] = DOT(ready_tiles[group, :, :rows], across_ref[:, columns])
    middles = []
    for group in range(half):
        low, high = columns_of(group, group_width), columns_of(group + half, group_width)
        arrived = diagonal_ref[:, low]
        own = lax.select(odd, near_ref[:, high], near_ref[:, low])
        middles.append(DOT_ROWS(lax.select(odd, own, arrived), lax.select(odd, arrived, own)))
        tile = lax.select(
            odd, ready_tiles[group + half, :, rows : 2 * rows], ready_tiles[group, :, rows : 2 * rows]
        )
        more = DOT(tile, arrived)
        ready_ref[:, low] += lax.select(odd, blank, more)
        ready_ref[:, high] += lax.select(odd, more, blank)
    sums = []
    for group in range(group_count):
        columns = columns_of(group, group_width)
        near, across = near_ref[:, columns], across_ref[:, columns]
        outer = DOT_ROWS(lax.select(odd, near, across), lax.select(odd, across, near))
        if group < half:
            middle = lax.select(odd, blank, middles[group])
        else:
            middle = lax.select(odd, middles[group - half], blank)
        sums.append(skewed_sum(jnp.concatenate([outer, middle, blank], axis=1), rows)[:, : 2 * rows])
    sums = jnp.concatenate(sums, axis=0)
    sum_ref[...] = jnp.concatenate([sums, jnp.zeros((group_count, width - 2 * rows), jnp.float32)], axis=1)


def two_kernel(rows, sum_ref, near_ref, two_ref, out_ref):
    odd = is_odd()
    group_count, width = out_ref.shape
    group_width = near_ref.shape[1] // group_count
    blank = jnp.zeros((rows, rows), jnp.float32)
    sums = []
    for group in range(group_count):
        columns = columns_of(group, group_width)
        near, two = near_ref[:, columns], two_ref[:, columns]
        outer = DOT_ROWS(lax.select(odd, near, two), lax.select(odd, two, near))
        sums.append(skewed_sum(jnp.concatenate([blank, outer], axis=1), rows))
    sums = jnp.concatenate(sums, axis=0)
    out_ref[...] = sum_ref[...] + jnp.concatenate(
        [jnp.zeros((group_count, width - 2 * rows), jnp.float32), sums], axis=1
    )


def pair_kernel(rows, factor, sum_ref, other_ref, across_ref, swap_ref, out_ref):
    odd = is_odd()
    group_count, width = out_ref.shape
    group_width = across_ref.shape[1] // group_count
    blank = jnp.zeros((rows, rows), jnp.float32)
    sums = []
    for group in range(group_count):
        columns = columns_of(group, group_width)
        across, swap = across_ref[:, columns], swap_ref[:, columns]
        outer = DOT_ROWS(lax.select(odd, swap, across), lax.select(odd, across, swap))
        sums.append(skewed_sum(jnp.concatenate([blank, outer], axis=1), rows))
    sums = jnp.concatenate(sums, axis=0)
    rest = jnp.concatenate([sums, jnp.zeros((group_count, width - 2 * rows), jnp.float32)], axis=1)
    out_ref[...] = (sum_ref[...] + other_ref[...] + rest) * factor


def add_kernel(left_ref, right_ref, known_ref, out_ref):
    out_ref[...] = left_ref[...] + right_ref[...]


def forward_kernel(far_ref, rest_ref, out_ref):
    half = out_ref.shape[1]
    out_ref[...] = lax.select(is_odd(), far_ref[:, half:], far_ref[:, :half])


def ready_kernel(
    tiles_ref, ready_ref, two_ref, query_ref, keys_ref, values_ref, sum_ref,
    gated_out, key_out, value_out, rest_ref, one, other, sems,
):
    odd = is_odd()
    group_count, rows, _ = tiles_ref.shape
    group_width = two_ref.shape[1] // group_count
    half = group_count // 2
    step = max(1, half // 2)
    copies = []
    for group in range(half):
        low, high = columns_of(group, group_width), columns_of(group + half, group_width)
        first = ready_ref[:, low] + DOT(tiles_ref[group, :, 2 * rows :], two_ref[:, low])
        second = ready_ref[:, high] + DOT(tiles_ref[group + half, :, 2 * rows :], two_ref[:, high])
        rest_ref[:, low] = lax.select(odd, first, second)
        known = lax.select(odd, second, first)
        one[:, low] = scaled(known, lax.select(odd, values_ref[:, high], query_ref[:, low]))
        other[:, low] = scaled(known, keys_ref[:, high])
        if (group + 1) % step == 0:
            start, size = (group + 1 - step) * group_width, step * group_width
            part, place = pl.ds(start, size), pl.ds(start + half * group_width, size)
            moves = [
                (0, one.at[:, part], gated_out.at[:, part]),
                (1, one.at[:, part], key_out.at[:, place]),
                (1, other.at[:, part], value_out.at[:, place]),
            ]
            copies += launch(odd, moves, sems, len(copies))
    finish(odd, copies)


def known_kernel(
    tiles_ref, late_ref, swap_ref, far_ref, query_ref, keys_ref, values_ref, gated_in, key_in, value_in,
    gated_out, key_out, value_out, done_ref, one, other, sems,
):
    odd = is_odd()
    done_ref[...] = jnp.zeros_like(done_ref)
    group_count, rows, _ = tiles_ref.shape
    group_width = far_ref.shape[1] // group_count
    step = max(1, group_count // PARTS)
    copies = []
    for group in range(group_count):
        columns = columns_of(group, group_width)
        arrived = jnp.concatenate([swap_ref[:, columns], far_ref[:, columns]], axis=0)
        late = late_ref[:, columns] + DOT(tiles_ref[group, :, rows:], arrived)
        one[:, columns] = scaled(late, lax.select(odd, query_ref[:, columns], values_ref[:, columns]))
        other[:, columns] = scaled(late, keys_ref[:, columns])
        if (group + 1) % step == 0:
            part = pl.ds((group + 1 - step) * group_width, step * group_width)
            moves = [
                (0, one.at[:, part], key_out.at[:, part]),
                (0, other.at[:, part], value_out.at[:, part]),
                (1, one.at[:, part], gated_out.at[:, part]),
            ]
            copies += launch(odd, moves, sems, len(copies))
    finish(odd, copies)


def last_kernel(
    tiles_ref, rest_ref, forwarded_ref, query_ref, keys_ref, values_ref, gated_in, key_in, value_in,
    gated_out, key_out, value_out, done_ref, one, other, sems,
):
    odd = is_odd()
    done_ref[...] = jnp.zeros_like(done_ref)
    group_count, rows, _ = tiles_ref.shape
    half = group_count // 2
    group_width = forwarded_ref.shape[1] // half
    step = max(1, half // 2)
    copies = []
    for group in range(half):
        low, high = columns_of(group, group_width), columns_of(group + half, group_width)
        tile = lax.select(
            odd, tiles_ref[group, :, rows : 2 * rows], tiles_ref[group + half, :, rows : 2 * rows]
        )
        ready = rest_ref[:, low] + DOT(tile, forwarded_ref[:, low])
        one[:, low] = scaled(ready, lax.select(odd, values_ref[:, low], query_ref[:, high]))
        other[:, low] = scaled(ready, keys_ref[:, low])
        if (group + 1) % step == 0:
            start, size = (group + 1 - step) * group_width, step * group_width
            part, place = pl.ds(start, size), pl.ds(start + half * group_width, size)
            moves = [
                (0, one.at[:, part], gated_out.at[:, place]),
                (1, one.at[:, part], key_out.at[:, part]),
                (1, other.at[:, part], value_out.at[:, part]),
            ]
            copies += launch(odd, moves, sems, len(copies))
    finish(odd, copies)


def shards(query, keys, values, cotangent, filter_taps):
    rows, local_width = query.shape
    group_count, taps = filter_taps.shape
    group_width = local_width // group_count
    half_width = local_width // 2
    factor = 1.0 / math.sqrt(rows * lax.axis_size("ctx") * group_width)

    def call(kernel, name, flops=10**6, **options):
        return pl.pallas_call(
            kernel,
            compiler_params=pltpu.CompilerParams(vmem_limit_bytes=VMEM_LIMIT),
            cost_estimate=pl.CostEstimate(flops=flops, bytes_accessed=10**5, transcendentals=0),
            name=name,
            **options,
        )

    def out_scratch(width, parts):
        return [pltpu.VMEM((rows, width), jnp.bfloat16)] * 2 + [pltpu.SemaphoreType.DMA((3 * parts,))]

    bf16, f32 = jnp.bfloat16, jnp.float32
    block, half_block = pltpu.VMEM((rows, local_width), bf16), pltpu.VMEM((rows, half_width), bf16)
    wide, half_wide = pltpu.VMEM((rows, local_width), f32), pltpu.VMEM((rows, half_width), f32)
    tiles, sums = pltpu.VMEM((group_count, rows, taps), bf16), pltpu.VMEM((group_count, taps), f32)
    mark = pltpu.VMEM((SUBLANES, group_width), f32)
    outs = [jax.ShapeDtypeStruct((rows, local_width), bf16)] * 3

    sent = call(
        diagonal_kernel,
        "diagonal",
        in_specs=[ANYWHERE] * 4,
        out_specs=WHOLE,
        out_shape=half_block,
        scratch_shapes=[half_block] * 2 + [pltpu.SemaphoreType.DMA((4,))],
    )(*in_hbm(query, keys, values, cotangent))
    diagonal = moved(sent, "ctx", (-1, 1))
    near, across = call(
        products_kernel,
        "products",
        in_specs=[WHOLE] * 4 + [ANYWHERE],
        out_specs=[WHOLE] * 2,
        out_shape=[block] * 2,
    )(*in_vmem(query, keys, values, cotangent), sent)
    two = moved(across, "ctx", (2, -2))
    far = moved(near, "ctx", (-2, 2))
    swap = moved(across, "ctx", (1, -1))

    ready_tiles, late_tiles = call(
        functools.partial(tiles_kernel, rows),
        "tiles",
        in_specs=[WHOLE],
        out_specs=[WHOLE] * 2,
        out_shape=[tiles] * 2,
    )(*in_vmem(filter_taps))
    partial, late, ready = call(
        functools.partial(own_kernel, rows),
        "own",
        flops=4 * 10**9,
        in_specs=[WHOLE] * 5,
        out_specs=[WHOLE] * 3,
        out_shape=[sums, wide, wide],
    )(*in_vmem(ready_tiles, late_tiles, near, across, diagonal))

    partial = call(
        functools.partial(two_kernel, rows),
        "two",
        in_specs=[WHOLE] * 3,
        out_specs=WHOLE,
        out_shape=sums,
    )(*in_vmem(partial, near, two))
    other = moved(partial, "ctx", (1, -1))

    gated, key_grad, value_grad, rest = call(
        ready_kernel,
        "ready",
        in_specs=[WHOLE] * 6 + [ANYWHERE],
        out_specs=[ANYWHERE] * 3 + [WHOLE],
        out_shape=outs + [half_wide],
        scratch_shapes=out_scratch(half_width, 2),
    )(*in_vmem(ready_tiles, ready, two, query, keys, values), partial)

    forwarded = call(
        forward_kernel,
        "forward",
        in_specs=[WHOLE, ANYWHERE],
        out_specs=WHOLE,
        out_shape=half_block,
    )(*in_vmem(far), rest)
    forwarded = moved(forwarded, "ctx", (1, -1))

    pair_sum = call(
        functools.partial(pair_kernel, rows, factor),
        "pair",
        in_specs=[WHOLE] * 4,
        out_specs=WHOLE,
        out_shape=sums,
    )(*in_vmem(partial, other, across, swap))
    gated, key_grad, value_grad, known_done = call(
        known_kernel,
        "known",
        flops=4 * 10**9,
        in_specs=[WHOLE] * 7 + [ANYWHERE] * 3,
        out_specs=[ANYWHERE] * 3 + [WHOLE],
        out_shape=outs + [mark],
        input_output_aliases={7: 0, 8: 1, 9: 2},
        scratch_shapes=out_scratch(local_width, PARTS),
    )(*in_vmem(late_tiles, late, swap, far, query, keys, values), gated, key_grad, value_grad)

    gated, key_grad, value_grad, last_done = call(
        last_kernel,
        "last",
        in_specs=[WHOLE] * 6 + [ANYWHERE] * 3,
        out_specs=[ANYWHERE] * 3 + [WHOLE],
        out_shape=outs + [mark],
        input_output_aliases={6: 0, 7: 1, 8: 2},
        scratch_shapes=out_scratch(half_width, 2),
    )(*in_vmem(ready_tiles, rest, forwarded, query, keys, values), gated, key_grad, value_grad)

    def adder(out_shape, after):
        add = call(
            add_kernel,
            "add",
            in_specs=[WHOLE] * 2 + [ANYWHERE],
            out_specs=WHOLE,
            out_shape=out_shape,
        )
        return lambda left, right: add(*in_vmem(left, right), after)

    whole_sums = jax.ShapeDtypeStruct((group_count, taps), f32)
    filter_grad = summed(pair_sum, "ctx", adder(sums, known_done), adder(whole_sums, last_done))
    return (gated, key_grad, value_grad, filter_grad)


def solution(mesh):
    in_specs = (P("ctx", "grp"), P("ctx", "grp"), P("ctx", "grp"), P("ctx", "grp"), P("grp", None))
    out_specs = (P("ctx", "grp"), P("ctx", "grp"), P("ctx", "grp"), P("grp", None))
    return jax.shard_map(shards, mesh=mesh, in_specs=in_specs, out_specs=out_specs, check_vma=False)
```

```python
import functools
import math

import jax
import jax.numpy as jnp
from jax import lax
from jax.experimental import pallas as pl
from jax.experimental.pallas import tpu as pltpu
from jax.sharding import PartitionSpec as P

SUBLANES = 8
PARTS = 4
VMEM_LIMIT = 16 * 1024 * 1024
WHOLE = pl.BlockSpec(memory_space=pltpu.VMEM)
ANYWHERE = pl.BlockSpec(memory_space=pl.ANY)
DOT_ROWS = functools.partial(
    lax.dot_general,
    dimension_numbers=(((1,), (1,)), ((), ())),
    preferred_element_type=jnp.float32,
)
DOT = functools.partial(jnp.dot, preferred_element_type=jnp.float32)


def in_vmem(*arrays):
    return [pltpu.with_memory_space_constraint(array, pltpu.VMEM) for array in arrays]


def in_hbm(*arrays):
    return [pltpu.with_memory_space_constraint(array, pltpu.HBM) for array in arrays]


def moved(block, axis, distances):
    size = lax.axis_size(axis)
    route = [(i, i + distances[i % 2]) for i in range(size)]
    return lax.ppermute(block, axis, [pair for pair in route if 0 <= pair[1] < size])


def summed(pair_sum, axis, add, add_last):
    size = lax.axis_size(axis)
    if size & (size - 1):
        even = lax.axis_index(axis) % 2 == 0
        return lax.psum(jnp.where(even, pair_sum, 0.0), axis)
    stride = 2
    while stride < size:
        hops = (stride, 2 * stride, 3 * stride) if 4 * stride <= size else (stride,)
        routes = [[(i, i ^ hop) for i in range(size)] for hop in hops]
        arrived = [lax.ppermute(pair_sum, axis, route) for route in routes]
        stride *= len(hops) + 1
        pair_sum = (add if stride < size else add_last)(pair_sum, *arrived)
    return pair_sum


def is_odd():
    return lax.rem(lax.axis_index("ctx"), 2) == 1


def product(left, right):
    return (left.astype(jnp.float32) * right.astype(jnp.float32)).astype(jnp.bfloat16)


def scaled(value, factor):
    return (value * factor.astype(jnp.float32)).astype(jnp.bfloat16)


def columns_of(group, width):
    return slice(group * width, (group + 1) * width)


def launch(odd, moves, sems, used):
    copies = [(*move, sems.at[used + place]) for place, move in enumerate(moves)]
    for parity, source, target, sem in copies:
        @pl.when(odd if parity else jnp.logical_not(odd))
        def _():
            pltpu.make_async_copy(source, target, sem).start()
    return copies


def finish(odd, copies):
    for parity, source, target, sem in copies:
        @pl.when(odd if parity else jnp.logical_not(odd))
        def _():
            pltpu.make_async_copy(source, target, sem).wait()


def skewed_sum(outer, rows):
    width = outer.shape[1]
    total = outer[:SUBLANES]
    for start in range(SUBLANES, rows, SUBLANES):
        total = total + pltpu.roll(outer[start : start + SUBLANES], width - start, 1)
    lines = [total[:1]] + [pltpu.roll(total[s : s + 1], width - s, 1) for s in range(1, SUBLANES)]
    return functools.reduce(jnp.add, lines)


def diagonal_kernel(query_hbm, keys_hbm, values_hbm, cotangent_hbm, out_ref, left, right, sems):
    odd = is_odd()
    half = out_ref.shape[1]
    low, high = pl.ds(0, half), pl.ds(half, half)
    copies = launch(
        odd,
        [
            (1, keys_hbm.at[:, low], left),
            (1, values_hbm.at[:, low], right),
            (0, cotangent_hbm.at[:, high], left),
            (0, query_hbm.at[:, high], right),
        ],
        sems,
        0,
    )
    finish(odd, copies)
    out_ref[...] = product(left[...], right[...])


def products_kernel(query_ref, keys_ref, values_ref, cotangent_ref, sent_ref, near_ref, across_ref):
    odd = is_odd()
    prod = product(keys_ref[...], values_ref[...])
    grad = product(cotangent_ref[...], query_ref[...])
    near_ref[...] = lax.select(odd, prod, grad)
    across_ref[...] = lax.select(odd, grad, prod)


def tiles_kernel(rows, taps_ref, ready_tiles, late_tiles):
    odd = is_odd()
    group_count, width = taps_ref.shape
    for group in range(group_count):
        row = taps_ref[group : group + 1, :].astype(jnp.float32)
        spread = jnp.concatenate(
            [jnp.zeros((SUBLANES, rows), jnp.float32), jnp.broadcast_to(row, (SUBLANES, width))],
            axis=1,
        )
        spread = pltpu.roll(spread, 0, 1, stride=1, stride_axis=0)
        bands = [
            pltpu.roll(spread, start, 1)[:, rows:] if start else spread[:, rows:]
            for start in range(0, rows, SUBLANES)
        ]
        band = jnp.concatenate(bands, axis=0)
        turned = [band[:, start : start + rows].T for start in range(0, width, rows)]
        turned = jnp.concatenate(turned, axis=1)
        ready_tiles[group] = lax.select(odd, band, turned).astype(jnp.bfloat16)
        late_tiles[group] = lax.select(odd, turned, band).astype(jnp.bfloat16)


def own_kernel(
    rows, ready_tiles, late_tiles, near_ref, across_ref, diagonal_ref, sum_ref, late_ref, ready_ref
):
    odd = is_odd()
    group_count, width = sum_ref.shape
    group_width = near_ref.shape[1] // group_count
    half = group_count // 2
    blank = jnp.zeros((rows, rows), jnp.float32)
    for group in range(group_count):
        columns = columns_of(group, group_width)
        late_ref[:, columns] = DOT(late_tiles[group, :, :rows], near_ref[:, columns])
        ready_ref[:, columns] = DOT(ready_tiles[group, :, :rows], across_ref[:, columns])
    middles = []
    for group in range(half):
        low, high = columns_of(group, group_width), columns_of(group + half, group_width)
        arrived = diagonal_ref[:, low]
        own = lax.select(odd, near_ref[:, high], near_ref[:, low])
        middles.append(DOT_ROWS(lax.select(odd, own, arrived), lax.select(odd, arrived, own)))
        tile = lax.select(
            odd, ready_tiles[group + half, :, rows : 2 * rows], ready_tiles[group, :, rows : 2 * rows]
        )
        more = DOT(tile, arrived)
        ready_ref[:, low] += lax.select(odd, blank, more)
        ready_ref[:, high] += lax.select(odd, more, blank)
    sums = []
    for group in range(group_count):
        columns = columns_of(group, group_width)
        near, across = near_ref[:, columns], across_ref[:, columns]
        outer = DOT_ROWS(lax.select(odd, near, across), lax.select(odd, across, near))
        if group < half:
            middle = lax.select(odd, blank, middles[group])
        else:
            middle = lax.select(odd, middles[group - half], blank)
        sums.append(skewed_sum(jnp.concatenate([outer, middle, blank], axis=1), rows)[:, : 2 * rows])
    sums = jnp.concatenate(sums, axis=0)
    sum_ref[...] = jnp.concatenate([sums, jnp.zeros((group_count, width - 2 * rows), jnp.float32)], axis=1)


def two_kernel(rows, sum_ref, near_ref, two_ref, out_ref):
    odd = is_odd()
    group_count, width = out_ref.shape
    group_width = near_ref.shape[1] // group_count
    blank = jnp.zeros((rows, rows), jnp.float32)
    sums = []
    for group in range(group_count):
        columns = columns_of(group, group_width)
        near, two = near_ref[:, columns], two_ref[:, columns]
        outer = DOT_ROWS(lax.select(odd, near, two), lax.select(odd, two, near))
        sums.append(skewed_sum(jnp.concatenate([blank, outer], axis=1), rows))
    sums = jnp.concatenate(sums, axis=0)
    out_ref[...] = sum_ref[...] + jnp.concatenate(
        [jnp.zeros((group_count, width - 2 * rows), jnp.float32), sums], axis=1
    )


def cross_kernel(rows, across_ref, swap_ref, out_ref):
    odd = is_odd()
    group_count, width = out_ref.shape
    group_width = across_ref.shape[1] // group_count
    blank = jnp.zeros((rows, rows), jnp.float32)
    sums = []
    for group in range(group_count):
        columns = columns_of(group, group_width)
        across, swap = across_ref[:, columns], swap_ref[:, columns]
        outer = DOT_ROWS(lax.select(odd, swap, across), lax.select(odd, across, swap))
        sums.append(skewed_sum(jnp.concatenate([blank, outer], axis=1), rows))
    sums = jnp.concatenate(sums, axis=0)
    out_ref[...] = jnp.concatenate([sums, jnp.zeros((group_count, width - 2 * rows), jnp.float32)], axis=1)


def pair_kernel(factor, sum_ref, other_ref, cross_ref, rest_ref, out_ref):
    out_ref[...] = (sum_ref[...] + other_ref[...] + cross_ref[...]) * factor


def add_kernel(*refs):
    *terms, _, out_ref = refs
    out_ref[...] = functools.reduce(jnp.add, [ref[...] for ref in terms])


def forward_kernel(far_ref, sum_ref, out_ref):
    half = out_ref.shape[1]
    out_ref[...] = lax.select(is_odd(), far_ref[:, half:], far_ref[:, :half])


def ready_kernel(
    tiles_ref, ready_ref, two_ref, query_ref, keys_ref, values_ref, sum_ref,
    gated_out, key_out, value_out, rest_ref, one, other, sems,
):
    odd = is_odd()
    group_count, rows, _ = tiles_ref.shape
    group_width = two_ref.shape[1] // group_count
    half = group_count // 2
    step = max(1, half // 2)
    copies = []
    for group in range(half):
        low, high = columns_of(group, group_width), columns_of(group + half, group_width)
        first = ready_ref[:, low] + DOT(tiles_ref[group, :, 2 * rows :], two_ref[:, low])
        second = ready_ref[:, high] + DOT(tiles_ref[group + half, :, 2 * rows :], two_ref[:, high])
        rest_ref[:, low] = lax.select(odd, first, second)
        known = lax.select(odd, second, first)
        one[:, low] = scaled(known, lax.select(odd, values_ref[:, high], query_ref[:, low]))
        other[:, low] = scaled(known, keys_ref[:, high])
        if (group + 1) % step == 0:
            start, size = (group + 1 - step) * group_width, step * group_width
            part, place = pl.ds(start, size), pl.ds(start + half * group_width, size)
            moves = [
                (0, one.at[:, part], gated_out.at[:, part]),
                (1, one.at[:, part], key_out.at[:, place]),
                (1, other.at[:, part], value_out.at[:, place]),
            ]
            copies += launch(odd, moves, sems, len(copies))
    finish(odd, copies)


def known_kernel(
    tiles_ref, late_ref, swap_ref, far_ref, query_ref, keys_ref, values_ref, gated_in, key_in, value_in,
    gated_out, key_out, value_out, done_ref, one, other, sems,
):
    odd = is_odd()
    done_ref[...] = jnp.zeros_like(done_ref)
    group_count, rows, _ = tiles_ref.shape
    group_width = far_ref.shape[1] // group_count
    step = max(1, group_count // PARTS)
    copies = []
    for group in range(group_count):
        columns = columns_of(group, group_width)
        arrived = jnp.concatenate([swap_ref[:, columns], far_ref[:, columns]], axis=0)
        late = late_ref[:, columns] + DOT(tiles_ref[group, :, rows:], arrived)
        one[:, columns] = scaled(late, lax.select(odd, query_ref[:, columns], values_ref[:, columns]))
        other[:, columns] = scaled(late, keys_ref[:, columns])
        if (group + 1) % step == 0:
            part = pl.ds((group + 1 - step) * group_width, step * group_width)
            moves = [
                (0, one.at[:, part], key_out.at[:, part]),
                (0, other.at[:, part], value_out.at[:, part]),
                (1, one.at[:, part], gated_out.at[:, part]),
            ]
            copies += launch(odd, moves, sems, len(copies))
    finish(odd, copies)


def last_kernel(
    tiles_ref, rest_ref, forwarded_ref, query_ref, keys_ref, values_ref, gated_in, key_in, value_in,
    gated_out, key_out, value_out, done_ref, one, other, sems,
):
    odd = is_odd()
    done_ref[...] = jnp.zeros_like(done_ref)
    group_count, rows, _ = tiles_ref.shape
    half = group_count // 2
    group_width = forwarded_ref.shape[1] // half
    step = max(1, half // 2)
    copies = []
    for group in range(half):
        low, high = columns_of(group, group_width), columns_of(group + half, group_width)
        tile = lax.select(
            odd, tiles_ref[group, :, rows : 2 * rows], tiles_ref[group + half, :, rows : 2 * rows]
        )
        ready = rest_ref[:, low] + DOT(tile, forwarded_ref[:, low])
        one[:, low] = scaled(ready, lax.select(odd, values_ref[:, low], query_ref[:, high]))
        other[:, low] = scaled(ready, keys_ref[:, low])
        if (group + 1) % step == 0:
            start, size = (group + 1 - step) * group_width, step * group_width
            part, place = pl.ds(start, size), pl.ds(start + half * group_width, size)
            moves = [
                (0, one.at[:, part], gated_out.at[:, place]),
                (1, one.at[:, part], key_out.at[:, part]),
                (1, other.at[:, part], value_out.at[:, part]),
            ]
            copies += launch(odd, moves, sems, len(copies))
    finish(odd, copies)


def shards(query, keys, values, cotangent, filter_taps):
    rows, local_width = query.shape
    group_count, taps = filter_taps.shape
    group_width = local_width // group_count
    half_width = local_width // 2
    factor = 1.0 / math.sqrt(rows * lax.axis_size("ctx") * group_width)

    def call(kernel, name, flops=10**6, **options):
        return pl.pallas_call(
            kernel,
            compiler_params=pltpu.CompilerParams(vmem_limit_bytes=VMEM_LIMIT),
            cost_estimate=pl.CostEstimate(flops=flops, bytes_accessed=10**5, transcendentals=0),
            name=name,
            **options,
        )

    def out_scratch(width, parts):
        return [pltpu.VMEM((rows, width), jnp.bfloat16)] * 2 + [pltpu.SemaphoreType.DMA((3 * parts,))]

    bf16, f32 = jnp.bfloat16, jnp.float32
    block, half_block = pltpu.VMEM((rows, local_width), bf16), pltpu.VMEM((rows, half_width), bf16)
    wide, half_wide = pltpu.VMEM((rows, local_width), f32), pltpu.VMEM((rows, half_width), f32)
    tiles, sums = pltpu.VMEM((group_count, rows, taps), bf16), pltpu.VMEM((group_count, taps), f32)
    mark = pltpu.VMEM((SUBLANES, group_width), f32)
    outs = [jax.ShapeDtypeStruct((rows, local_width), bf16)] * 3

    sent = call(
        diagonal_kernel,
        "diagonal",
        in_specs=[ANYWHERE] * 4,
        out_specs=WHOLE,
        out_shape=half_block,
        scratch_shapes=[half_block] * 2 + [pltpu.SemaphoreType.DMA((4,))],
    )(*in_hbm(query, keys, values, cotangent))
    diagonal = moved(sent, "ctx", (-1, 1))
    near, across = call(
        products_kernel,
        "products",
        in_specs=[WHOLE] * 4 + [ANYWHERE],
        out_specs=[WHOLE] * 2,
        out_shape=[block] * 2,
    )(*in_vmem(query, keys, values, cotangent), sent)
    two = moved(across, "ctx", (2, -2))
    far = moved(near, "ctx", (-2, 2))
    swap = moved(across, "ctx", (1, -1))

    ready_tiles, late_tiles = call(
        functools.partial(tiles_kernel, rows),
        "tiles",
        in_specs=[WHOLE],
        out_specs=[WHOLE] * 2,
        out_shape=[tiles] * 2,
    )(*in_vmem(filter_taps))
    partial, late, ready = call(
        functools.partial(own_kernel, rows),
        "own",
        flops=4 * 10**9,
        in_specs=[WHOLE] * 5,
        out_specs=[WHOLE] * 3,
        out_shape=[sums, wide, wide],
    )(*in_vmem(ready_tiles, late_tiles, near, across, diagonal))

    partial = call(
        functools.partial(two_kernel, rows),
        "two",
        in_specs=[WHOLE] * 3,
        out_specs=WHOLE,
        out_shape=sums,
    )(*in_vmem(partial, near, two))
    other = moved(partial, "ctx", (1, -1))

    gated, key_grad, value_grad, rest = call(
        ready_kernel,
        "ready",
        in_specs=[WHOLE] * 6 + [ANYWHERE],
        out_specs=[ANYWHERE] * 3 + [WHOLE],
        out_shape=outs + [half_wide],
        scratch_shapes=out_scratch(half_width, 2),
    )(*in_vmem(ready_tiles, ready, two, query, keys, values), partial)

    forwarded = call(
        forward_kernel,
        "forward",
        in_specs=[WHOLE, ANYWHERE],
        out_specs=WHOLE,
        out_shape=half_block,
    )(*in_vmem(far), partial)
    forwarded = moved(forwarded, "ctx", (1, -1))

    cross = call(
        functools.partial(cross_kernel, rows),
        "cross",
        in_specs=[WHOLE] * 2,
        out_specs=WHOLE,
        out_shape=sums,
    )(*in_vmem(across, swap))
    pair_sum = call(
        functools.partial(pair_kernel, factor),
        "pair",
        in_specs=[WHOLE] * 3 + [ANYWHERE],
        out_specs=WHOLE,
        out_shape=sums,
    )(*in_vmem(partial, other, cross), rest)

    gated, key_grad, value_grad, known_done = call(
        known_kernel,
        "known",
        flops=4 * 10**9,
        in_specs=[WHOLE] * 7 + [ANYWHERE] * 3,
        out_specs=[ANYWHERE] * 3 + [WHOLE],
        out_shape=outs + [mark],
        input_output_aliases={7: 0, 8: 1, 9: 2},
        scratch_shapes=out_scratch(local_width, PARTS),
    )(*in_vmem(late_tiles, late, swap, far, query, keys, values), gated, key_grad, value_grad)

    gated, key_grad, value_grad, last_done = call(
        last_kernel,
        "last",
        in_specs=[WHOLE] * 6 + [ANYWHERE] * 3,
        out_specs=[ANYWHERE] * 3 + [WHOLE],
        out_shape=outs + [mark],
        input_output_aliases={6: 0, 7: 1, 8: 2},
        scratch_shapes=out_scratch(half_width, 2),
    )(*in_vmem(ready_tiles, rest, forwarded, query, keys, values), gated, key_grad, value_grad)

    def adder(out_shape, after):
        def add(*terms):
            return call(
                add_kernel,
                "add",
                in_specs=[WHOLE] * len(terms) + [ANYWHERE],
                out_specs=WHOLE,
                out_shape=out_shape,
            )(*in_vmem(*terms), after)

        return add

    whole_sums = jax.ShapeDtypeStruct((group_count, taps), f32)
    filter_grad = summed(pair_sum, "ctx", adder(sums, known_done), adder(whole_sums, last_done))
    return (gated, key_grad, value_grad, filter_grad)


def solution(mesh):
    in_specs = (P("ctx", "grp"), P("ctx", "grp"), P("ctx", "grp"), P("ctx", "grp"), P("grp", None))
    out_specs = (P("ctx", "grp"), P("ctx", "grp"), P("ctx", "grp"), P("grp", None))
    return jax.shard_map(shards, mesh=mesh, in_specs=in_specs, out_specs=out_specs, check_vma=False)
```

```python
import functools
import math

import jax
import jax.numpy as jnp
from jax import lax
from jax.experimental import pallas as pl
from jax.experimental.pallas import tpu as pltpu
from jax.sharding import PartitionSpec as P

SUBLANES = 8
PARTS = 2
VMEM_LIMIT = 16 * 1024 * 1024
WHOLE = pl.BlockSpec(memory_space=pltpu.VMEM)
ANYWHERE = pl.BlockSpec(memory_space=pl.ANY)
DOT_ROWS = functools.partial(
    lax.dot_general,
    dimension_numbers=(((1,), (1,)), ((), ())),
    preferred_element_type=jnp.float32,
)
DOT = functools.partial(jnp.dot, preferred_element_type=jnp.float32)


def in_vmem(*arrays):
    return [pltpu.with_memory_space_constraint(array, pltpu.VMEM) for array in arrays]


def in_hbm(*arrays):
    return [pltpu.with_memory_space_constraint(array, pltpu.HBM) for array in arrays]


def moved(block, axis, distances):
    size = lax.axis_size(axis)
    route = [(i, i + distances[i % 2]) for i in range(size)]
    return lax.ppermute(block, axis, [pair for pair in route if 0 <= pair[1] < size])


def sum_terms(pair_sum, axis, add):
    size = lax.axis_size(axis)
    if size & (size - 1):
        even = lax.axis_index(axis) % 2 == 0
        return [lax.psum(jnp.where(even, pair_sum, 0.0), axis)]
    terms = [pair_sum]
    stride = 2
    while stride < size:
        own = terms[0] if len(terms) == 1 else add(*terms)
        hops = (3 * stride, 2 * stride, stride) if 4 * stride <= size else (stride,)
        terms = [own] + [lax.ppermute(own, axis, [(i, i ^ hop) for i in range(size)]) for hop in hops]
        stride *= len(hops) + 1
    return terms


def is_odd():
    return lax.rem(lax.axis_index("ctx"), 2) == 1


def product(left, right):
    return (left.astype(jnp.float32) * right.astype(jnp.float32)).astype(jnp.bfloat16)


def scaled(value, factor):
    return (value * factor.astype(jnp.float32)).astype(jnp.bfloat16)


def columns_of(group, width):
    return slice(group * width, (group + 1) * width)


def launch(odd, moves, sems, used):
    copies = [(*move, sems.at[used + place]) for place, move in enumerate(moves)]
    for parity, source, target, sem in copies:
        @pl.when(odd if parity else jnp.logical_not(odd))
        def _():
            pltpu.make_async_copy(source, target, sem).start()
    return copies


def finish(odd, copies):
    for parity, source, target, sem in copies:
        @pl.when(odd if parity else jnp.logical_not(odd))
        def _():
            pltpu.make_async_copy(source, target, sem).wait()


def skewed_sum(outer, rows):
    width = outer.shape[1]
    total = outer[:SUBLANES]
    for start in range(SUBLANES, rows, SUBLANES):
        total = total + pltpu.roll(outer[start : start + SUBLANES], width - start, 1)
    lines = [total[:1]] + [pltpu.roll(total[s : s + 1], width - s, 1) for s in range(1, SUBLANES)]
    return functools.reduce(jnp.add, lines)


def diagonal_kernel(query_hbm, keys_hbm, values_hbm, cotangent_hbm, out_ref, left, right, sems):
    odd = is_odd()
    half = out_ref.shape[1]
    low, high = pl.ds(0, half), pl.ds(half, half)
    copies = launch(
        odd,
        [
            (1, keys_hbm.at[:, low], left),
            (1, values_hbm.at[:, low], right),
            (0, cotangent_hbm.at[:, high], left),
            (0, query_hbm.at[:, high], right),
        ],
        sems,
        0,
    )
    finish(odd, copies)
    out_ref[...] = product(left[...], right[...])


def products_kernel(query_ref, keys_ref, values_ref, cotangent_ref, sent_ref, near_ref, across_ref):
    odd = is_odd()
    prod = product(keys_ref[...], values_ref[...])
    grad = product(cotangent_ref[...], query_ref[...])
    near_ref[...] = lax.select(odd, prod, grad)
    across_ref[...] = lax.select(odd, grad, prod)


def tiles_kernel(rows, taps_ref, ready_tiles, late_tiles):
    odd = is_odd()
    group_count, width = taps_ref.shape
    for group in range(group_count):
        row = taps_ref[group : group + 1, :].astype(jnp.float32)
        spread = jnp.concatenate(
            [jnp.zeros((SUBLANES, rows), jnp.float32), jnp.broadcast_to(row, (SUBLANES, width))],
            axis=1,
        )
        spread = pltpu.roll(spread, 0, 1, stride=1, stride_axis=0)
        bands = [
            pltpu.roll(spread, start, 1)[:, rows:] if start else spread[:, rows:]
            for start in range(0, rows, SUBLANES)
        ]
        band = jnp.concatenate(bands, axis=0)
        turned = [band[:, start : start + rows].T for start in range(0, width, rows)]
        turned = jnp.concatenate(turned, axis=1)
        ready_tiles[group] = lax.select(odd, band, turned).astype(jnp.bfloat16)
        late_tiles[group] = lax.select(odd, turned, band).astype(jnp.bfloat16)


def own_kernel(
    rows, ready_tiles, late_tiles, near_ref, across_ref, diagonal_ref, sum_ref, late_ref, ready_ref
):
    odd = is_odd()
    group_count, width = sum_ref.shape
    group_width = near_ref.shape[1] // group_count
    half = group_count // 2
    blank = jnp.zeros((rows, rows), jnp.float32)
    for group in range(group_count):
        columns = columns_of(group, group_width)
        late_ref[:, columns] = DOT(late_tiles[group, :, :rows], near_ref[:, columns])
        ready_ref[:, columns] = DOT(ready_tiles[group, :, :rows], across_ref[:, columns])
    middles = []
    for group in range(half):
        low, high = columns_of(group, group_width), columns_of(group + half, group_width)
        arrived = diagonal_ref[:, low]
        own = lax.select(odd, near_ref[:, high], near_ref[:, low])
        middles.append(DOT_ROWS(lax.select(odd, own, arrived), lax.select(odd, arrived, own)))
        tile = lax.select(
            odd, ready_tiles[group + half, :, rows : 2 * rows], ready_tiles[group, :, rows : 2 * rows]
        )
        more = DOT(tile, arrived)
        ready_ref[:, low] += lax.select(odd, blank, more)
        ready_ref[:, high] += lax.select(odd, more, blank)
    sums = []
    for group in range(group_count):
        columns = columns_of(group, group_width)
        near, across = near_ref[:, columns], across_ref[:, columns]
        outer = DOT_ROWS(lax.select(odd, near, across), lax.select(odd, across, near))
        if group < half:
            middle = lax.select(odd, blank, middles[group])
        else:
            middle = lax.select(odd, middles[group - half], blank)
        sums.append(skewed_sum(jnp.concatenate([outer, middle, blank], axis=1), rows)[:, : 2 * rows])
    sums = jnp.concatenate(sums, axis=0)
    sum_ref[...] = jnp.concatenate([sums, jnp.zeros((group_count, width - 2 * rows), jnp.float32)], axis=1)


def two_kernel(rows, sum_ref, near_ref, two_ref, out_ref):
    odd = is_odd()
    group_count, width = out_ref.shape
    group_width = near_ref.shape[1] // group_count
    blank = jnp.zeros((rows, rows), jnp.float32)
    sums = []
    for group in range(group_count):
        columns = columns_of(group, group_width)
        near, two = near_ref[:, columns], two_ref[:, columns]
        outer = DOT_ROWS(lax.select(odd, near, two), lax.select(odd, two, near))
        sums.append(skewed_sum(jnp.concatenate([blank, outer], axis=1), rows))
    sums = jnp.concatenate(sums, axis=0)
    out_ref[...] = sum_ref[...] + jnp.concatenate(
        [jnp.zeros((group_count, width - 2 * rows), jnp.float32), sums], axis=1
    )


def cross_kernel(rows, across_ref, swap_ref, out_ref):
    odd = is_odd()
    group_count, width = out_ref.shape
    group_width = across_ref.shape[1] // group_count
    blank = jnp.zeros((rows, rows), jnp.float32)
    sums = []
    for group in range(group_count):
        columns = columns_of(group, group_width)
        across, swap = across_ref[:, columns], swap_ref[:, columns]
        outer = DOT_ROWS(lax.select(odd, swap, across), lax.select(odd, across, swap))
        sums.append(skewed_sum(jnp.concatenate([blank, outer], axis=1), rows))
    sums = jnp.concatenate(sums, axis=0)
    out_ref[...] = jnp.concatenate([sums, jnp.zeros((group_count, width - 2 * rows), jnp.float32)], axis=1)


def pair_kernel(factor, sum_ref, other_ref, cross_ref, rest_ref, out_ref):
    out_ref[...] = (sum_ref[...] + other_ref[...] + cross_ref[...]) * factor


def add_kernel(*refs):
    *terms, out_ref = refs
    out_ref[...] = functools.reduce(jnp.add, [ref[...] for ref in terms])


def forward_kernel(far_ref, sum_ref, out_ref):
    half = out_ref.shape[1]
    out_ref[...] = lax.select(is_odd(), far_ref[:, half:], far_ref[:, :half])


def ready_kernel(
    tiles_ref, ready_ref, two_ref, query_ref, keys_ref, values_ref, sum_ref, rest_ref, one, other
):
    odd = is_odd()
    group_count, rows, _ = tiles_ref.shape
    group_width = two_ref.shape[1] // group_count
    half = group_count // 2
    for group in range(half):
        low, high = columns_of(group, group_width), columns_of(group + half, group_width)
        first = ready_ref[:, low] + DOT(tiles_ref[group, :, 2 * rows :], two_ref[:, low])
        second = ready_ref[:, high] + DOT(tiles_ref[group + half, :, 2 * rows :], two_ref[:, high])
        rest_ref[:, low] = lax.select(odd, first, second)
        known = lax.select(odd, second, first)
        one[:, low] = scaled(known, lax.select(odd, values_ref[:, high], query_ref[:, low]))
        other[:, low] = scaled(known, keys_ref[:, high])


def known_kernel(tiles_ref, late_ref, swap_ref, far_ref, query_ref, keys_ref, values_ref, one, other):
    odd = is_odd()
    group_count, rows, _ = tiles_ref.shape
    group_width = far_ref.shape[1] // group_count
    for group in range(group_count):
        columns = columns_of(group, group_width)
        arrived = jnp.concatenate([swap_ref[:, columns], far_ref[:, columns]], axis=0)
        late = late_ref[:, columns] + DOT(tiles_ref[group, :, rows:], arrived)
        one[:, columns] = scaled(late, lax.select(odd, query_ref[:, columns], values_ref[:, columns]))
        other[:, columns] = scaled(late, keys_ref[:, columns])


def last_kernel(
    tiles_ref, rest_ref, forwarded_ref, query_ref, keys_ref, values_ref,
    ready_one, ready_other, known_one, known_other, *refs,
):
    *terms, gated_out, key_out, value_out, filter_out, one, other, total, sems = refs
    odd = is_odd()
    group_count, rows, _ = tiles_ref.shape
    half = group_count // 2
    group_width = forwarded_ref.shape[1] // half
    step = max(1, half // PARTS)
    low_half, high_half = pl.ds(0, half * group_width), pl.ds(half * group_width, half * group_width)
    copies = launch(
        odd,
        [
            (0, known_one, key_out),
            (0, known_other, value_out),
            (0, ready_one, gated_out.at[:, low_half]),
            (1, known_one, gated_out),
            (1, ready_one, key_out.at[:, high_half]),
            (1, ready_other, value_out.at[:, high_half]),
        ],
        sems,
        0,
    )
    total[...] = functools.reduce(jnp.add, [term[...] for term in terms])
    copies += launch(odd, [(0, total, filter_out), (1, total, filter_out)], sems, len(copies))
    for group in range(half):
        low, high = columns_of(group, group_width), columns_of(group + half, group_width)
        tile = lax.select(
            odd, tiles_ref[group, :, rows : 2 * rows], tiles_ref[group + half, :, rows : 2 * rows]
        )
        ready = rest_ref[:, low] + DOT(tile, forwarded_ref[:, low])
        one[:, low] = scaled(ready, lax.select(odd, values_ref[:, low], query_ref[:, high]))
        other[:, low] = scaled(ready, keys_ref[:, low])
        if (group + 1) % step == 0:
            start, size = (group + 1 - step) * group_width, step * group_width
            part, place = pl.ds(start, size), pl.ds(start + half * group_width, size)
            moves = [
                (0, one.at[:, part], gated_out.at[:, place]),
                (1, one.at[:, part], key_out.at[:, part]),
                (1, other.at[:, part], value_out.at[:, part]),
            ]
            copies += launch(odd, moves, sems, len(copies))
    finish(odd, copies)


def shards(query, keys, values, cotangent, filter_taps):
    rows, local_width = query.shape
    group_count, taps = filter_taps.shape
    group_width = local_width // group_count
    half_width = local_width // 2
    factor = 1.0 / math.sqrt(rows * lax.axis_size("ctx") * group_width)

    def call(kernel, name, flops=10**6, **options):
        return pl.pallas_call(
            kernel,
            compiler_params=pltpu.CompilerParams(vmem_limit_bytes=VMEM_LIMIT),
            cost_estimate=pl.CostEstimate(flops=flops, bytes_accessed=10**5, transcendentals=0),
            name=name,
            **options,
        )

    bf16, f32 = jnp.bfloat16, jnp.float32
    block, half_block = pltpu.VMEM((rows, local_width), bf16), pltpu.VMEM((rows, half_width), bf16)
    wide, half_wide = pltpu.VMEM((rows, local_width), f32), pltpu.VMEM((rows, half_width), f32)
    tiles, sums = pltpu.VMEM((group_count, rows, taps), bf16), pltpu.VMEM((group_count, taps), f32)
    outs = [jax.ShapeDtypeStruct((rows, local_width), bf16)] * 3

    sent = call(
        diagonal_kernel,
        "diagonal",
        in_specs=[ANYWHERE] * 4,
        out_specs=WHOLE,
        out_shape=half_block,
        scratch_shapes=[half_block] * 2 + [pltpu.SemaphoreType.DMA((4,))],
    )(*in_hbm(query, keys, values, cotangent))
    diagonal = moved(sent, "ctx", (-1, 1))
    near, across = call(
        products_kernel,
        "products",
        in_specs=[WHOLE] * 4 + [ANYWHERE],
        out_specs=[WHOLE] * 2,
        out_shape=[block] * 2,
    )(*in_vmem(query, keys, values, cotangent), sent)
    two = moved(across, "ctx", (2, -2))
    far = moved(near, "ctx", (-2, 2))
    swap = moved(across, "ctx", (1, -1))

    ready_tiles, late_tiles = call(
        functools.partial(tiles_kernel, rows),
        "tiles",
        in_specs=[WHOLE],
        out_specs=[WHOLE] * 2,
        out_shape=[tiles] * 2,
    )(*in_vmem(filter_taps))
    partial, late, ready = call(
        functools.partial(own_kernel, rows),
        "own",
        flops=4 * 10**9,
        in_specs=[WHOLE] * 5,
        out_specs=[WHOLE] * 3,
        out_shape=[sums, wide, wide],
    )(*in_vmem(ready_tiles, late_tiles, near, across, diagonal))

    partial = call(
        functools.partial(two_kernel, rows),
        "two",
        in_specs=[WHOLE] * 3,
        out_specs=WHOLE,
        out_shape=sums,
    )(*in_vmem(partial, near, two))
    other = moved(partial, "ctx", (1, -1))

    rest, ready_one, ready_other = call(
        ready_kernel,
        "ready",
        in_specs=[WHOLE] * 6 + [ANYWHERE],
        out_specs=[WHOLE] * 3,
        out_shape=[half_wide, half_block, half_block],
    )(*in_vmem(ready_tiles, ready, two, query, keys, values), partial)

    forwarded = call(
        forward_kernel,
        "forward",
        in_specs=[WHOLE, ANYWHERE],
        out_specs=WHOLE,
        out_shape=half_block,
    )(*in_vmem(far), partial)
    forwarded = moved(forwarded, "ctx", (1, -1))

    cross = call(
        functools.partial(cross_kernel, rows),
        "cross",
        in_specs=[WHOLE] * 2,
        out_specs=WHOLE,
        out_shape=sums,
    )(*in_vmem(across, swap))
    pair_sum = call(
        functools.partial(pair_kernel, factor),
        "pair",
        in_specs=[WHOLE] * 3 + [ANYWHERE],
        out_specs=WHOLE,
        out_shape=sums,
    )(*in_vmem(partial, other, cross), rest)

    known_one, known_other = call(
        known_kernel,
        "known",
        flops=4 * 10**9,
        in_specs=[WHOLE] * 7,
        out_specs=[WHOLE] * 2,
        out_shape=[block] * 2,
    )(*in_vmem(late_tiles, late, swap, far, query, keys, values))

    def add(*terms):
        return call(
            add_kernel,
            "add",
            in_specs=[WHOLE] * len(terms),
            out_specs=WHOLE,
            out_shape=sums,
        )(*in_vmem(*terms))

    terms = sum_terms(pair_sum, "ctx", add)
    return call(
        last_kernel,
        "last",
        in_specs=[WHOLE] * (10 + len(terms)),
        out_specs=[ANYWHERE] * 4,
        out_shape=outs + [jax.ShapeDtypeStruct((group_count, taps), f32)],
        scratch_shapes=[half_block] * 2 + [sums, pltpu.SemaphoreType.DMA((8 + 3 * PARTS,))],
    )(
        *in_vmem(ready_tiles, rest, forwarded, query, keys, values),
        *in_vmem(ready_one, ready_other, known_one, known_other, *terms),
    )


def solution(mesh):
    in_specs = (P("ctx", "grp"), P("ctx", "grp"), P("ctx", "grp"), P("ctx", "grp"), P("grp", None))
    out_specs = (P("ctx", "grp"), P("ctx", "grp"), P("ctx", "grp"), P("grp", None))
    return jax.shard_map(shards, mesh=mesh, in_specs=in_specs, out_specs=out_specs, check_vma=False)
```

```python
import functools
import math

import jax
import jax.numpy as jnp
from jax import lax
from jax.experimental import pallas as pl
from jax.experimental.pallas import tpu as pltpu
from jax.sharding import PartitionSpec as P

SUBLANES = 8
PARTS = 2
VMEM_LIMIT = 16 * 1024 * 1024
WHOLE = pl.BlockSpec(memory_space=pltpu.VMEM)
ANYWHERE = pl.BlockSpec(memory_space=pl.ANY)
DOT_ROWS = functools.partial(
    lax.dot_general,
    dimension_numbers=(((1,), (1,)), ((), ())),
    preferred_element_type=jnp.float32,
)
DOT = functools.partial(jnp.dot, preferred_element_type=jnp.float32)


def in_vmem(*arrays):
    return [pltpu.with_memory_space_constraint(array, pltpu.VMEM) for array in arrays]


def in_hbm(*arrays):
    return [pltpu.with_memory_space_constraint(array, pltpu.HBM) for array in arrays]


def moved(block, axis, distances):
    size = lax.axis_size(axis)
    route = [(i, i + distances[i % 2]) for i in range(size)]
    return lax.ppermute(block, axis, [pair for pair in route if 0 <= pair[1] < size])


def sum_terms(pair_sum, axis, add):
    size = lax.axis_size(axis)
    if size & (size - 1):
        even = lax.axis_index(axis) % 2 == 0
        return [lax.psum(jnp.where(even, pair_sum, 0.0), axis)]
    terms = [pair_sum]
    stride = 2
    while stride < size:
        own = terms[0] if len(terms) == 1 else add(*terms)
        hops = (3 * stride, 2 * stride, stride) if 4 * stride <= size else (stride,)
        terms = [own] + [lax.ppermute(own, axis, [(i, i ^ hop) for i in range(size)]) for hop in hops]
        stride *= len(hops) + 1
    return terms


def is_odd():
    return lax.rem(lax.axis_index("ctx"), 2) == 1


def product(left, right):
    return (left.astype(jnp.float32) * right.astype(jnp.float32)).astype(jnp.bfloat16)


def scaled(value, factor):
    return (value * factor.astype(jnp.float32)).astype(jnp.bfloat16)


def columns_of(group, width):
    return slice(group * width, (group + 1) * width)


def launch(odd, moves, sems, used):
    copies = [(*move, sems.at[used + place]) for place, move in enumerate(moves)]
    for parity, source, target, sem in copies:
        @pl.when(odd if parity else jnp.logical_not(odd))
        def _():
            pltpu.make_async_copy(source, target, sem).start()
    return copies


def finish(odd, copies):
    for parity, source, target, sem in copies:
        @pl.when(odd if parity else jnp.logical_not(odd))
        def _():
            pltpu.make_async_copy(source, target, sem).wait()


def skewed_sum(outer, rows):
    width = outer.shape[1]
    total = outer[:SUBLANES]
    for start in range(SUBLANES, rows, SUBLANES):
        total = total + pltpu.roll(outer[start : start + SUBLANES], width - start, 1)
    lines = [total[:1]] + [pltpu.roll(total[s : s + 1], width - s, 1) for s in range(1, SUBLANES)]
    return functools.reduce(jnp.add, lines)


def diagonal_kernel(query_hbm, keys_hbm, values_hbm, cotangent_hbm, out_ref, left, right, sems):
    odd = is_odd()
    half = out_ref.shape[1]
    low, high = pl.ds(0, half), pl.ds(half, half)
    copies = launch(
        odd,
        [
            (1, keys_hbm.at[:, low], left),
            (1, values_hbm.at[:, low], right),
            (0, cotangent_hbm.at[:, high], left),
            (0, query_hbm.at[:, high], right),
        ],
        sems,
        0,
    )
    finish(odd, copies)
    out_ref[...] = product(left[...], right[...])


def products_kernel(query_ref, keys_ref, values_ref, cotangent_ref, sent_ref, near_ref, across_ref):
    odd = is_odd()
    prod = product(keys_ref[...], values_ref[...])
    grad = product(cotangent_ref[...], query_ref[...])
    near_ref[...] = lax.select(odd, prod, grad)
    across_ref[...] = lax.select(odd, grad, prod)


def tiles_kernel(rows, taps_ref, ready_tiles, late_tiles):
    odd = is_odd()
    group_count, width = taps_ref.shape
    for group in range(group_count):
        row = taps_ref[group : group + 1, :].astype(jnp.float32)
        spread = jnp.concatenate(
            [jnp.zeros((SUBLANES, rows), jnp.float32), jnp.broadcast_to(row, (SUBLANES, width))],
            axis=1,
        )
        spread = pltpu.roll(spread, 0, 1, stride=1, stride_axis=0)
        bands = [
            pltpu.roll(spread, start, 1)[:, rows:] if start else spread[:, rows:]
            for start in range(0, rows, SUBLANES)
        ]
        band = jnp.concatenate(bands, axis=0)
        turned = [band[:, start : start + rows].T for start in range(0, width, rows)]
        turned = jnp.concatenate(turned, axis=1)
        ready_tiles[group] = lax.select(odd, band, turned).astype(jnp.bfloat16)
        late_tiles[group] = lax.select(odd, turned, band).astype(jnp.bfloat16)


def own_kernel(
    rows, ready_tiles, late_tiles, near_ref, across_ref, diagonal_ref, sum_ref, late_ref, ready_ref
):
    odd = is_odd()
    group_count, width = sum_ref.shape
    group_width = near_ref.shape[1] // group_count
    half = group_count // 2
    blank = jnp.zeros((rows, rows), jnp.float32)
    for group in range(group_count):
        columns = columns_of(group, group_width)
        late_ref[:, columns] = DOT(late_tiles[group, :, :rows], near_ref[:, columns])
        ready_ref[:, columns] = DOT(ready_tiles[group, :, :rows], across_ref[:, columns])
    middles = []
    for group in range(half):
        low, high = columns_of(group, group_width), columns_of(group + half, group_width)
        arrived = diagonal_ref[:, low]
        own = lax.select(odd, near_ref[:, high], near_ref[:, low])
        middles.append(DOT_ROWS(lax.select(odd, own, arrived), lax.select(odd, arrived, own)))
        tile = lax.select(
            odd, ready_tiles[group + half, :, rows : 2 * rows], ready_tiles[group, :, rows : 2 * rows]
        )
        more = DOT(tile, arrived)
        ready_ref[:, low] += lax.select(odd, blank, more)
        ready_ref[:, high] += lax.select(odd, more, blank)
    sums = []
    for group in range(group_count):
        columns = columns_of(group, group_width)
        near, across = near_ref[:, columns], across_ref[:, columns]
        outer = DOT_ROWS(lax.select(odd, near, across), lax.select(odd, across, near))
        if group < half:
            middle = lax.select(odd, blank, middles[group])
        else:
            middle = lax.select(odd, middles[group - half], blank)
        sums.append(skewed_sum(jnp.concatenate([outer, middle, blank], axis=1), rows)[:, : 2 * rows])
    sums = jnp.concatenate(sums, axis=0)
    sum_ref[...] = jnp.concatenate([sums, jnp.zeros((group_count, width - 2 * rows), jnp.float32)], axis=1)


def two_kernel(rows, sum_ref, near_ref, two_ref, out_ref):
    odd = is_odd()
    group_count, width = out_ref.shape
    group_width = near_ref.shape[1] // group_count
    blank = jnp.zeros((rows, rows), jnp.float32)
    sums = []
    for group in range(group_count):
        columns = columns_of(group, group_width)
        near, two = near_ref[:, columns], two_ref[:, columns]
        outer = DOT_ROWS(lax.select(odd, near, two), lax.select(odd, two, near))
        sums.append(skewed_sum(jnp.concatenate([blank, outer], axis=1), rows))
    sums = jnp.concatenate(sums, axis=0)
    out_ref[...] = sum_ref[...] + jnp.concatenate(
        [jnp.zeros((group_count, width - 2 * rows), jnp.float32), sums], axis=1
    )


def cross_kernel(rows, across_ref, swap_ref, out_ref):
    odd = is_odd()
    group_count, width = out_ref.shape
    group_width = across_ref.shape[1] // group_count
    blank = jnp.zeros((rows, rows), jnp.float32)
    sums = []
    for group in range(group_count):
        columns = columns_of(group, group_width)
        across, swap = across_ref[:, columns], swap_ref[:, columns]
        outer = DOT_ROWS(lax.select(odd, swap, across), lax.select(odd, across, swap))
        sums.append(skewed_sum(jnp.concatenate([blank, outer], axis=1), rows))
    sums = jnp.concatenate(sums, axis=0)
    out_ref[...] = jnp.concatenate([sums, jnp.zeros((group_count, width - 2 * rows), jnp.float32)], axis=1)


def pair_kernel(factor, sum_ref, other_ref, cross_ref, rest_ref, out_ref):
    out_ref[...] = (sum_ref[...] + other_ref[...] + cross_ref[...]) * factor


def add_kernel(*refs):
    *terms, _, out_ref = refs
    out_ref[...] = functools.reduce(jnp.add, [ref[...] for ref in terms])


def forward_kernel(far_ref, rest_ref, out_ref):
    half = out_ref.shape[1]
    out_ref[...] = lax.select(is_odd(), far_ref[:, half:], far_ref[:, :half])


def ready_kernel(
    tiles_ref, ready_ref, two_ref, query_ref, keys_ref, values_ref, sum_ref, rest_ref, one, other
):
    odd = is_odd()
    group_count, rows, _ = tiles_ref.shape
    group_width = two_ref.shape[1] // group_count
    half = group_count // 2
    for group in range(half):
        low, high = columns_of(group, group_width), columns_of(group + half, group_width)
        first = ready_ref[:, low] + DOT(tiles_ref[group, :, 2 * rows :], two_ref[:, low])
        second = ready_ref[:, high] + DOT(tiles_ref[group + half, :, 2 * rows :], two_ref[:, high])
        rest_ref[:, low] = lax.select(odd, first, second)
        known = lax.select(odd, second, first)
        one[:, low] = scaled(known, lax.select(odd, values_ref[:, high], query_ref[:, low]))
        other[:, low] = scaled(known, keys_ref[:, high])


def known_kernel(tiles_ref, late_ref, swap_ref, far_ref, query_ref, keys_ref, values_ref, one, other):
    odd = is_odd()
    group_count, rows, _ = tiles_ref.shape
    group_width = far_ref.shape[1] // group_count
    for group in range(group_count):
        columns = columns_of(group, group_width)
        arrived = jnp.concatenate([swap_ref[:, columns], far_ref[:, columns]], axis=0)
        late = late_ref[:, columns] + DOT(tiles_ref[group, :, rows:], arrived)
        one[:, columns] = scaled(late, lax.select(odd, query_ref[:, columns], values_ref[:, columns]))
        other[:, columns] = scaled(late, keys_ref[:, columns])


def last_kernel(
    tiles_ref, rest_ref, forwarded_ref, query_ref, keys_ref, values_ref,
    ready_one, ready_other, known_one, known_other,
    gated_out, key_out, value_out, mark_ref, one, other, sems,
):
    odd = is_odd()
    mark_ref[...] = jnp.zeros_like(mark_ref)
    group_count, rows, _ = tiles_ref.shape
    half = group_count // 2
    group_width = forwarded_ref.shape[1] // half
    step = max(1, half // PARTS)
    low_half, high_half = pl.ds(0, half * group_width), pl.ds(half * group_width, half * group_width)
    copies = launch(
        odd,
        [
            (0, known_one, key_out),
            (0, known_other, value_out),
            (0, ready_one, gated_out.at[:, low_half]),
            (1, known_one, gated_out),
            (1, ready_one, key_out.at[:, high_half]),
            (1, ready_other, value_out.at[:, high_half]),
        ],
        sems,
        0,
    )
    for group in range(half):
        low, high = columns_of(group, group_width), columns_of(group + half, group_width)
        tile = lax.select(
            odd, tiles_ref[group, :, rows : 2 * rows], tiles_ref[group + half, :, rows : 2 * rows]
        )
        ready = rest_ref[:, low] + DOT(tile, forwarded_ref[:, low])
        one[:, low] = scaled(ready, lax.select(odd, values_ref[:, low], query_ref[:, high]))
        other[:, low] = scaled(ready, keys_ref[:, low])
        if (group + 1) % step == 0:
            start, size = (group + 1 - step) * group_width, step * group_width
            part, place = pl.ds(start, size), pl.ds(start + half * group_width, size)
            moves = [
                (0, one.at[:, part], gated_out.at[:, place]),
                (1, one.at[:, part], key_out.at[:, part]),
                (1, other.at[:, part], value_out.at[:, part]),
            ]
            copies += launch(odd, moves, sems, len(copies))
    finish(odd, copies)


def shards(query, keys, values, cotangent, filter_taps):
    rows, local_width = query.shape
    group_count, taps = filter_taps.shape
    group_width = local_width // group_count
    half_width = local_width // 2
    factor = 1.0 / math.sqrt(rows * lax.axis_size("ctx") * group_width)

    def call(kernel, name, flops=10**6, **options):
        return pl.pallas_call(
            kernel,
            compiler_params=pltpu.CompilerParams(vmem_limit_bytes=VMEM_LIMIT),
            cost_estimate=pl.CostEstimate(flops=flops, bytes_accessed=10**5, transcendentals=0),
            name=name,
            **options,
        )

    bf16, f32 = jnp.bfloat16, jnp.float32
    block, half_block = pltpu.VMEM((rows, local_width), bf16), pltpu.VMEM((rows, half_width), bf16)
    wide, half_wide = pltpu.VMEM((rows, local_width), f32), pltpu.VMEM((rows, half_width), f32)
    tiles, sums = pltpu.VMEM((group_count, rows, taps), bf16), pltpu.VMEM((group_count, taps), f32)
    outs = [jax.ShapeDtypeStruct((rows, local_width), bf16)] * 3

    sent = call(
        diagonal_kernel,
        "diagonal",
        in_specs=[ANYWHERE] * 4,
        out_specs=WHOLE,
        out_shape=half_block,
        scratch_shapes=[half_block] * 2 + [pltpu.SemaphoreType.DMA((4,))],
    )(*in_hbm(query, keys, values, cotangent))
    diagonal = moved(sent, "ctx", (-1, 1))
    near, across = call(
        products_kernel,
        "products",
        in_specs=[WHOLE] * 4 + [ANYWHERE],
        out_specs=[WHOLE] * 2,
        out_shape=[block] * 2,
    )(*in_vmem(query, keys, values, cotangent), sent)
    two = moved(across, "ctx", (2, -2))
    far = moved(near, "ctx", (-2, 2))
    swap = moved(across, "ctx", (1, -1))

    ready_tiles, late_tiles = call(
        functools.partial(tiles_kernel, rows),
        "tiles",
        in_specs=[WHOLE],
        out_specs=[WHOLE] * 2,
        out_shape=[tiles] * 2,
    )(*in_vmem(filter_taps))
    partial, late, ready = call(
        functools.partial(own_kernel, rows),
        "own",
        flops=4 * 10**9,
        in_specs=[WHOLE] * 5,
        out_specs=[WHOLE] * 3,
        out_shape=[sums, wide, wide],
    )(*in_vmem(ready_tiles, late_tiles, near, across, diagonal))

    partial = call(
        functools.partial(two_kernel, rows),
        "two",
        in_specs=[WHOLE] * 3,
        out_specs=WHOLE,
        out_shape=sums,
    )(*in_vmem(partial, near, two))
    other = moved(partial, "ctx", (1, -1))

    rest, ready_one, ready_other = call(
        ready_kernel,
        "ready",
        in_specs=[WHOLE] * 6 + [ANYWHERE],
        out_specs=[WHOLE] * 3,
        out_shape=[half_wide, half_block, half_block],
    )(*in_vmem(ready_tiles, ready, two, query, keys, values), partial)

    forwarded = call(
        forward_kernel,
        "forward",
        in_specs=[WHOLE, ANYWHERE],
        out_specs=WHOLE,
        out_shape=half_block,
    )(*in_vmem(far), rest)
    forwarded = moved(forwarded, "ctx", (1, -1))

    cross = call(
        functools.partial(cross_kernel, rows),
        "cross",
        in_specs=[WHOLE] * 2,
        out_specs=WHOLE,
        out_shape=sums,
    )(*in_vmem(across, swap))
    pair_sum = call(
        functools.partial(pair_kernel, factor),
        "pair",
        in_specs=[WHOLE] * 3 + [ANYWHERE],
        out_specs=WHOLE,
        out_shape=sums,
    )(*in_vmem(partial, other, cross), rest)

    known_one, known_other = call(
        known_kernel,
        "known",
        flops=4 * 10**9,
        in_specs=[WHOLE] * 7,
        out_specs=[WHOLE] * 2,
        out_shape=[block] * 2,
    )(*in_vmem(late_tiles, late, swap, far, query, keys, values))

    def add(*terms, out_shape=sums, after=known_one):
        return call(
            add_kernel,
            "add",
            in_specs=[WHOLE] * len(terms) + [ANYWHERE],
            out_specs=WHOLE,
            out_shape=out_shape,
        )(*in_vmem(*terms), after)

    terms = sum_terms(pair_sum, "ctx", add)
    gated, key_grad, value_grad, mark = call(
        last_kernel,
        "last",
        in_specs=[WHOLE] * 10,
        out_specs=[ANYWHERE] * 3 + [WHOLE],
        out_shape=outs + [pltpu.VMEM((SUBLANES, group_width), f32)],
        scratch_shapes=[half_block] * 2 + [pltpu.SemaphoreType.DMA((6 + 3 * PARTS,))],
    )(
        *in_vmem(ready_tiles, rest, forwarded, query, keys, values),
        *in_vmem(ready_one, ready_other, known_one, known_other),
    )
    whole_sums = jax.ShapeDtypeStruct((group_count, taps), f32)
    return (gated, key_grad, value_grad, add(*terms, out_shape=whole_sums, after=mark))


def solution(mesh):
    in_specs = (P("ctx", "grp"), P("ctx", "grp"), P("ctx", "grp"), P("ctx", "grp"), P("grp", None))
    out_specs = (P("ctx", "grp"), P("ctx", "grp"), P("ctx", "grp"), P("grp", None))
    return jax.shard_map(shards, mesh=mesh, in_specs=in_specs, out_specs=out_specs, check_vma=False)
```

```python
import functools
import math

import jax
import jax.numpy as jnp
from jax import lax
from jax.experimental import pallas as pl
from jax.experimental.pallas import tpu as pltpu
from jax.sharding import PartitionSpec as P

SUBLANES = 8
PARTS = 2
VMEM_LIMIT = 16 * 1024 * 1024
WHOLE = pl.BlockSpec(memory_space=pltpu.VMEM)
ANYWHERE = pl.BlockSpec(memory_space=pl.ANY)
DOT_ROWS = functools.partial(
    lax.dot_general,
    dimension_numbers=(((1,), (1,)), ((), ())),
    preferred_element_type=jnp.float32,
)
DOT = functools.partial(jnp.dot, preferred_element_type=jnp.float32)


def in_vmem(*arrays):
    return [pltpu.with_memory_space_constraint(array, pltpu.VMEM) for array in arrays]


def in_hbm(*arrays):
    return [pltpu.with_memory_space_constraint(array, pltpu.HBM) for array in arrays]


def moved(block, axis, distances):
    size = lax.axis_size(axis)
    route = [(i, i + distances[i % 2]) for i in range(size)]
    return lax.ppermute(block, axis, [pair for pair in route if 0 <= pair[1] < size])


def sum_terms(pair_sum, axis, add):
    size = lax.axis_size(axis)
    if size & (size - 1):
        even = lax.axis_index(axis) % 2 == 0
        return [lax.psum(jnp.where(even, pair_sum, 0.0), axis)]
    terms = [pair_sum]
    stride = 2
    while stride < size:
        own = terms[0] if len(terms) == 1 else add(*terms)
        hops = (3 * stride, 2 * stride, stride) if 4 * stride <= size else (stride,)
        terms = [own] + [lax.ppermute(own, axis, [(i, i ^ hop) for i in range(size)]) for hop in hops]
        stride *= len(hops) + 1
    return terms


def is_odd():
    return lax.rem(lax.axis_index("ctx"), 2) == 1


def product(left, right):
    return (left.astype(jnp.float32) * right.astype(jnp.float32)).astype(jnp.bfloat16)


def scaled(value, factor):
    return (value * factor.astype(jnp.float32)).astype(jnp.bfloat16)


def columns_of(group, width):
    return slice(group * width, (group + 1) * width)


def launch(odd, moves, sems, used, priority=0):
    copies = [(*move, sems.at[used + place]) for place, move in enumerate(moves)]
    for parity, source, target, sem in copies:
        @pl.when(odd if parity else jnp.logical_not(odd))
        def _():
            pltpu.make_async_copy(source, target, sem).start(priority=priority)
    return copies


def finish(odd, copies):
    for parity, source, target, sem in copies:
        @pl.when(odd if parity else jnp.logical_not(odd))
        def _():
            pltpu.make_async_copy(source, target, sem).wait()


def skewed_sum(outer, rows):
    width = outer.shape[1]
    total = outer[:SUBLANES]
    for start in range(SUBLANES, rows, SUBLANES):
        total = total + pltpu.roll(outer[start : start + SUBLANES], width - start, 1)
    lines = [total[:1]] + [pltpu.roll(total[s : s + 1], width - s, 1) for s in range(1, SUBLANES)]
    return functools.reduce(jnp.add, lines)


def diagonal_kernel(query_hbm, keys_hbm, values_hbm, cotangent_hbm, out_ref, left, right, sems):
    odd = is_odd()
    rows, half = out_ref.shape
    size = rows // PARTS
    pieces = []
    for piece in range(PARTS):
        lines, low, high = pl.ds(piece * size, size), pl.ds(0, half), pl.ds(half, half)
        moves = [
            (1, keys_hbm.at[lines, low], left.at[lines]),
            (1, values_hbm.at[lines, low], right.at[lines]),
            (0, cotangent_hbm.at[lines, high], left.at[lines]),
            (0, query_hbm.at[lines, high], right.at[lines]),
        ]
        pieces.append((lines, launch(odd, moves, sems, 4 * piece, priority=1)))
    for lines, copies in pieces:
        finish(odd, copies)
        out_ref[lines, :] = product(left[lines, :], right[lines, :])


def products_kernel(query_ref, keys_ref, values_ref, cotangent_ref, sent_ref, near_ref, across_ref):
    odd = is_odd()
    prod = product(keys_ref[...], values_ref[...])
    grad = product(cotangent_ref[...], query_ref[...])
    near_ref[...] = lax.select(odd, prod, grad)
    across_ref[...] = lax.select(odd, grad, prod)


def tiles_kernel(rows, taps_ref, ready_tiles, late_tiles):
    odd = is_odd()
    group_count, width = taps_ref.shape
    for group in range(group_count):
        row = taps_ref[group : group + 1, :].astype(jnp.float32)
        spread = jnp.concatenate(
            [jnp.zeros((SUBLANES, rows), jnp.float32), jnp.broadcast_to(row, (SUBLANES, width))],
            axis=1,
        )
        spread = pltpu.roll(spread, 0, 1, stride=1, stride_axis=0)
        bands = [
            pltpu.roll(spread, start, 1)[:, rows:] if start else spread[:, rows:]
            for start in range(0, rows, SUBLANES)
        ]
        band = jnp.concatenate(bands, axis=0)
        turned = [band[:, start : start + rows].T for start in range(0, width, rows)]
        turned = jnp.concatenate(turned, axis=1)
        ready_tiles[group] = lax.select(odd, band, turned).astype(jnp.bfloat16)
        late_tiles[group] = lax.select(odd, turned, band).astype(jnp.bfloat16)


def own_kernel(
    rows, ready_tiles, late_tiles, near_ref, across_ref, diagonal_ref, sum_ref, late_ref, ready_ref
):
    odd = is_odd()
    group_count, width = sum_ref.shape
    group_width = near_ref.shape[1] // group_count
    half = group_count // 2
    blank = jnp.zeros((rows, rows), jnp.float32)
    for group in range(group_count):
        columns = columns_of(group, group_width)
        late_ref[:, columns] = DOT(late_tiles[group, :, :rows], near_ref[:, columns])
        ready_ref[:, columns] = DOT(ready_tiles[group, :, :rows], across_ref[:, columns])
    middles = []
    for group in range(half):
        low, high = columns_of(group, group_width), columns_of(group + half, group_width)
        arrived = diagonal_ref[:, low]
        own = lax.select(odd, near_ref[:, high], near_ref[:, low])
        middles.append(DOT_ROWS(lax.select(odd, own, arrived), lax.select(odd, arrived, own)))
        tile = lax.select(
            odd, ready_tiles[group + half, :, rows : 2 * rows], ready_tiles[group, :, rows : 2 * rows]
        )
        more = DOT(tile, arrived)
        ready_ref[:, low] += lax.select(odd, blank, more)
        ready_ref[:, high] += lax.select(odd, more, blank)
    sums = []
    for group in range(group_count):
        columns = columns_of(group, group_width)
        near, across = near_ref[:, columns], across_ref[:, columns]
        outer = DOT_ROWS(lax.select(odd, near, across), lax.select(odd, across, near))
        if group < half:
            middle = lax.select(odd, blank, middles[group])
        else:
            middle = lax.select(odd, middles[group - half], blank)
        sums.append(skewed_sum(jnp.concatenate([outer, middle, blank], axis=1), rows)[:, : 2 * rows])
    sums = jnp.concatenate(sums, axis=0)
    sum_ref[...] = jnp.concatenate([sums, jnp.zeros((group_count, width - 2 * rows), jnp.float32)], axis=1)


def two_kernel(rows, sum_ref, near_ref, two_ref, out_ref):
    odd = is_odd()
    group_count, width = out_ref.shape
    group_width = near_ref.shape[1] // group_count
    blank = jnp.zeros((rows, rows), jnp.float32)
    sums = []
    for group in range(group_count):
        columns = columns_of(group, group_width)
        near, two = near_ref[:, columns], two_ref[:, columns]
        outer = DOT_ROWS(lax.select(odd, near, two), lax.select(odd, two, near))
        sums.append(skewed_sum(jnp.concatenate([blank, outer], axis=1), rows))
    sums = jnp.concatenate(sums, axis=0)
    out_ref[...] = sum_ref[...] + jnp.concatenate(
        [jnp.zeros((group_count, width - 2 * rows), jnp.float32), sums], axis=1
    )


def cross_kernel(rows, across_ref, swap_ref, out_ref):
    odd = is_odd()
    group_count, width = out_ref.shape
    group_width = across_ref.shape[1] // group_count
    blank = jnp.zeros((rows, rows), jnp.float32)
    sums = []
    for group in range(group_count):
        columns = columns_of(group, group_width)
        across, swap = across_ref[:, columns], swap_ref[:, columns]
        outer = DOT_ROWS(lax.select(odd, swap, across), lax.select(odd, across, swap))
        sums.append(skewed_sum(jnp.concatenate([blank, outer], axis=1), rows))
    sums = jnp.concatenate(sums, axis=0)
    out_ref[...] = jnp.concatenate([sums, jnp.zeros((group_count, width - 2 * rows), jnp.float32)], axis=1)


def pair_kernel(factor, sum_ref, other_ref, cross_ref, rest_ref, out_ref):
    out_ref[...] = (sum_ref[...] + other_ref[...] + cross_ref[...]) * factor


def add_kernel(*refs):
    *terms, _, out_ref = refs
    out_ref[...] = functools.reduce(jnp.add, [ref[...] for ref in terms])


def forward_kernel(far_ref, rest_ref, out_ref):
    half = out_ref.shape[1]
    out_ref[...] = lax.select(is_odd(), far_ref[:, half:], far_ref[:, :half])


def ready_kernel(
    tiles_ref, ready_ref, two_ref, query_ref, keys_ref, values_ref, sum_ref, rest_ref, one, other
):
    odd = is_odd()
    group_count, rows, _ = tiles_ref.shape
    group_width = two_ref.shape[1] // group_count
    half = group_count // 2
    for group in range(half):
        low, high = columns_of(group, group_width), columns_of(group + half, group_width)
        first = ready_ref[:, low] + DOT(tiles_ref[group, :, 2 * rows :], two_ref[:, low])
        second = ready_ref[:, high] + DOT(tiles_ref[group + half, :, 2 * rows :], two_ref[:, high])
        rest_ref[:, low] = lax.select(odd, first, second)
        known = lax.select(odd, second, first)
        one[:, low] = scaled(known, lax.select(odd, values_ref[:, high], query_ref[:, low]))
        other[:, low] = scaled(known, keys_ref[:, high])


def known_kernel(tiles_ref, late_ref, swap_ref, far_ref, query_ref, keys_ref, values_ref, one, other):
    odd = is_odd()
    group_count, rows, _ = tiles_ref.shape
    group_width = far_ref.shape[1] // group_count
    for group in range(group_count):
        columns = columns_of(group, group_width)
        arrived = jnp.concatenate([swap_ref[:, columns], far_ref[:, columns]], axis=0)
        late = late_ref[:, columns] + DOT(tiles_ref[group, :, rows:], arrived)
        one[:, columns] = scaled(late, lax.select(odd, query_ref[:, columns], values_ref[:, columns]))
        other[:, columns] = scaled(late, keys_ref[:, columns])


def last_kernel(
    tiles_ref, rest_ref, forwarded_ref, query_ref, keys_ref, values_ref,
    ready_one, ready_other, known_one, known_other,
    gated_out, key_out, value_out, mark_ref, one, other, sems,
):
    odd = is_odd()
    mark_ref[...] = jnp.zeros_like(mark_ref)
    group_count, rows, _ = tiles_ref.shape
    half = group_count // 2
    group_width = forwarded_ref.shape[1] // half
    step = max(1, half // PARTS)
    low_half, high_half = pl.ds(0, half * group_width), pl.ds(half * group_width, half * group_width)
    copies = launch(
        odd,
        [
            (0, known_one, key_out),
            (0, known_other, value_out),
            (0, ready_one, gated_out.at[:, low_half]),
            (1, known_one, gated_out),
            (1, ready_one, key_out.at[:, high_half]),
            (1, ready_other, value_out.at[:, high_half]),
        ],
        sems,
        0,
    )
    for group in range(half):
        low, high = columns_of(group, group_width), columns_of(group + half, group_width)
        tile = lax.select(
            odd, tiles_ref[group, :, rows : 2 * rows], tiles_ref[group + half, :, rows : 2 * rows]
        )
        ready = rest_ref[:, low] + DOT(tile, forwarded_ref[:, low])
        one[:, low] = scaled(ready, lax.select(odd, values_ref[:, low], query_ref[:, high]))
        other[:, low] = scaled(ready, keys_ref[:, low])
        if (group + 1) % step == 0:
            start, size = (group + 1 - step) * group_width, step * group_width
            part, place = pl.ds(start, size), pl.ds(start + half * group_width, size)
            moves = [
                (0, one.at[:, part], gated_out.at[:, place]),
                (1, one.at[:, part], key_out.at[:, part]),
                (1, other.at[:, part], value_out.at[:, part]),
            ]
            copies += launch(odd, moves, sems, len(copies))
    finish(odd, copies)


def shards(query, keys, values, cotangent, filter_taps):
    rows, local_width = query.shape
    group_count, taps = filter_taps.shape
    group_width = local_width // group_count
    half_width = local_width // 2
    factor = 1.0 / math.sqrt(rows * lax.axis_size("ctx") * group_width)

    def call(kernel, name, flops=10**6, **options):
        return pl.pallas_call(
            kernel,
            compiler_params=pltpu.CompilerParams(vmem_limit_bytes=VMEM_LIMIT),
            cost_estimate=pl.CostEstimate(flops=flops, bytes_accessed=10**5, transcendentals=0),
            name=name,
            **options,
        )

    bf16, f32 = jnp.bfloat16, jnp.float32
    block, half_block = pltpu.VMEM((rows, local_width), bf16), pltpu.VMEM((rows, half_width), bf16)
    wide, half_wide = pltpu.VMEM((rows, local_width), f32), pltpu.VMEM((rows, half_width), f32)
    tiles, sums = pltpu.VMEM((group_count, rows, taps), bf16), pltpu.VMEM((group_count, taps), f32)
    outs = [jax.ShapeDtypeStruct((rows, local_width), bf16)] * 3

    sent = call(
        diagonal_kernel,
        "diagonal",
        in_specs=[ANYWHERE] * 4,
        out_specs=WHOLE,
        out_shape=half_block,
        scratch_shapes=[half_block] * 2 + [pltpu.SemaphoreType.DMA((4 * PARTS,))],
    )(*in_hbm(query, keys, values, cotangent))
    diagonal = moved(sent, "ctx", (-1, 1))
    near, across = call(
        products_kernel,
        "products",
        in_specs=[WHOLE] * 4 + [ANYWHERE],
        out_specs=[WHOLE] * 2,
        out_shape=[block] * 2,
    )(*in_vmem(query, keys, values, cotangent), sent)
    two = moved(across, "ctx", (2, -2))
    far = moved(near, "ctx", (-2, 2))
    swap = moved(across, "ctx", (1, -1))

    ready_tiles, late_tiles = call(
        functools.partial(tiles_kernel, rows),
        "tiles",
        in_specs=[WHOLE],
        out_specs=[WHOLE] * 2,
        out_shape=[tiles] * 2,
    )(*in_vmem(filter_taps))
    partial, late, ready = call(
        functools.partial(own_kernel, rows),
        "own",
        flops=4 * 10**9,
        in_specs=[WHOLE] * 5,
        out_specs=[WHOLE] * 3,
        out_shape=[sums, wide, wide],
    )(*in_vmem(ready_tiles, late_tiles, near, across, diagonal))

    partial = call(
        functools.partial(two_kernel, rows),
        "two",
        in_specs=[WHOLE] * 3,
        out_specs=WHOLE,
        out_shape=sums,
    )(*in_vmem(partial, near, two))
    other = moved(partial, "ctx", (1, -1))

    rest, ready_one, ready_other = call(
        ready_kernel,
        "ready",
        in_specs=[WHOLE] * 6 + [ANYWHERE],
        out_specs=[WHOLE] * 3,
        out_shape=[half_wide, half_block, half_block],
    )(*in_vmem(ready_tiles, ready, two, query, keys, values), partial)

    forwarded = call(
        forward_kernel,
        "forward",
        in_specs=[WHOLE, ANYWHERE],
        out_specs=WHOLE,
        out_shape=half_block,
    )(*in_vmem(far), rest)
    forwarded = moved(forwarded, "ctx", (1, -1))

    cross = call(
        functools.partial(cross_kernel, rows),
        "cross",
        in_specs=[WHOLE] * 2,
        out_specs=WHOLE,
        out_shape=sums,
    )(*in_vmem(across, swap))
    pair_sum = call(
        functools.partial(pair_kernel, factor),
        "pair",
        in_specs=[WHOLE] * 3 + [ANYWHERE],
        out_specs=WHOLE,
        out_shape=sums,
    )(*in_vmem(partial, other, cross), rest)

    known_one, known_other = call(
        known_kernel,
        "known",
        flops=4 * 10**9,
        in_specs=[WHOLE] * 7,
        out_specs=[WHOLE] * 2,
        out_shape=[block] * 2,
    )(*in_vmem(late_tiles, late, swap, far, query, keys, values))

    def add(*terms, out_shape=sums, after=known_one):
        return call(
            add_kernel,
            "add",
            in_specs=[WHOLE] * len(terms) + [ANYWHERE],
            out_specs=WHOLE,
            out_shape=out_shape,
        )(*in_vmem(*terms), after)

    terms = sum_terms(pair_sum, "ctx", add)
    gated, key_grad, value_grad, mark = call(
        last_kernel,
        "last",
        in_specs=[WHOLE] * 10,
        out_specs=[ANYWHERE] * 3 + [WHOLE],
        out_shape=outs + [pltpu.VMEM((SUBLANES, group_width), f32)],
        scratch_shapes=[half_block] * 2 + [pltpu.SemaphoreType.DMA((6 + 3 * PARTS,))],
    )(
        *in_vmem(ready_tiles, rest, forwarded, query, keys, values),
        *in_vmem(ready_one, ready_other, known_one, known_other),
    )
    whole_sums = jax.ShapeDtypeStruct((group_count, taps), f32)
    return (gated, key_grad, value_grad, add(*terms, out_shape=whole_sums, after=mark))


def solution(mesh):
    in_specs = (P("ctx", "grp"), P("ctx", "grp"), P("ctx", "grp"), P("ctx", "grp"), P("grp", None))
    out_specs = (P("ctx", "grp"), P("ctx", "grp"), P("ctx", "grp"), P("grp", None))
    return jax.shard_map(shards, mesh=mesh, in_specs=in_specs, out_specs=out_specs, check_vma=False)
```

```python
import functools
import math

import jax
import jax.numpy as jnp
from jax import lax
from jax.experimental import pallas as pl
from jax.experimental.pallas import tpu as pltpu
from jax.sharding import PartitionSpec as P

SUBLANES = 8
PARTS = 2
VMEM_LIMIT = 16 * 1024 * 1024
WHOLE = pl.BlockSpec(memory_space=pltpu.VMEM)
ANYWHERE = pl.BlockSpec(memory_space=pl.ANY)
DOT_ROWS = functools.partial(
    lax.dot_general,
    dimension_numbers=(((1,), (1,)), ((), ())),
    preferred_element_type=jnp.float32,
)
DOT = functools.partial(jnp.dot, preferred_element_type=jnp.float32)


def in_vmem(*arrays):
    return [pltpu.with_memory_space_constraint(array, pltpu.VMEM) for array in arrays]


def in_hbm(*arrays):
    return [pltpu.with_memory_space_constraint(array, pltpu.HBM) for array in arrays]


def moved(block, axis, distances):
    size = lax.axis_size(axis)
    route = [(i, i + distances[i % 2]) for i in range(size)]
    return lax.ppermute(block, axis, [pair for pair in route if 0 <= pair[1] < size])


def sum_terms(pair_sum, axis, add):
    size = lax.axis_size(axis)
    if size & (size - 1):
        even = lax.axis_index(axis) % 2 == 0
        return [lax.psum(jnp.where(even, pair_sum, 0.0), axis)]
    terms = [pair_sum]
    stride = 2
    while stride < size:
        own = terms[0] if len(terms) == 1 else add(*terms)
        hops = (3 * stride, 2 * stride, stride) if 4 * stride <= size else (stride,)
        terms = [own] + [lax.ppermute(own, axis, [(i, i ^ hop) for i in range(size)]) for hop in hops]
        stride *= len(hops) + 1
    return terms


def is_odd():
    return lax.rem(lax.axis_index("ctx"), 2) == 1


def is_ahead():
    return lax.rem(lax.axis_index("grp"), 2) == 1


def early_groups(group_count):
    return 3 * group_count // 4


def product(left, right):
    return (left.astype(jnp.float32) * right.astype(jnp.float32)).astype(jnp.bfloat16)


def scaled(value, factor):
    return (value * factor.astype(jnp.float32)).astype(jnp.bfloat16)


def columns_of(group, width):
    return slice(group * width, (group + 1) * width)


def launch(odd, moves, sems, used):
    copies = [(*move, sems.at[used + place]) for place, move in enumerate(moves)]
    for parity, source, target, sem in copies:
        @pl.when(odd if parity else jnp.logical_not(odd))
        def _():
            pltpu.make_async_copy(source, target, sem).start()
    return copies


def finish(odd, copies):
    for parity, source, target, sem in copies:
        @pl.when(odd if parity else jnp.logical_not(odd))
        def _():
            pltpu.make_async_copy(source, target, sem).wait()


def skewed_sum(outer, rows):
    width = outer.shape[1]
    total = outer[:SUBLANES]
    for start in range(SUBLANES, rows, SUBLANES):
        total = total + pltpu.roll(outer[start : start + SUBLANES], width - start, 1)
    lines = [total[:1]] + [pltpu.roll(total[s : s + 1], width - s, 1) for s in range(1, SUBLANES)]
    return functools.reduce(jnp.add, lines)


def diagonal_kernel(
    query_hbm, keys_hbm, values_hbm, cotangent_hbm, taps_hbm, out_ref, ready_tiles, late_tiles,
    left, right, taps_ref, sems,
):
    odd = is_odd()
    rows, half = out_ref.shape
    group_count = taps_ref.shape[0]
    low, high = pl.ds(0, half), pl.ds(half, half)
    copies = launch(
        odd,
        [
            (1, keys_hbm.at[:, low], left),
            (1, values_hbm.at[:, low], right),
            (0, cotangent_hbm.at[:, high], left),
            (0, query_hbm.at[:, high], right),
        ],
        sems,
        0,
    )

    @pl.when(is_ahead())
    def _():
        copy = pltpu.make_async_copy(taps_hbm, taps_ref, sems.at[4])
        copy.start()
        copy.wait()
        build_tiles(odd, rows, taps_ref, ready_tiles, late_tiles, range(early_groups(group_count)))

    finish(odd, copies)
    out_ref[...] = product(left[...], right[...])


def products_kernel(query_ref, keys_ref, values_ref, cotangent_ref, sent_ref, near_ref, across_ref):
    odd = is_odd()
    prod = product(keys_ref[...], values_ref[...])
    grad = product(cotangent_ref[...], query_ref[...])
    near_ref[...] = lax.select(odd, prod, grad)
    across_ref[...] = lax.select(odd, grad, prod)


def build_tiles(odd, rows, taps_ref, ready_tiles, late_tiles, groups):
    width = taps_ref.shape[1]
    for group in groups:
        row = taps_ref[group : group + 1, :].astype(jnp.float32)
        spread = jnp.concatenate(
            [jnp.zeros((SUBLANES, rows), jnp.float32), jnp.broadcast_to(row, (SUBLANES, width))],
            axis=1,
        )
        spread = pltpu.roll(spread, 0, 1, stride=1, stride_axis=0)
        bands = [
            pltpu.roll(spread, start, 1)[:, rows:] if start else spread[:, rows:]
            for start in range(0, rows, SUBLANES)
        ]
        band = jnp.concatenate(bands, axis=0)
        turned = [band[:, start : start + rows].T for start in range(0, width, rows)]
        turned = jnp.concatenate(turned, axis=1)
        ready_tiles[group] = lax.select(odd, band, turned).astype(jnp.bfloat16)
        late_tiles[group] = lax.select(odd, turned, band).astype(jnp.bfloat16)


def tiles_kernel(rows, taps_ref, ready_in, late_in, ready_tiles, late_tiles):
    odd = is_odd()
    group_count = taps_ref.shape[0]
    early = early_groups(group_count)

    @pl.when(jnp.logical_not(is_ahead()))
    def _():
        build_tiles(odd, rows, taps_ref, ready_tiles, late_tiles, range(early))

    @pl.when(is_ahead())
    def _():
        ready_tiles[:early] = ready_in[:early]
        late_tiles[:early] = late_in[:early]

    build_tiles(odd, rows, taps_ref, ready_tiles, late_tiles, range(early, group_count))


def own_kernel(
    rows, ready_tiles, late_tiles, near_ref, across_ref, diagonal_ref, sum_ref, late_ref, ready_ref
):
    odd = is_odd()
    group_count, width = sum_ref.shape
    group_width = near_ref.shape[1] // group_count
    half = group_count // 2
    blank = jnp.zeros((rows, rows), jnp.float32)
    for group in range(group_count):
        columns = columns_of(group, group_width)
        late_ref[:, columns] = DOT(late_tiles[group, :, :rows], near_ref[:, columns])
        ready_ref[:, columns] = DOT(ready_tiles[group, :, :rows], across_ref[:, columns])
    middles = []
    for group in range(half):
        low, high = columns_of(group, group_width), columns_of(group + half, group_width)
        arrived = diagonal_ref[:, low]
        own = lax.select(odd, near_ref[:, high], near_ref[:, low])
        middles.append(DOT_ROWS(lax.select(odd, own, arrived), lax.select(odd, arrived, own)))
        tile = lax.select(
            odd, ready_tiles[group + half, :, rows : 2 * rows], ready_tiles[group, :, rows : 2 * rows]
        )
        more = DOT(tile, arrived)
        ready_ref[:, low] += lax.select(odd, blank, more)
        ready_ref[:, high] += lax.select(odd, more, blank)
    sums = []
    for group in range(group_count):
        columns = columns_of(group, group_width)
        near, across = near_ref[:, columns], across_ref[:, columns]
        outer = DOT_ROWS(lax.select(odd, near, across), lax.select(odd, across, near))
        if group < half:
            middle = lax.select(odd, blank, middles[group])
        else:
            middle = lax.select(odd, middles[group - half], blank)
        sums.append(skewed_sum(jnp.concatenate([outer, middle, blank], axis=1), rows)[:, : 2 * rows])
    sums = jnp.concatenate(sums, axis=0)
    sum_ref[...] = jnp.concatenate([sums, jnp.zeros((group_count, width - 2 * rows), jnp.float32)], axis=1)


def two_kernel(rows, sum_ref, near_ref, two_ref, out_ref):
    odd = is_odd()
    group_count, width = out_ref.shape
    group_width = near_ref.shape[1] // group_count
    blank = jnp.zeros((rows, rows), jnp.float32)
    sums = []
    for group in range(group_count):
        columns = columns_of(group, group_width)
        near, two = near_ref[:, columns], two_ref[:, columns]
        outer = DOT_ROWS(lax.select(odd, near, two), lax.select(odd, two, near))
        sums.append(skewed_sum(jnp.concatenate([blank, outer], axis=1), rows))
    sums = jnp.concatenate(sums, axis=0)
    out_ref[...] = sum_ref[...] + jnp.concatenate(
        [jnp.zeros((group_count, width - 2 * rows), jnp.float32), sums], axis=1
    )


def cross_kernel(rows, across_ref, swap_ref, out_ref):
    odd = is_odd()
    group_count, width = out_ref.shape
    group_width = across_ref.shape[1] // group_count
    blank = jnp.zeros((rows, rows), jnp.float32)
    sums = []
    for group in range(group_count):
        columns = columns_of(group, group_width)
        across, swap = across_ref[:, columns], swap_ref[:, columns]
        outer = DOT_ROWS(lax.select(odd, swap, across), lax.select(odd, across, swap))
        sums.append(skewed_sum(jnp.concatenate([blank, outer], axis=1), rows))
    sums = jnp.concatenate(sums, axis=0)
    out_ref[...] = jnp.concatenate([sums, jnp.zeros((group_count, width - 2 * rows), jnp.float32)], axis=1)


def pair_kernel(factor, sum_ref, other_ref, cross_ref, rest_ref, out_ref):
    out_ref[...] = (sum_ref[...] + other_ref[...] + cross_ref[...]) * factor


def add_kernel(*refs):
    *terms, _, out_ref = refs
    out_ref[...] = functools.reduce(jnp.add, [ref[...] for ref in terms])


def forward_kernel(far_ref, rest_ref, out_ref):
    half = out_ref.shape[1]
    out_ref[...] = lax.select(is_odd(), far_ref[:, half:], far_ref[:, :half])


def ready_kernel(
    tiles_ref, ready_ref, two_ref, query_ref, keys_ref, values_ref, sum_ref, rest_ref, one, other
):
    odd = is_odd()
    group_count, rows, _ = tiles_ref.shape
    group_width = two_ref.shape[1] // group_count
    half = group_count // 2
    for group in range(half):
        low, high = columns_of(group, group_width), columns_of(group + half, group_width)
        first = ready_ref[:, low] + DOT(tiles_ref[group, :, 2 * rows :], two_ref[:, low])
        second = ready_ref[:, high] + DOT(tiles_ref[group + half, :, 2 * rows :], two_ref[:, high])
        rest_ref[:, low] = lax.select(odd, first, second)
        known = lax.select(odd, second, first)
        one[:, low] = scaled(known, lax.select(odd, values_ref[:, high], query_ref[:, low]))
        other[:, low] = scaled(known, keys_ref[:, high])


def known_kernel(tiles_ref, late_ref, swap_ref, far_ref, query_ref, keys_ref, values_ref, one, other):
    odd = is_odd()
    group_count, rows, _ = tiles_ref.shape
    group_width = far_ref.shape[1] // group_count
    for group in range(group_count):
        columns = columns_of(group, group_width)
        arrived = jnp.concatenate([swap_ref[:, columns], far_ref[:, columns]], axis=0)
        late = late_ref[:, columns] + DOT(tiles_ref[group, :, rows:], arrived)
        one[:, columns] = scaled(late, lax.select(odd, query_ref[:, columns], values_ref[:, columns]))
        other[:, columns] = scaled(late, keys_ref[:, columns])


def last_kernel(
    tiles_ref, rest_ref, forwarded_ref, query_ref, keys_ref, values_ref,
    ready_one, ready_other, known_one, known_other,
    gated_out, key_out, value_out, mark_ref, one, other, sems,
):
    odd = is_odd()
    mark_ref[...] = jnp.zeros_like(mark_ref)
    group_count, rows, _ = tiles_ref.shape
    half = group_count // 2
    group_width = forwarded_ref.shape[1] // half
    step = max(1, half // PARTS)
    low_half, high_half = pl.ds(0, half * group_width), pl.ds(half * group_width, half * group_width)
    copies = launch(
        odd,
        [
            (0, known_one, key_out),
            (0, known_other, value_out),
            (0, ready_one, gated_out.at[:, low_half]),
            (1, known_one, gated_out),
            (1, ready_one, key_out.at[:, high_half]),
            (1, ready_other, value_out.at[:, high_half]),
        ],
        sems,
        0,
    )
    for group in range(half):
        low, high = columns_of(group, group_width), columns_of(group + half, group_width)
        tile = lax.select(
            odd, tiles_ref[group, :, rows : 2 * rows], tiles_ref[group + half, :, rows : 2 * rows]
        )
        ready = rest_ref[:, low] + DOT(tile, forwarded_ref[:, low])
        one[:, low] = scaled(ready, lax.select(odd, values_ref[:, low], query_ref[:, high]))
        other[:, low] = scaled(ready, keys_ref[:, low])
        if (group + 1) % step == 0:
            start, size = (group + 1 - step) * group_width, step * group_width
            part, place = pl.ds(start, size), pl.ds(start + half * group_width, size)
            moves = [
                (0, one.at[:, part], gated_out.at[:, place]),
                (1, one.at[:, part], key_out.at[:, part]),
                (1, other.at[:, part], value_out.at[:, part]),
            ]
            copies += launch(odd, moves, sems, len(copies))
    finish(odd, copies)


def shards(query, keys, values, cotangent, filter_taps):
    rows, local_width = query.shape
    group_count, taps = filter_taps.shape
    group_width = local_width // group_count
    half_width = local_width // 2
    factor = 1.0 / math.sqrt(rows * lax.axis_size("ctx") * group_width)

    def call(kernel, name, flops=10**6, **options):
        return pl.pallas_call(
            kernel,
            compiler_params=pltpu.CompilerParams(vmem_limit_bytes=VMEM_LIMIT),
            cost_estimate=pl.CostEstimate(flops=flops, bytes_accessed=10**5, transcendentals=0),
            name=name,
            **options,
        )

    bf16, f32 = jnp.bfloat16, jnp.float32
    block, half_block = pltpu.VMEM((rows, local_width), bf16), pltpu.VMEM((rows, half_width), bf16)
    wide, half_wide = pltpu.VMEM((rows, local_width), f32), pltpu.VMEM((rows, half_width), f32)
    tiles, sums = pltpu.VMEM((group_count, rows, taps), bf16), pltpu.VMEM((group_count, taps), f32)
    outs = [jax.ShapeDtypeStruct((rows, local_width), bf16)] * 3

    sent, ready_tiles, late_tiles = call(
        diagonal_kernel,
        "diagonal",
        in_specs=[ANYWHERE] * 5,
        out_specs=[WHOLE] * 3,
        out_shape=[half_block, tiles, tiles],
        scratch_shapes=[half_block] * 2
        + [pltpu.VMEM((group_count, taps), bf16), pltpu.SemaphoreType.DMA((5,))],
    )(*in_hbm(query, keys, values, cotangent, filter_taps))
    diagonal = moved(sent, "ctx", (-1, 1))
    near, across = call(
        products_kernel,
        "products",
        in_specs=[WHOLE] * 4 + [ANYWHERE],
        out_specs=[WHOLE] * 2,
        out_shape=[block] * 2,
    )(*in_vmem(query, keys, values, cotangent), sent)
    two = moved(across, "ctx", (2, -2))
    far = moved(near, "ctx", (-2, 2))
    swap = moved(across, "ctx", (1, -1))

    ready_tiles, late_tiles = call(
        functools.partial(tiles_kernel, rows),
        "tiles",
        in_specs=[WHOLE] * 3,
        out_specs=[WHOLE] * 2,
        out_shape=[tiles] * 2,
    )(*in_vmem(filter_taps, ready_tiles, late_tiles))
    partial, late, ready = call(
        functools.partial(own_kernel, rows),
        "own",
        flops=4 * 10**9,
        in_specs=[WHOLE] * 5,
        out_specs=[WHOLE] * 3,
        out_shape=[sums, wide, wide],
    )(*in_vmem(ready_tiles, late_tiles, near, across, diagonal))

    partial = call(
        functools.partial(two_kernel, rows),
        "two",
        in_specs=[WHOLE] * 3,
        out_specs=WHOLE,
        out_shape=sums,
    )(*in_vmem(partial, near, two))
    other = moved(partial, "ctx", (1, -1))

    rest, ready_one, ready_other = call(
        ready_kernel,
        "ready",
        in_specs=[WHOLE] * 6 + [ANYWHERE],
        out_specs=[WHOLE] * 3,
        out_shape=[half_wide, half_block, half_block],
    )(*in_vmem(ready_tiles, ready, two, query, keys, values), partial)

    forwarded = call(
        forward_kernel,
        "forward",
        in_specs=[WHOLE, ANYWHERE],
        out_specs=WHOLE,
        out_shape=half_block,
    )(*in_vmem(far), rest)
    forwarded = moved(forwarded, "ctx", (1, -1))

    cross = call(
        functools.partial(cross_kernel, rows),
        "cross",
        in_specs=[WHOLE] * 2,
        out_specs=WHOLE,
        out_shape=sums,
    )(*in_vmem(across, swap))
    pair_sum = call(
        functools.partial(pair_kernel, factor),
        "pair",
        in_specs=[WHOLE] * 3 + [ANYWHERE],
        out_specs=WHOLE,
        out_shape=sums,
    )(*in_vmem(partial, other, cross), rest)

    known_one, known_other = call(
        known_kernel,
        "known",
        flops=4 * 10**9,
        in_specs=[WHOLE] * 7,
        out_specs=[WHOLE] * 2,
        out_shape=[block] * 2,
    )(*in_vmem(late_tiles, late, swap, far, query, keys, values))

    def add(*terms, out_shape=sums, after=known_one):
        return call(
            add_kernel,
            "add",
            in_specs=[WHOLE] * len(terms) + [ANYWHERE],
            out_specs=WHOLE,
            out_shape=out_shape,
        )(*in_vmem(*terms), after)

    terms = sum_terms(pair_sum, "ctx", add)
    gated, key_grad, value_grad, mark = call(
        last_kernel,
        "last",
        in_specs=[WHOLE] * 10,
        out_specs=[ANYWHERE] * 3 + [WHOLE],
        out_shape=outs + [pltpu.VMEM((SUBLANES, group_width), f32)],
        scratch_shapes=[half_block] * 2 + [pltpu.SemaphoreType.DMA((6 + 3 * PARTS,))],
    )(
        *in_vmem(ready_tiles, rest, forwarded, query, keys, values),
        *in_vmem(ready_one, ready_other, known_one, known_other),
    )
    whole_sums = jax.ShapeDtypeStruct((group_count, taps), f32)
    return (gated, key_grad, value_grad, add(*terms, out_shape=whole_sums, after=mark))


def solution(mesh):
    in_specs = (P("ctx", "grp"), P("ctx", "grp"), P("ctx", "grp"), P("ctx", "grp"), P("grp", None))
    out_specs = (P("ctx", "grp"), P("ctx", "grp"), P("ctx", "grp"), P("grp", None))
    return jax.shard_map(shards, mesh=mesh, in_specs=in_specs, out_specs=out_specs, check_vma=False)
```

```python
import functools
import math

import jax
import jax.numpy as jnp
from jax import lax
from jax.experimental import pallas as pl
from jax.experimental.pallas import tpu as pltpu
from jax.sharding import PartitionSpec as P

SUBLANES = 8
PARTS = 2
VMEM_LIMIT = 16 * 1024 * 1024
WHOLE = pl.BlockSpec(memory_space=pltpu.VMEM)
ANYWHERE = pl.BlockSpec(memory_space=pl.ANY)
DOT_ROWS = functools.partial(
    lax.dot_general,
    dimension_numbers=(((1,), (1,)), ((), ())),
    preferred_element_type=jnp.float32,
)
DOT = functools.partial(jnp.dot, preferred_element_type=jnp.float32)


def in_vmem(*arrays):
    return [pltpu.with_memory_space_constraint(array, pltpu.VMEM) for array in arrays]


def in_hbm(*arrays):
    return [pltpu.with_memory_space_constraint(array, pltpu.HBM) for array in arrays]


def moved(block, axis, distances):
    size = lax.axis_size(axis)
    route = [(i, i + distances[i % 2]) for i in range(size)]
    return lax.ppermute(block, axis, [pair for pair in route if 0 <= pair[1] < size])


def sum_terms(pair_sum, axis, add):
    size = lax.axis_size(axis)
    if size & (size - 1):
        even = lax.axis_index(axis) % 2 == 0
        return [lax.psum(jnp.where(even, pair_sum, 0.0), axis)]
    terms = [pair_sum]
    stride = 2
    while stride < size:
        own = terms[0] if len(terms) == 1 else add(*terms)
        members = 4 if 4 * stride <= size else 2
        terms = [own]
        for turn in range(1, members):
            places = [(i, i // stride % members) for i in range(size)]
            route = [(i, i + ((place + turn) % members - place) * stride) for i, place in places]
            terms.append(lax.ppermute(own, axis, route))
        stride *= members
    return terms


def is_odd():
    return lax.rem(lax.axis_index("ctx"), 2) == 1


def product(left, right):
    return (left.astype(jnp.float32) * right.astype(jnp.float32)).astype(jnp.bfloat16)


def scaled(value, factor):
    return (value * factor.astype(jnp.float32)).astype(jnp.bfloat16)


def columns_of(group, width):
    return slice(group * width, (group + 1) * width)


def launch(odd, moves, sems, used):
    copies = [(*move, sems.at[used + place]) for place, move in enumerate(moves)]
    for parity, source, target, sem in copies:
        @pl.when(odd if parity else jnp.logical_not(odd))
        def _():
            pltpu.make_async_copy(source, target, sem).start()
    return copies


def finish(odd, copies):
    for parity, source, target, sem in copies:
        @pl.when(odd if parity else jnp.logical_not(odd))
        def _():
            pltpu.make_async_copy(source, target, sem).wait()


def skewed_sum(outer, rows):
    width = outer.shape[1]
    total = outer[:SUBLANES]
    for start in range(SUBLANES, rows, SUBLANES):
        total = total + pltpu.roll(outer[start : start + SUBLANES], width - start, 1)
    lines = [total[:1]] + [pltpu.roll(total[s : s + 1], width - s, 1) for s in range(1, SUBLANES)]
    return functools.reduce(jnp.add, lines)


def diagonal_kernel(query_hbm, keys_hbm, values_hbm, cotangent_hbm, out_ref, left, right, sems):
    odd = is_odd()
    half = out_ref.shape[1]
    low, high = pl.ds(0, half), pl.ds(half, half)
    copies = launch(
        odd,
        [
            (1, keys_hbm.at[:, low], left),
            (1, values_hbm.at[:, low], right),
            (0, cotangent_hbm.at[:, high], left),
            (0, query_hbm.at[:, high], right),
        ],
        sems,
        0,
    )
    finish(odd, copies)
    out_ref[...] = product(left[...], right[...])


def products_kernel(query_ref, keys_ref, values_ref, cotangent_ref, sent_ref, near_ref, across_ref):
    odd = is_odd()
    prod = product(keys_ref[...], values_ref[...])
    grad = product(cotangent_ref[...], query_ref[...])
    near_ref[...] = lax.select(odd, prod, grad)
    across_ref[...] = lax.select(odd, grad, prod)


def tiles_kernel(rows, taps_ref, ready_tiles, late_tiles):
    odd = is_odd()
    group_count, width = taps_ref.shape
    for group in range(group_count):
        row = taps_ref[group : group + 1, :].astype(jnp.float32)
        spread = jnp.concatenate(
            [jnp.zeros((SUBLANES, rows), jnp.float32), jnp.broadcast_to(row, (SUBLANES, width))],
            axis=1,
        )
        spread = pltpu.roll(spread, 0, 1, stride=1, stride_axis=0)
        bands = [
            pltpu.roll(spread, start, 1)[:, rows:] if start else spread[:, rows:]
            for start in range(0, rows, SUBLANES)
        ]
        band = jnp.concatenate(bands, axis=0)
        turned = [band[:, start : start + rows].T for start in range(0, width, rows)]
        turned = jnp.concatenate(turned, axis=1)
        ready_tiles[group] = lax.select(odd, band, turned).astype(jnp.bfloat16)
        late_tiles[group] = lax.select(odd, turned, band).astype(jnp.bfloat16)


def own_kernel(
    rows, ready_tiles, late_tiles, near_ref, across_ref, diagonal_ref, sum_ref, late_ref, ready_ref
):
    odd = is_odd()
    group_count, width = sum_ref.shape
    group_width = near_ref.shape[1] // group_count
    half = group_count // 2
    blank = jnp.zeros((rows, rows), jnp.float32)
    for group in range(group_count):
        columns = columns_of(group, group_width)
        late_ref[:, columns] = DOT(late_tiles[group, :, :rows], near_ref[:, columns])
        ready_ref[:, columns] = DOT(ready_tiles[group, :, :rows], across_ref[:, columns])
    middles = []
    for group in range(half):
        low, high = columns_of(group, group_width), columns_of(group + half, group_width)
        arrived = diagonal_ref[:, low]
        own = lax.select(odd, near_ref[:, high], near_ref[:, low])
        middles.append(DOT_ROWS(lax.select(odd, own, arrived), lax.select(odd, arrived, own)))
        tile = lax.select(
            odd, ready_tiles[group + half, :, rows : 2 * rows], ready_tiles[group, :, rows : 2 * rows]
        )
        more = DOT(tile, arrived)
        ready_ref[:, low] += lax.select(odd, blank, more)
        ready_ref[:, high] += lax.select(odd, more, blank)
    sums = []
    for group in range(group_count):
        columns = columns_of(group, group_width)
        near, across = near_ref[:, columns], across_ref[:, columns]
        outer = DOT_ROWS(lax.select(odd, near, across), lax.select(odd, across, near))
        if group < half:
            middle = lax.select(odd, blank, middles[group])
        else:
            middle = lax.select(odd, middles[group - half], blank)
        sums.append(skewed_sum(jnp.concatenate([outer, middle, blank], axis=1), rows)[:, : 2 * rows])
    sums = jnp.concatenate(sums, axis=0)
    sum_ref[...] = jnp.concatenate([sums, jnp.zeros((group_count, width - 2 * rows), jnp.float32)], axis=1)


def two_kernel(rows, sum_ref, near_ref, two_ref, out_ref):
    odd = is_odd()
    group_count, width = out_ref.shape
    group_width = near_ref.shape[1] // group_count
    blank = jnp.zeros((rows, rows), jnp.float32)
    sums = []
    for group in range(group_count):
        columns = columns_of(group, group_width)
        near, two = near_ref[:, columns], two_ref[:, columns]
        outer = DOT_ROWS(lax.select(odd, near, two), lax.select(odd, two, near))
        sums.append(skewed_sum(jnp.concatenate([blank, outer], axis=1), rows))
    sums = jnp.concatenate(sums, axis=0)
    out_ref[...] = sum_ref[...] + jnp.concatenate(
        [jnp.zeros((group_count, width - 2 * rows), jnp.float32), sums], axis=1
    )


def cross_kernel(rows, across_ref, swap_ref, out_ref):
    odd = is_odd()
    group_count, width = out_ref.shape
    group_width = across_ref.shape[1] // group_count
    blank = jnp.zeros((rows, rows), jnp.float32)
    sums = []
    for group in range(group_count):
        columns = columns_of(group, group_width)
        across, swap = across_ref[:, columns], swap_ref[:, columns]
        outer = DOT_ROWS(lax.select(odd, swap, across), lax.select(odd, across, swap))
        sums.append(skewed_sum(jnp.concatenate([blank, outer], axis=1), rows))
    sums = jnp.concatenate(sums, axis=0)
    out_ref[...] = jnp.concatenate([sums, jnp.zeros((group_count, width - 2 * rows), jnp.float32)], axis=1)


def pair_kernel(factor, sum_ref, other_ref, cross_ref, rest_ref, out_ref):
    out_ref[...] = (sum_ref[...] + other_ref[...] + cross_ref[...]) * factor


def add_kernel(*refs):
    *terms, _, out_ref = refs
    out_ref[...] = functools.reduce(jnp.add, [ref[...] for ref in terms])


def forward_kernel(far_ref, rest_ref, out_ref):
    half = out_ref.shape[1]
    out_ref[...] = lax.select(is_odd(), far_ref[:, half:], far_ref[:, :half])


def ready_kernel(
    tiles_ref, ready_ref, two_ref, query_ref, keys_ref, values_ref, sum_ref, rest_ref, one, other
):
    odd = is_odd()
    group_count, rows, _ = tiles_ref.shape
    group_width = two_ref.shape[1] // group_count
    half = group_count // 2
    for group in range(half):
        low, high = columns_of(group, group_width), columns_of(group + half, group_width)
        first = ready_ref[:, low] + DOT(tiles_ref[group, :, 2 * rows :], two_ref[:, low])
        second = ready_ref[:, high] + DOT(tiles_ref[group + half, :, 2 * rows :], two_ref[:, high])
        rest_ref[:, low] = lax.select(odd, first, second)
        known = lax.select(odd, second, first)
        one[:, low] = scaled(known, lax.select(odd, values_ref[:, high], query_ref[:, low]))
        other[:, low] = scaled(known, keys_ref[:, high])


def known_kernel(tiles_ref, late_ref, swap_ref, far_ref, query_ref, keys_ref, values_ref, one, other):
    odd = is_odd()
    group_count, rows, _ = tiles_ref.shape
    group_width = far_ref.shape[1] // group_count
    for group in range(group_count):
        columns = columns_of(group, group_width)
        arrived = jnp.concatenate([swap_ref[:, columns], far_ref[:, columns]], axis=0)
        late = late_ref[:, columns] + DOT(tiles_ref[group, :, rows:], arrived)
        one[:, columns] = scaled(late, lax.select(odd, query_ref[:, columns], values_ref[:, columns]))
        other[:, columns] = scaled(late, keys_ref[:, columns])


def last_kernel(
    tiles_ref, rest_ref, forwarded_ref, query_ref, keys_ref, values_ref,
    ready_one, ready_other, known_one, known_other,
    gated_out, key_out, value_out, mark_ref, one, other, sems,
):
    odd = is_odd()
    mark_ref[...] = jnp.zeros_like(mark_ref)
    group_count, rows, _ = tiles_ref.shape
    half = group_count // 2
    group_width = forwarded_ref.shape[1] // half
    step = max(1, half // PARTS)
    low_half, high_half = pl.ds(0, half * group_width), pl.ds(half * group_width, half * group_width)
    copies = launch(
        odd,
        [
            (0, known_one, key_out),
            (0, known_other, value_out),
            (0, ready_one, gated_out.at[:, low_half]),
            (1, known_one, gated_out),
            (1, ready_one, key_out.at[:, high_half]),
            (1, ready_other, value_out.at[:, high_half]),
        ],
        sems,
        0,
    )
    for group in range(half):
        low, high = columns_of(group, group_width), columns_of(group + half, group_width)
        tile = lax.select(
            odd, tiles_ref[group, :, rows : 2 * rows], tiles_ref[group + half, :, rows : 2 * rows]
        )
        ready = rest_ref[:, low] + DOT(tile, forwarded_ref[:, low])
        one[:, low] = scaled(ready, lax.select(odd, values_ref[:, low], query_ref[:, high]))
        other[:, low] = scaled(ready, keys_ref[:, low])
        if (group + 1) % step == 0:
            start, size = (group + 1 - step) * group_width, step * group_width
            part, place = pl.ds(start, size), pl.ds(start + half * group_width, size)
            moves = [
                (0, one.at[:, part], gated_out.at[:, place]),
                (1, one.at[:, part], key_out.at[:, part]),
                (1, other.at[:, part], value_out.at[:, part]),
            ]
            copies += launch(odd, moves, sems, len(copies))
    finish(odd, copies)


def shards(query, keys, values, cotangent, filter_taps):
    rows, local_width = query.shape
    group_count, taps = filter_taps.shape
    group_width = local_width // group_count
    half_width = local_width // 2
    factor = 1.0 / math.sqrt(rows * lax.axis_size("ctx") * group_width)

    def call(kernel, name, flops=10**6, **options):
        return pl.pallas_call(
            kernel,
            compiler_params=pltpu.CompilerParams(vmem_limit_bytes=VMEM_LIMIT),
            cost_estimate=pl.CostEstimate(flops=flops, bytes_accessed=10**5, transcendentals=0),
            name=name,
            **options,
        )

    bf16, f32 = jnp.bfloat16, jnp.float32
    block, half_block = pltpu.VMEM((rows, local_width), bf16), pltpu.VMEM((rows, half_width), bf16)
    wide, half_wide = pltpu.VMEM((rows, local_width), f32), pltpu.VMEM((rows, half_width), f32)
    tiles, sums = pltpu.VMEM((group_count, rows, taps), bf16), pltpu.VMEM((group_count, taps), f32)
    outs = [jax.ShapeDtypeStruct((rows, local_width), bf16)] * 3

    sent = call(
        diagonal_kernel,
        "diagonal",
        in_specs=[ANYWHERE] * 4,
        out_specs=WHOLE,
        out_shape=half_block,
        scratch_shapes=[half_block] * 2 + [pltpu.SemaphoreType.DMA((4,))],
    )(*in_hbm(query, keys, values, cotangent))
    diagonal = moved(sent, "ctx", (-1, 1))
    near, across = call(
        products_kernel,
        "products",
        in_specs=[WHOLE] * 4 + [ANYWHERE],
        out_specs=[WHOLE] * 2,
        out_shape=[block] * 2,
    )(*in_vmem(query, keys, values, cotangent), sent)
    two = moved(across, "ctx", (2, -2))
    far = moved(near, "ctx", (-2, 2))
    swap = moved(across, "ctx", (1, -1))

    ready_tiles, late_tiles = call(
        functools.partial(tiles_kernel, rows),
        "tiles",
        in_specs=[WHOLE],
        out_specs=[WHOLE] * 2,
        out_shape=[tiles] * 2,
    )(*in_vmem(filter_taps))
    partial, late, ready = call(
        functools.partial(own_kernel, rows),
        "own",
        flops=4 * 10**9,
        in_specs=[WHOLE] * 5,
        out_specs=[WHOLE] * 3,
        out_shape=[sums, wide, wide],
    )(*in_vmem(ready_tiles, late_tiles, near, across, diagonal))

    partial = call(
        functools.partial(two_kernel, rows),
        "two",
        in_specs=[WHOLE] * 3,
        out_specs=WHOLE,
        out_shape=sums,
    )(*in_vmem(partial, near, two))
    other = moved(partial, "ctx", (1, -1))

    rest, ready_one, ready_other = call(
        ready_kernel,
        "ready",
        in_specs=[WHOLE] * 6 + [ANYWHERE],
        out_specs=[WHOLE] * 3,
        out_shape=[half_wide, half_block, half_block],
    )(*in_vmem(ready_tiles, ready, two, query, keys, values), partial)

    forwarded = call(
        forward_kernel,
        "forward",
        in_specs=[WHOLE, ANYWHERE],
        out_specs=WHOLE,
        out_shape=half_block,
    )(*in_vmem(far), rest)
    forwarded = moved(forwarded, "ctx", (1, -1))

    cross = call(
        functools.partial(cross_kernel, rows),
        "cross",
        in_specs=[WHOLE] * 2,
        out_specs=WHOLE,
        out_shape=sums,
    )(*in_vmem(across, swap))
    pair_sum = call(
        functools.partial(pair_kernel, factor),
        "pair",
        in_specs=[WHOLE] * 3 + [ANYWHERE],
        out_specs=WHOLE,
        out_shape=sums,
    )(*in_vmem(partial, other, cross), rest)

    known_one, known_other = call(
        known_kernel,
        "known",
        flops=4 * 10**9,
        in_specs=[WHOLE] * 7,
        out_specs=[WHOLE] * 2,
        out_shape=[block] * 2,
    )(*in_vmem(late_tiles, late, swap, far, query, keys, values))

    def add(*terms, out_shape=sums, after=known_one):
        return call(
            add_kernel,
            "add",
            in_specs=[WHOLE] * len(terms) + [ANYWHERE],
            out_specs=WHOLE,
            out_shape=out_shape,
        )(*in_vmem(*terms), after)

    terms = sum_terms(pair_sum, "ctx", add)
    gated, key_grad, value_grad, mark = call(
        last_kernel,
        "last",
        in_specs=[WHOLE] * 10,
        out_specs=[ANYWHERE] * 3 + [WHOLE],
        out_shape=outs + [pltpu.VMEM((SUBLANES, group_width), f32)],
        scratch_shapes=[half_block] * 2 + [pltpu.SemaphoreType.DMA((6 + 3 * PARTS,))],
    )(
        *in_vmem(ready_tiles, rest, forwarded, query, keys, values),
        *in_vmem(ready_one, ready_other, known_one, known_other),
    )
    whole_sums = jax.ShapeDtypeStruct((group_count, taps), f32)
    return (gated, key_grad, value_grad, add(*terms, out_shape=whole_sums, after=mark))


def solution(mesh):
    in_specs = (P("ctx", "grp"), P("ctx", "grp"), P("ctx", "grp"), P("ctx", "grp"), P("grp", None))
    out_specs = (P("ctx", "grp"), P("ctx", "grp"), P("ctx", "grp"), P("grp", None))
    return jax.shard_map(shards, mesh=mesh, in_specs=in_specs, out_specs=out_specs, check_vma=False)
```

```python
import functools
import math

import jax
import jax.numpy as jnp
from jax import lax
from jax.experimental import pallas as pl
from jax.experimental.pallas import tpu as pltpu
from jax.sharding import PartitionSpec as P

SUBLANES = 8
PARTS = 2
VMEM_LIMIT = 16 * 1024 * 1024
WHOLE = pl.BlockSpec(memory_space=pltpu.VMEM)
ANYWHERE = pl.BlockSpec(memory_space=pl.ANY)
DOT_ROWS = functools.partial(
    lax.dot_general,
    dimension_numbers=(((1,), (1,)), ((), ())),
    preferred_element_type=jnp.float32,
)
DOT = functools.partial(jnp.dot, preferred_element_type=jnp.float32)


def in_vmem(*arrays):
    return [pltpu.with_memory_space_constraint(array, pltpu.VMEM) for array in arrays]


def in_hbm(*arrays):
    return [pltpu.with_memory_space_constraint(array, pltpu.HBM) for array in arrays]


def moved(block, axis, distances):
    size = lax.axis_size(axis)
    route = [(i, i + distances[i % 2]) for i in range(size)]
    return lax.ppermute(block, axis, [pair for pair in route if 0 <= pair[1] < size])


def sum_terms(pair_sum, axis, add):
    size = lax.axis_size(axis)
    if size & (size - 1):
        even = lax.axis_index(axis) % 2 == 0
        return [lax.psum(jnp.where(even, pair_sum, 0.0), axis)]
    terms = [pair_sum]
    stride = 2
    while stride < size:
        own = terms[0] if len(terms) == 1 else add(*terms)
        members = 4 if 4 * stride <= size else 2
        terms = [own]
        for turn in range(1, members):
            places = [(i, i // stride % members) for i in range(size)]
            route = [(i, i + ((place + turn) % members - place) * stride) for i, place in places]
            terms.append(lax.ppermute(own, axis, route))
        stride *= members
    return terms


def is_odd():
    return lax.rem(lax.axis_index("ctx"), 2) == 1


def product(left, right):
    return (left.astype(jnp.float32) * right.astype(jnp.float32)).astype(jnp.bfloat16)


def scaled(value, factor):
    return (value * factor.astype(jnp.float32)).astype(jnp.bfloat16)


def columns_of(group, width):
    return slice(group * width, (group + 1) * width)


def launch(odd, moves, sems, used):
    copies = [(*move, sems.at[used + place]) for place, move in enumerate(moves)]
    for parity, source, target, sem in copies:
        @pl.when(odd if parity else jnp.logical_not(odd))
        def _():
            pltpu.make_async_copy(source, target, sem).start()
    return copies


def finish(odd, copies):
    for parity, source, target, sem in copies:
        @pl.when(odd if parity else jnp.logical_not(odd))
        def _():
            pltpu.make_async_copy(source, target, sem).wait()


def lines_summed(total):
    line = lax.broadcasted_iota(jnp.int32, total.shape, 0)
    bit = 1
    while bit < SUBLANES:
        total = jnp.where((line & bit) == bit, pltpu.roll(total, total.shape[1] - bit, 1), total)
        bit *= 2
    return jnp.sum(total, axis=0, keepdims=True)


def skewed_sum(outer, rows):
    width = outer.shape[1]
    total = outer[:SUBLANES]
    for start in range(SUBLANES, rows, SUBLANES):
        total = total + pltpu.roll(outer[start : start + SUBLANES], width - start, 1)
    return lines_summed(total)


def skewed_pair(outer, rows):
    width = outer.shape[1]
    lane = lax.broadcasted_iota(jnp.int32, (SUBLANES, width), 1)
    high = outer[:SUBLANES]
    low = jnp.zeros_like(high)
    for start in range(SUBLANES, rows, SUBLANES):
        turned = pltpu.roll(outer[start : start + SUBLANES], width - start, 1)
        above = lane < width - start
        high = high + jnp.where(above, turned, 0.0)
        low = low + jnp.where(above, 0.0, turned)
    return lines_summed(jnp.concatenate([low, high], axis=1))


def diagonal_kernel(query_hbm, keys_hbm, values_hbm, cotangent_hbm, out_ref, left, right, sems):
    odd = is_odd()
    half = out_ref.shape[1]
    low, high = pl.ds(0, half), pl.ds(half, half)
    copies = launch(
        odd,
        [
            (1, keys_hbm.at[:, low], left),
            (1, values_hbm.at[:, low], right),
            (0, cotangent_hbm.at[:, high], left),
            (0, query_hbm.at[:, high], right),
        ],
        sems,
        0,
    )
    finish(odd, copies)
    out_ref[...] = product(left[...], right[...])


def products_kernel(query_ref, keys_ref, values_ref, cotangent_ref, sent_ref, near_ref, across_ref):
    odd = is_odd()
    prod = product(keys_ref[...], values_ref[...])
    grad = product(cotangent_ref[...], query_ref[...])
    near_ref[...] = lax.select(odd, prod, grad)
    across_ref[...] = lax.select(odd, grad, prod)


def tiles_kernel(rows, taps_ref, ready_tiles, late_tiles):
    odd = is_odd()
    group_count, width = taps_ref.shape
    for group in range(group_count):
        row = taps_ref[group : group + 1, :].astype(jnp.float32)
        spread = jnp.concatenate(
            [jnp.zeros((SUBLANES, rows), jnp.float32), jnp.broadcast_to(row, (SUBLANES, width))],
            axis=1,
        )
        spread = pltpu.roll(spread, 0, 1, stride=1, stride_axis=0)
        bands = [
            pltpu.roll(spread, start, 1)[:, rows:] if start else spread[:, rows:]
            for start in range(0, rows, SUBLANES)
        ]
        band = jnp.concatenate(bands, axis=0)
        turned = [band[:, start : start + rows].T for start in range(0, width, rows)]
        turned = jnp.concatenate(turned, axis=1)
        ready_tiles[group] = lax.select(odd, band, turned).astype(jnp.bfloat16)
        late_tiles[group] = lax.select(odd, turned, band).astype(jnp.bfloat16)


def own_kernel(
    rows, ready_tiles, late_tiles, near_ref, across_ref, diagonal_ref, sum_ref, late_ref, ready_ref
):
    odd = is_odd()
    group_count, width = sum_ref.shape
    group_width = near_ref.shape[1] // group_count
    half = group_count // 2
    blank = jnp.zeros((rows, rows), jnp.float32)
    for group in range(group_count):
        columns = columns_of(group, group_width)
        late_ref[:, columns] = DOT(late_tiles[group, :, :rows], near_ref[:, columns])
        ready_ref[:, columns] = DOT(ready_tiles[group, :, :rows], across_ref[:, columns])
    middles = []
    for group in range(half):
        low, high = columns_of(group, group_width), columns_of(group + half, group_width)
        arrived = diagonal_ref[:, low]
        own = lax.select(odd, near_ref[:, high], near_ref[:, low])
        middles.append(DOT_ROWS(lax.select(odd, own, arrived), lax.select(odd, arrived, own)))
        tile = lax.select(
            odd, ready_tiles[group + half, :, rows : 2 * rows], ready_tiles[group, :, rows : 2 * rows]
        )
        more = DOT(tile, arrived)
        ready_ref[:, low] += lax.select(odd, blank, more)
        ready_ref[:, high] += lax.select(odd, more, blank)
    sums = []
    for group in range(group_count):
        columns = columns_of(group, group_width)
        near, across = near_ref[:, columns], across_ref[:, columns]
        outer = DOT_ROWS(lax.select(odd, near, across), lax.select(odd, across, near))
        if group < half:
            middle = lax.select(odd, blank, middles[group])
        else:
            middle = lax.select(odd, middles[group - half], blank)
        sums.append(skewed_sum(jnp.concatenate([outer, middle, blank], axis=1), rows)[:, : 2 * rows])
    sums = jnp.concatenate(sums, axis=0)
    sum_ref[...] = jnp.concatenate([sums, jnp.zeros((group_count, width - 2 * rows), jnp.float32)], axis=1)


def two_kernel(rows, sum_ref, near_ref, two_ref, out_ref):
    odd = is_odd()
    group_count, width = out_ref.shape
    group_width = near_ref.shape[1] // group_count
    sums = []
    for group in range(group_count):
        columns = columns_of(group, group_width)
        near, two = near_ref[:, columns], two_ref[:, columns]
        outer = DOT_ROWS(lax.select(odd, near, two), lax.select(odd, two, near))
        sums.append(skewed_pair(outer, rows))
    sums = jnp.concatenate(sums, axis=0)
    out_ref[...] = sum_ref[...] + jnp.concatenate(
        [jnp.zeros((group_count, width - 2 * rows), jnp.float32), sums], axis=1
    )


def cross_kernel(rows, across_ref, swap_ref, out_ref):
    odd = is_odd()
    group_count, width = out_ref.shape
    group_width = across_ref.shape[1] // group_count
    sums = []
    for group in range(group_count):
        columns = columns_of(group, group_width)
        across, swap = across_ref[:, columns], swap_ref[:, columns]
        outer = DOT_ROWS(lax.select(odd, swap, across), lax.select(odd, across, swap))
        sums.append(skewed_pair(outer, rows))
    sums = jnp.concatenate(sums, axis=0)
    out_ref[...] = jnp.concatenate([sums, jnp.zeros((group_count, width - 2 * rows), jnp.float32)], axis=1)


def pair_kernel(factor, sum_ref, other_ref, cross_ref, rest_ref, out_ref):
    out_ref[...] = (sum_ref[...] + other_ref[...] + cross_ref[...]) * factor


def add_kernel(*refs):
    *terms, _, out_ref = refs
    out_ref[...] = functools.reduce(jnp.add, [ref[...] for ref in terms])


def forward_kernel(far_ref, rest_ref, out_ref):
    half = out_ref.shape[1]
    out_ref[...] = lax.select(is_odd(), far_ref[:, half:], far_ref[:, :half])


def ready_kernel(
    tiles_ref, ready_ref, two_ref, query_ref, keys_ref, values_ref, sum_ref, rest_ref, one, other
):
    odd = is_odd()
    group_count, rows, _ = tiles_ref.shape
    group_width = two_ref.shape[1] // group_count
    half = group_count // 2
    for group in range(half):
        low, high = columns_of(group, group_width), columns_of(group + half, group_width)
        first = ready_ref[:, low] + DOT(tiles_ref[group, :, 2 * rows :], two_ref[:, low])
        second = ready_ref[:, high] + DOT(tiles_ref[group + half, :, 2 * rows :], two_ref[:, high])
        rest_ref[:, low] = lax.select(odd, first, second)
        known = lax.select(odd, second, first)
        one[:, low] = scaled(known, lax.select(odd, values_ref[:, high], query_ref[:, low]))
        other[:, low] = scaled(known, keys_ref[:, high])


def known_kernel(tiles_ref, late_ref, swap_ref, far_ref, query_ref, keys_ref, values_ref, one, other):
    odd = is_odd()
    group_count, rows, _ = tiles_ref.shape
    group_width = far_ref.shape[1] // group_count
    for group in range(group_count):
        columns = columns_of(group, group_width)
        arrived = jnp.concatenate([swap_ref[:, columns], far_ref[:, columns]], axis=0)
        late = late_ref[:, columns] + DOT(tiles_ref[group, :, rows:], arrived)
        one[:, columns] = scaled(late, lax.select(odd, query_ref[:, columns], values_ref[:, columns]))
        other[:, columns] = scaled(late, keys_ref[:, columns])


def last_kernel(
    tiles_ref, rest_ref, forwarded_ref, query_ref, keys_ref, values_ref,
    ready_one, ready_other, known_one, known_other,
    gated_out, key_out, value_out, mark_ref, one, other, sems,
):
    odd = is_odd()
    mark_ref[...] = jnp.zeros_like(mark_ref)
    group_count, rows, _ = tiles_ref.shape
    half = group_count // 2
    group_width = forwarded_ref.shape[1] // half
    step = max(1, half // PARTS)
    low_half, high_half = pl.ds(0, half * group_width), pl.ds(half * group_width, half * group_width)
    copies = launch(
        odd,
        [
            (0, known_one, key_out),
            (0, known_other, value_out),
            (0, ready_one, gated_out.at[:, low_half]),
            (1, known_one, gated_out),
            (1, ready_one, key_out.at[:, high_half]),
            (1, ready_other, value_out.at[:, high_half]),
        ],
        sems,
        0,
    )
    for group in range(half):
        low, high = columns_of(group, group_width), columns_of(group + half, group_width)
        tile = lax.select(
            odd, tiles_ref[group, :, rows : 2 * rows], tiles_ref[group + half, :, rows : 2 * rows]
        )
        ready = rest_ref[:, low] + DOT(tile, forwarded_ref[:, low])
        one[:, low] = scaled(ready, lax.select(odd, values_ref[:, low], query_ref[:, high]))
        other[:, low] = scaled(ready, keys_ref[:, low])
        if (group + 1) % step == 0:
            start, size = (group + 1 - step) * group_width, step * group_width
            part, place = pl.ds(start, size), pl.ds(start + half * group_width, size)
            moves = [
                (0, one.at[:, part], gated_out.at[:, place]),
                (1, one.at[:, part], key_out.at[:, part]),
                (1, other.at[:, part], value_out.at[:, part]),
            ]
            copies += launch(odd, moves, sems, len(copies))
    finish(odd, copies)


def shards(query, keys, values, cotangent, filter_taps):
    rows, local_width = query.shape
    group_count, taps = filter_taps.shape
    group_width = local_width // group_count
    half_width = local_width // 2
    factor = 1.0 / math.sqrt(rows * lax.axis_size("ctx") * group_width)

    def call(kernel, name, flops=10**6, **options):
        return pl.pallas_call(
            kernel,
            compiler_params=pltpu.CompilerParams(vmem_limit_bytes=VMEM_LIMIT),
            cost_estimate=pl.CostEstimate(flops=flops, bytes_accessed=10**5, transcendentals=0),
            name=name,
            **options,
        )

    bf16, f32 = jnp.bfloat16, jnp.float32
    block, half_block = pltpu.VMEM((rows, local_width), bf16), pltpu.VMEM((rows, half_width), bf16)
    wide, half_wide = pltpu.VMEM((rows, local_width), f32), pltpu.VMEM((rows, half_width), f32)
    tiles, sums = pltpu.VMEM((group_count, rows, taps), bf16), pltpu.VMEM((group_count, taps), f32)
    outs = [jax.ShapeDtypeStruct((rows, local_width), bf16)] * 3

    sent = call(
        diagonal_kernel,
        "diagonal",
        in_specs=[ANYWHERE] * 4,
        out_specs=WHOLE,
        out_shape=half_block,
        scratch_shapes=[half_block] * 2 + [pltpu.SemaphoreType.DMA((4,))],
    )(*in_hbm(query, keys, values, cotangent))
    diagonal = moved(sent, "ctx", (-1, 1))
    near, across = call(
        products_kernel,
        "products",
        in_specs=[WHOLE] * 4 + [ANYWHERE],
        out_specs=[WHOLE] * 2,
        out_shape=[block] * 2,
    )(*in_vmem(query, keys, values, cotangent), sent)
    two = moved(across, "ctx", (2, -2))
    far = moved(near, "ctx", (-2, 2))
    swap = moved(across, "ctx", (1, -1))

    ready_tiles, late_tiles = call(
        functools.partial(tiles_kernel, rows),
        "tiles",
        in_specs=[WHOLE],
        out_specs=[WHOLE] * 2,
        out_shape=[tiles] * 2,
    )(*in_vmem(filter_taps))
    partial, late, ready = call(
        functools.partial(own_kernel, rows),
        "own",
        flops=4 * 10**9,
        in_specs=[WHOLE] * 5,
        out_specs=[WHOLE] * 3,
        out_shape=[sums, wide, wide],
    )(*in_vmem(ready_tiles, late_tiles, near, across, diagonal))

    partial = call(
        functools.partial(two_kernel, rows),
        "two",
        in_specs=[WHOLE] * 3,
        out_specs=WHOLE,
        out_shape=sums,
    )(*in_vmem(partial, near, two))
    other = moved(partial, "ctx", (1, -1))

    rest, ready_one, ready_other = call(
        ready_kernel,
        "ready",
        in_specs=[WHOLE] * 6 + [ANYWHERE],
        out_specs=[WHOLE] * 3,
        out_shape=[half_wide, half_block, half_block],
    )(*in_vmem(ready_tiles, ready, two, query, keys, values), partial)

    forwarded = call(
        forward_kernel,
        "forward",
        in_specs=[WHOLE, ANYWHERE],
        out_specs=WHOLE,
        out_shape=half_block,
    )(*in_vmem(far), rest)
    forwarded = moved(forwarded, "ctx", (1, -1))

    cross = call(
        functools.partial(cross_kernel, rows),
        "cross",
        in_specs=[WHOLE] * 2,
        out_specs=WHOLE,
        out_shape=sums,
    )(*in_vmem(across, swap))
    pair_sum = call(
        functools.partial(pair_kernel, factor),
        "pair",
        in_specs=[WHOLE] * 3 + [ANYWHERE],
        out_specs=WHOLE,
        out_shape=sums,
    )(*in_vmem(partial, other, cross), rest)

    known_one, known_other = call(
        known_kernel,
        "known",
        flops=4 * 10**9,
        in_specs=[WHOLE] * 7,
        out_specs=[WHOLE] * 2,
        out_shape=[block] * 2,
    )(*in_vmem(late_tiles, late, swap, far, query, keys, values))

    def add(*terms, out_shape=sums, after=known_one):
        return call(
            add_kernel,
            "add",
            in_specs=[WHOLE] * len(terms) + [ANYWHERE],
            out_specs=WHOLE,
            out_shape=out_shape,
        )(*in_vmem(*terms), after)

    terms = sum_terms(pair_sum, "ctx", add)
    gated, key_grad, value_grad, mark = call(
        last_kernel,
        "last",
        in_specs=[WHOLE] * 10,
        out_specs=[ANYWHERE] * 3 + [WHOLE],
        out_shape=outs + [pltpu.VMEM((SUBLANES, group_width), f32)],
        scratch_shapes=[half_block] * 2 + [pltpu.SemaphoreType.DMA((6 + 3 * PARTS,))],
    )(
        *in_vmem(ready_tiles, rest, forwarded, query, keys, values),
        *in_vmem(ready_one, ready_other, known_one, known_other),
    )
    whole_sums = jax.ShapeDtypeStruct((group_count, taps), f32)
    return (gated, key_grad, value_grad, add(*terms, out_shape=whole_sums, after=mark))


def solution(mesh):
    in_specs = (P("ctx", "grp"), P("ctx", "grp"), P("ctx", "grp"), P("ctx", "grp"), P("grp", None))
    out_specs = (P("ctx", "grp"), P("ctx", "grp"), P("ctx", "grp"), P("grp", None))
    return jax.shard_map(shards, mesh=mesh, in_specs=in_specs, out_specs=out_specs, check_vma=False)
```

```python
import functools
import math

import jax
import jax.numpy as jnp
from jax import lax
from jax.experimental import pallas as pl
from jax.experimental.pallas import tpu as pltpu
from jax.sharding import PartitionSpec as P

SUBLANES = 8
PARTS = 2
VMEM_LIMIT = 16 * 1024 * 1024
WHOLE = pl.BlockSpec(memory_space=pltpu.VMEM)
ANYWHERE = pl.BlockSpec(memory_space=pl.ANY)
DOT_ROWS = functools.partial(
    lax.dot_general,
    dimension_numbers=(((1,), (1,)), ((), ())),
    preferred_element_type=jnp.float32,
)
DOT = functools.partial(jnp.dot, preferred_element_type=jnp.float32)


def in_vmem(*arrays):
    return [pltpu.with_memory_space_constraint(array, pltpu.VMEM) for array in arrays]


def in_hbm(*arrays):
    return [pltpu.with_memory_space_constraint(array, pltpu.HBM) for array in arrays]


def moved(block, axis, distances):
    size = lax.axis_size(axis)
    route = [(i, i + distances[i % 2]) for i in range(size)]
    return lax.ppermute(block, axis, [pair for pair in route if 0 <= pair[1] < size])


def sum_terms(pair_sum, axis, add):
    size = lax.axis_size(axis)
    if size & (size - 1):
        even = lax.axis_index(axis) % 2 == 0
        return [lax.psum(jnp.where(even, pair_sum, 0.0), axis)]
    terms = [pair_sum]
    stride = 2
    while stride < size:
        own = terms[0] if len(terms) == 1 else add(*terms)
        members = 4 if 4 * stride <= size else 2
        terms = [own]
        for turn in range(1, members):
            places = [(i, i // stride % members) for i in range(size)]
            route = [(i, i + ((place + turn) % members - place) * stride) for i, place in places]
            terms.append(lax.ppermute(own, axis, route))
        stride *= members
    return terms


def is_odd():
    return lax.rem(lax.axis_index("ctx"), 2) == 1


def product(left, right):
    return (left.astype(jnp.float32) * right.astype(jnp.float32)).astype(jnp.bfloat16)


def scaled(value, factor):
    return (value * factor.astype(jnp.float32)).astype(jnp.bfloat16)


def columns_of(group, width):
    return slice(group * width, (group + 1) * width)


def launch(odd, moves, sems, used):
    copies = [(*move, sems.at[used + place]) for place, move in enumerate(moves)]
    for parity, source, target, sem in copies:
        @pl.when(odd if parity else jnp.logical_not(odd))
        def _():
            pltpu.make_async_copy(source, target, sem).start()
    return copies


def finish(odd, copies):
    for parity, source, target, sem in copies:
        @pl.when(odd if parity else jnp.logical_not(odd))
        def _():
            pltpu.make_async_copy(source, target, sem).wait()


def lines_summed(total):
    line = lax.broadcasted_iota(jnp.int32, total.shape, 0)
    bit = 1
    while bit < SUBLANES:
        total = jnp.where((line & bit) == bit, pltpu.roll(total, total.shape[1] - bit, 1), total)
        bit *= 2
    return jnp.sum(total, axis=0, keepdims=True)


def skewed_sum(outer, rows):
    width = outer.shape[1]
    total = outer[:SUBLANES]
    for start in range(SUBLANES, rows, SUBLANES):
        total = total + pltpu.roll(outer[start : start + SUBLANES], width - start, 1)
    return lines_summed(total)


def skewed_pair(outer, rows):
    width = outer.shape[1]
    lane = lax.broadcasted_iota(jnp.int32, (SUBLANES, width), 1)
    high = outer[:SUBLANES]
    low = jnp.zeros_like(high)
    for start in range(SUBLANES, rows, SUBLANES):
        turned = pltpu.roll(outer[start : start + SUBLANES], width - start, 1)
        above = lane < width - start
        high = high + jnp.where(above, turned, 0.0)
        low = low + jnp.where(above, 0.0, turned)
    return lines_summed(jnp.concatenate([low, high], axis=1))


def load_kernel(
    query_hbm, keys_hbm, values_hbm, cotangent_hbm,
    query_ref, keys_ref, values_ref, near_ref, across_ref, sent_ref, cotangent_ref, sems,
):
    odd = is_odd()
    half = sent_ref.shape[1]
    pairs = (
        ((keys_hbm, keys_ref), (values_hbm, values_ref)),
        ((cotangent_hbm, cotangent_ref), (query_hbm, query_ref)),
    )
    parts = [pl.ds(0, half), pl.ds(half, half)]
    moves = []
    for parity in (0, 1):
        first = 1 - parity
        for part in (parts[first], parts[parity]):
            for pair in (pairs[first], pairs[parity]):
                moves.extend((parity, source.at[:, part], target.at[:, part]) for source, target in pair)
    copies = launch(odd, moves, sems, 0)
    sides = len(moves) // 2
    for parity in (0, 1):
        mine = copies[parity * sides : (parity + 1) * sides]

        @pl.when(odd if parity else jnp.logical_not(odd))
        def _():
            order = (1 - parity, parity)
            for place, part in enumerate(order):
                columns = slice(part * half, (part + 1) * half)
                for _, source, target, sem in mine[place * sides // 2 : (place + 1) * sides // 2]:
                    pltpu.make_async_copy(source, target, sem).wait()
                prod = product(keys_ref[:, columns], values_ref[:, columns])
                grad = product(cotangent_ref[:, columns], query_ref[:, columns])
                near = prod if parity else grad
                near_ref[:, columns] = near
                across_ref[:, columns] = grad if parity else prod
                if place == 0:
                    sent_ref[...] = near


def tiles_kernel(rows, taps_ref, ready_tiles, late_tiles):
    odd = is_odd()
    group_count, width = taps_ref.shape
    for group in range(group_count):
        row = taps_ref[group : group + 1, :].astype(jnp.float32)
        spread = jnp.concatenate(
            [jnp.zeros((SUBLANES, rows), jnp.float32), jnp.broadcast_to(row, (SUBLANES, width))],
            axis=1,
        )
        spread = pltpu.roll(spread, 0, 1, stride=1, stride_axis=0)
        bands = [
            pltpu.roll(spread, start, 1)[:, rows:] if start else spread[:, rows:]
            for start in range(0, rows, SUBLANES)
        ]
        band = jnp.concatenate(bands, axis=0)
        turned = [band[:, start : start + rows].T for start in range(0, width, rows)]
        turned = jnp.concatenate(turned, axis=1)
        ready_tiles[group] = lax.select(odd, band, turned).astype(jnp.bfloat16)
        late_tiles[group] = lax.select(odd, turned, band).astype(jnp.bfloat16)


def own_kernel(
    rows, ready_tiles, late_tiles, near_ref, across_ref, diagonal_ref, sum_ref, late_ref, ready_ref
):
    odd = is_odd()
    group_count, width = sum_ref.shape
    group_width = near_ref.shape[1] // group_count
    half = group_count // 2
    blank = jnp.zeros((rows, rows), jnp.float32)
    for group in range(group_count):
        columns = columns_of(group, group_width)
        late_ref[:, columns] = DOT(late_tiles[group, :, :rows], near_ref[:, columns])
        ready_ref[:, columns] = DOT(ready_tiles[group, :, :rows], across_ref[:, columns])
    middles = []
    for group in range(half):
        low, high = columns_of(group, group_width), columns_of(group + half, group_width)
        arrived = diagonal_ref[:, low]
        own = lax.select(odd, near_ref[:, high], near_ref[:, low])
        middles.append(DOT_ROWS(lax.select(odd, own, arrived), lax.select(odd, arrived, own)))
        tile = lax.select(
            odd, ready_tiles[group + half, :, rows : 2 * rows], ready_tiles[group, :, rows : 2 * rows]
        )
        more = DOT(tile, arrived)
        ready_ref[:, low] += lax.select(odd, blank, more)
        ready_ref[:, high] += lax.select(odd, more, blank)
    sums = []
    for group in range(group_count):
        columns = columns_of(group, group_width)
        near, across = near_ref[:, columns], across_ref[:, columns]
        outer = DOT_ROWS(lax.select(odd, near, across), lax.select(odd, across, near))
        if group < half:
            middle = lax.select(odd, blank, middles[group])
        else:
            middle = lax.select(odd, middles[group - half], blank)
        sums.append(skewed_sum(jnp.concatenate([outer, middle, blank], axis=1), rows)[:, : 2 * rows])
    sums = jnp.concatenate(sums, axis=0)
    sum_ref[...] = jnp.concatenate([sums, jnp.zeros((group_count, width - 2 * rows), jnp.float32)], axis=1)


def two_kernel(rows, sum_ref, near_ref, two_ref, out_ref):
    odd = is_odd()
    group_count, width = out_ref.shape
    group_width = near_ref.shape[1] // group_count
    sums = []
    for group in range(group_count):
        columns = columns_of(group, group_width)
        near, two = near_ref[:, columns], two_ref[:, columns]
        outer = DOT_ROWS(lax.select(odd, near, two), lax.select(odd, two, near))
        sums.append(skewed_pair(outer, rows))
    sums = jnp.concatenate(sums, axis=0)
    out_ref[...] = sum_ref[...] + jnp.concatenate(
        [jnp.zeros((group_count, width - 2 * rows), jnp.float32), sums], axis=1
    )


def cross_kernel(rows, across_ref, swap_ref, out_ref):
    odd = is_odd()
    group_count, width = out_ref.shape
    group_width = across_ref.shape[1] // group_count
    sums = []
    for group in range(group_count):
        columns = columns_of(group, group_width)
        across, swap = across_ref[:, columns], swap_ref[:, columns]
        outer = DOT_ROWS(lax.select(odd, swap, across), lax.select(odd, across, swap))
        sums.append(skewed_pair(outer, rows))
    sums = jnp.concatenate(sums, axis=0)
    out_ref[...] = jnp.concatenate([sums, jnp.zeros((group_count, width - 2 * rows), jnp.float32)], axis=1)


def pair_kernel(factor, sum_ref, other_ref, cross_ref, rest_ref, out_ref):
    out_ref[...] = (sum_ref[...] + other_ref[...] + cross_ref[...]) * factor


def add_kernel(*refs):
    *terms, _, out_ref = refs
    out_ref[...] = functools.reduce(jnp.add, [ref[...] for ref in terms])


def forward_kernel(far_ref, rest_ref, out_ref):
    half = out_ref.shape[1]
    out_ref[...] = lax.select(is_odd(), far_ref[:, half:], far_ref[:, :half])


def ready_kernel(
    tiles_ref, ready_ref, two_ref, query_ref, keys_ref, values_ref, sum_ref, rest_ref, one, other
):
    odd = is_odd()
    group_count, rows, _ = tiles_ref.shape
    group_width = two_ref.shape[1] // group_count
    half = group_count // 2
    for group in range(half):
        low, high = columns_of(group, group_width), columns_of(group + half, group_width)
        first = ready_ref[:, low] + DOT(tiles_ref[group, :, 2 * rows :], two_ref[:, low])
        second = ready_ref[:, high] + DOT(tiles_ref[group + half, :, 2 * rows :], two_ref[:, high])
        rest_ref[:, low] = lax.select(odd, first, second)
        known = lax.select(odd, second, first)
        one[:, low] = scaled(known, lax.select(odd, values_ref[:, high], query_ref[:, low]))
        other[:, low] = scaled(known, keys_ref[:, high])


def known_kernel(tiles_ref, late_ref, swap_ref, far_ref, query_ref, keys_ref, values_ref, one, other):
    odd = is_odd()
    group_count, rows, _ = tiles_ref.shape
    group_width = far_ref.shape[1] // group_count
    for group in range(group_count):
        columns = columns_of(group, group_width)
        arrived = jnp.concatenate([swap_ref[:, columns], far_ref[:, columns]], axis=0)
        late = late_ref[:, columns] + DOT(tiles_ref[group, :, rows:], arrived)
        one[:, columns] = scaled(late, lax.select(odd, query_ref[:, columns], values_ref[:, columns]))
        other[:, columns] = scaled(late, keys_ref[:, columns])


def last_kernel(
    tiles_ref, rest_ref, forwarded_ref, query_ref, keys_ref, values_ref,
    ready_one, ready_other, known_one, known_other,
    gated_out, key_out, value_out, mark_ref, one, other, sems,
):
    odd = is_odd()
    mark_ref[...] = jnp.zeros_like(mark_ref)
    group_count, rows, _ = tiles_ref.shape
    half = group_count // 2
    group_width = forwarded_ref.shape[1] // half
    step = max(1, half // PARTS)
    low_half, high_half = pl.ds(0, half * group_width), pl.ds(half * group_width, half * group_width)
    copies = launch(
        odd,
        [
            (0, known_one, key_out),
            (0, known_other, value_out),
            (0, ready_one, gated_out.at[:, low_half]),
            (1, known_one, gated_out),
            (1, ready_one, key_out.at[:, high_half]),
            (1, ready_other, value_out.at[:, high_half]),
        ],
        sems,
        0,
    )
    for group in range(half):
        low, high = columns_of(group, group_width), columns_of(group + half, group_width)
        tile = lax.select(
            odd, tiles_ref[group, :, rows : 2 * rows], tiles_ref[group + half, :, rows : 2 * rows]
        )
        ready = rest_ref[:, low] + DOT(tile, forwarded_ref[:, low])
        one[:, low] = scaled(ready, lax.select(odd, values_ref[:, low], query_ref[:, high]))
        other[:, low] = scaled(ready, keys_ref[:, low])
        if (group + 1) % step == 0:
            start, size = (group + 1 - step) * group_width, step * group_width
            part, place = pl.ds(start, size), pl.ds(start + half * group_width, size)
            moves = [
                (0, one.at[:, part], gated_out.at[:, place]),
                (1, one.at[:, part], key_out.at[:, part]),
                (1, other.at[:, part], value_out.at[:, part]),
            ]
            copies += launch(odd, moves, sems, len(copies))
    finish(odd, copies)


def shards(query, keys, values, cotangent, filter_taps):
    rows, local_width = query.shape
    group_count, taps = filter_taps.shape
    group_width = local_width // group_count
    half_width = local_width // 2
    factor = 1.0 / math.sqrt(rows * lax.axis_size("ctx") * group_width)

    def call(kernel, name, flops=10**6, **options):
        return pl.pallas_call(
            kernel,
            compiler_params=pltpu.CompilerParams(vmem_limit_bytes=VMEM_LIMIT),
            cost_estimate=pl.CostEstimate(flops=flops, bytes_accessed=10**5, transcendentals=0),
            name=name,
            **options,
        )

    bf16, f32 = jnp.bfloat16, jnp.float32
    block, half_block = pltpu.VMEM((rows, local_width), bf16), pltpu.VMEM((rows, half_width), bf16)
    wide, half_wide = pltpu.VMEM((rows, local_width), f32), pltpu.VMEM((rows, half_width), f32)
    tiles, sums = pltpu.VMEM((group_count, rows, taps), bf16), pltpu.VMEM((group_count, taps), f32)
    outs = [jax.ShapeDtypeStruct((rows, local_width), bf16)] * 3

    query, keys, values, near, across, sent = call(
        load_kernel,
        "load",
        in_specs=[ANYWHERE] * 4,
        out_specs=[WHOLE] * 6,
        out_shape=[block] * 5 + [half_block],
        scratch_shapes=[block, pltpu.SemaphoreType.DMA((16,))],
    )(*in_hbm(query, keys, values, cotangent))
    diagonal = moved(sent, "ctx", (-1, 1))
    two = moved(across, "ctx", (2, -2))
    far = moved(near, "ctx", (-2, 2))
    swap = moved(across, "ctx", (1, -1))

    ready_tiles, late_tiles = call(
        functools.partial(tiles_kernel, rows),
        "tiles",
        in_specs=[WHOLE],
        out_specs=[WHOLE] * 2,
        out_shape=[tiles] * 2,
    )(*in_vmem(filter_taps))
    partial, late, ready = call(
        functools.partial(own_kernel, rows),
        "own",
        flops=4 * 10**9,
        in_specs=[WHOLE] * 5,
        out_specs=[WHOLE] * 3,
        out_shape=[sums, wide, wide],
    )(*in_vmem(ready_tiles, late_tiles, near, across, diagonal))

    partial = call(
        functools.partial(two_kernel, rows),
        "two",
        in_specs=[WHOLE] * 3,
        out_specs=WHOLE,
        out_shape=sums,
    )(*in_vmem(partial, near, two))
    other = moved(partial, "ctx", (1, -1))

    rest, ready_one, ready_other = call(
        ready_kernel,
        "ready",
        in_specs=[WHOLE] * 6 + [ANYWHERE],
        out_specs=[WHOLE] * 3,
        out_shape=[half_wide, half_block, half_block],
    )(*in_vmem(ready_tiles, ready, two, query, keys, values), partial)

    forwarded = call(
        forward_kernel,
        "forward",
        in_specs=[WHOLE, ANYWHERE],
        out_specs=WHOLE,
        out_shape=half_block,
    )(*in_vmem(far), rest)
    forwarded = moved(forwarded, "ctx", (1, -1))

    cross = call(
        functools.partial(cross_kernel, rows),
        "cross",
        in_specs=[WHOLE] * 2,
        out_specs=WHOLE,
        out_shape=sums,
    )(*in_vmem(across, swap))
    pair_sum = call(
        functools.partial(pair_kernel, factor),
        "pair",
        in_specs=[WHOLE] * 3 + [ANYWHERE],
        out_specs=WHOLE,
        out_shape=sums,
    )(*in_vmem(partial, other, cross), rest)

    known_one, known_other = call(
        known_kernel,
        "known",
        flops=4 * 10**9,
        in_specs=[WHOLE] * 7,
        out_specs=[WHOLE] * 2,
        out_shape=[block] * 2,
    )(*in_vmem(late_tiles, late, swap, far, query, keys, values))

    def add(*terms, out_shape=sums, after=known_one):
        return call(
            add_kernel,
            "add",
            in_specs=[WHOLE] * len(terms) + [ANYWHERE],
            out_specs=WHOLE,
            out_shape=out_shape,
        )(*in_vmem(*terms), after)

    terms = sum_terms(pair_sum, "ctx", add)
    gated, key_grad, value_grad, mark = call(
        last_kernel,
        "last",
        in_specs=[WHOLE] * 10,
        out_specs=[ANYWHERE] * 3 + [WHOLE],
        out_shape=outs + [pltpu.VMEM((SUBLANES, group_width), f32)],
        scratch_shapes=[half_block] * 2 + [pltpu.SemaphoreType.DMA((6 + 3 * PARTS,))],
    )(
        *in_vmem(ready_tiles, rest, forwarded, query, keys, values),
        *in_vmem(ready_one, ready_other, known_one, known_other),
    )
    whole_sums = jax.ShapeDtypeStruct((group_count, taps), f32)
    return (gated, key_grad, value_grad, add(*terms, out_shape=whole_sums, after=mark))


def solution(mesh):
    in_specs = (P("ctx", "grp"), P("ctx", "grp"), P("ctx", "grp"), P("ctx", "grp"), P("grp", None))
    out_specs = (P("ctx", "grp"), P("ctx", "grp"), P("ctx", "grp"), P("grp", None))
    return jax.shard_map(shards, mesh=mesh, in_specs=in_specs, out_specs=out_specs, check_vma=False)
```

```python
import functools
import math

import jax
import jax.numpy as jnp
from jax import lax
from jax.experimental import pallas as pl
from jax.experimental.pallas import tpu as pltpu
from jax.sharding import PartitionSpec as P

SUBLANES = 8
PARTS = 2
VMEM_LIMIT = 16 * 1024 * 1024
WHOLE = pl.BlockSpec(memory_space=pltpu.VMEM)
ANYWHERE = pl.BlockSpec(memory_space=pl.ANY)
DOT_ROWS = functools.partial(
    lax.dot_general,
    dimension_numbers=(((1,), (1,)), ((), ())),
    preferred_element_type=jnp.float32,
)
DOT = functools.partial(jnp.dot, preferred_element_type=jnp.float32)


def in_vmem(*arrays):
    return [pltpu.with_memory_space_constraint(array, pltpu.VMEM) for array in arrays]


def in_hbm(*arrays):
    return [pltpu.with_memory_space_constraint(array, pltpu.HBM) for array in arrays]


def moved(block, axis, distances):
    size = lax.axis_size(axis)
    route = [(i, i + distances[i % 2]) for i in range(size)]
    return lax.ppermute(block, axis, [pair for pair in route if 0 <= pair[1] < size])


def sum_terms(pair_sum, axis, add):
    size = lax.axis_size(axis)
    if size & (size - 1):
        even = lax.axis_index(axis) % 2 == 0
        return [lax.psum(jnp.where(even, pair_sum, 0.0), axis)]
    terms = [pair_sum]
    stride = 2
    while stride < size:
        own = terms[0] if len(terms) == 1 else add(*terms)
        members = 4 if 4 * stride <= size else 2
        rounds = [(1, (0, 3)), (2, range(4)), (3, range(4)), (1, (1, 2))] if members == 4 else [(1, range(2))]
        terms = [own]
        for turn, senders in rounds:
            places = [(i, i // stride % members) for i in range(size)]
            route = [
                (i, i + ((place + turn) % members - place) * stride) for i, place in places if place in senders
            ]
            terms.append(lax.ppermute(own, axis, route))
        stride *= members
    return terms


def is_odd():
    return lax.rem(lax.axis_index("ctx"), 2) == 1


def product(left, right):
    return (left.astype(jnp.float32) * right.astype(jnp.float32)).astype(jnp.bfloat16)


def scaled(value, factor):
    return (value * factor.astype(jnp.float32)).astype(jnp.bfloat16)


def columns_of(group, width):
    return slice(group * width, (group + 1) * width)


def launch(odd, moves, sems, used):
    copies = [(*move, sems.at[used + place]) for place, move in enumerate(moves)]
    for parity, source, target, sem in copies:
        @pl.when(odd if parity else jnp.logical_not(odd))
        def _():
            pltpu.make_async_copy(source, target, sem).start()
    return copies


def finish(odd, copies):
    for parity, source, target, sem in copies:
        @pl.when(odd if parity else jnp.logical_not(odd))
        def _():
            pltpu.make_async_copy(source, target, sem).wait()


def lines_summed(total):
    line = lax.broadcasted_iota(jnp.int32, total.shape, 0)
    bit = 1
    while bit < SUBLANES:
        total = jnp.where((line & bit) == bit, pltpu.roll(total, total.shape[1] - bit, 1), total)
        bit *= 2
    return jnp.sum(total, axis=0, keepdims=True)


def skewed_sum(outer, rows):
    width = outer.shape[1]
    total = outer[:SUBLANES]
    for start in range(SUBLANES, rows, SUBLANES):
        total = total + pltpu.roll(outer[start : start + SUBLANES], width - start, 1)
    return lines_summed(total)


def skewed_pair(outer, rows):
    width = outer.shape[1]
    lane = lax.broadcasted_iota(jnp.int32, (SUBLANES, width), 1)
    high = outer[:SUBLANES]
    low = jnp.zeros_like(high)
    for start in range(SUBLANES, rows, SUBLANES):
        turned = pltpu.roll(outer[start : start + SUBLANES], width - start, 1)
        above = lane < width - start
        high = high + jnp.where(above, turned, 0.0)
        low = low + jnp.where(above, 0.0, turned)
    return lines_summed(jnp.concatenate([low, high], axis=1))


def diagonal_kernel(query_hbm, keys_hbm, values_hbm, cotangent_hbm, out_ref, left, right, sems):
    odd = is_odd()
    half = out_ref.shape[1]
    low, high = pl.ds(0, half), pl.ds(half, half)
    copies = launch(
        odd,
        [
            (1, keys_hbm.at[:, low], left),
            (1, values_hbm.at[:, low], right),
            (0, cotangent_hbm.at[:, high], left),
            (0, query_hbm.at[:, high], right),
        ],
        sems,
        0,
    )
    finish(odd, copies)
    out_ref[...] = product(left[...], right[...])


def products_kernel(query_ref, keys_ref, values_ref, cotangent_ref, sent_ref, near_ref, across_ref):
    odd = is_odd()
    prod = product(keys_ref[...], values_ref[...])
    grad = product(cotangent_ref[...], query_ref[...])
    near_ref[...] = lax.select(odd, prod, grad)
    across_ref[...] = lax.select(odd, grad, prod)


def tiles_kernel(rows, taps_ref, ready_tiles, late_tiles):
    odd = is_odd()
    group_count, width = taps_ref.shape
    for group in range(group_count):
        row = taps_ref[group : group + 1, :].astype(jnp.float32)
        spread = jnp.concatenate(
            [jnp.zeros((SUBLANES, rows), jnp.float32), jnp.broadcast_to(row, (SUBLANES, width))],
            axis=1,
        )
        spread = pltpu.roll(spread, 0, 1, stride=1, stride_axis=0)
        bands = [
            pltpu.roll(spread, start, 1)[:, rows:] if start else spread[:, rows:]
            for start in range(0, rows, SUBLANES)
        ]
        band = jnp.concatenate(bands, axis=0)
        turned = [band[:, start : start + rows].T for start in range(0, width, rows)]
        turned = jnp.concatenate(turned, axis=1)
        ready_tiles[group] = lax.select(odd, band, turned).astype(jnp.bfloat16)
        late_tiles[group] = lax.select(odd, turned, band).astype(jnp.bfloat16)


def own_kernel(
    rows, ready_tiles, late_tiles, near_ref, across_ref, diagonal_ref, sum_ref, late_ref, ready_ref
):
    odd = is_odd()
    group_count, width = sum_ref.shape
    group_width = near_ref.shape[1] // group_count
    half = group_count // 2
    blank = jnp.zeros((rows, rows), jnp.float32)
    for group in range(group_count):
        columns = columns_of(group, group_width)
        late_ref[:, columns] = DOT(late_tiles[group, :, :rows], near_ref[:, columns])
        ready_ref[:, columns] = DOT(ready_tiles[group, :, :rows], across_ref[:, columns])
    middles = []
    for group in range(half):
        low, high = columns_of(group, group_width), columns_of(group + half, group_width)
        arrived = diagonal_ref[:, low]
        own = lax.select(odd, near_ref[:, high], near_ref[:, low])
        middles.append(DOT_ROWS(lax.select(odd, own, arrived), lax.select(odd, arrived, own)))
        tile = lax.select(
            odd, ready_tiles[group + half, :, rows : 2 * rows], ready_tiles[group, :, rows : 2 * rows]
        )
        more = DOT(tile, arrived)
        ready_ref[:, low] += lax.select(odd, blank, more)
        ready_ref[:, high] += lax.select(odd, more, blank)
    sums = []
    for group in range(group_count):
        columns = columns_of(group, group_width)
        near, across = near_ref[:, columns], across_ref[:, columns]
        outer = DOT_ROWS(lax.select(odd, near, across), lax.select(odd, across, near))
        if group < half:
            middle = lax.select(odd, blank, middles[group])
        else:
            middle = lax.select(odd, middles[group - half], blank)
        sums.append(skewed_sum(jnp.concatenate([outer, middle, blank], axis=1), rows)[:, : 2 * rows])
    sums = jnp.concatenate(sums, axis=0)
    sum_ref[...] = jnp.concatenate([sums, jnp.zeros((group_count, width - 2 * rows), jnp.float32)], axis=1)


def two_kernel(rows, sum_ref, near_ref, two_ref, out_ref):
    odd = is_odd()
    group_count, width = out_ref.shape
    group_width = near_ref.shape[1] // group_count
    sums = []
    for group in range(group_count):
        columns = columns_of(group, group_width)
        near, two = near_ref[:, columns], two_ref[:, columns]
        outer = DOT_ROWS(lax.select(odd, near, two), lax.select(odd, two, near))
        sums.append(skewed_pair(outer, rows))
    sums = jnp.concatenate(sums, axis=0)
    out_ref[...] = sum_ref[...] + jnp.concatenate(
        [jnp.zeros((group_count, width - 2 * rows), jnp.float32), sums], axis=1
    )


def cross_kernel(rows, across_ref, swap_ref, out_ref):
    odd = is_odd()
    group_count, width = out_ref.shape
    group_width = across_ref.shape[1] // group_count
    sums = []
    for group in range(group_count):
        columns = columns_of(group, group_width)
        across, swap = across_ref[:, columns], swap_ref[:, columns]
        outer = DOT_ROWS(lax.select(odd, swap, across), lax.select(odd, across, swap))
        sums.append(skewed_pair(outer, rows))
    sums = jnp.concatenate(sums, axis=0)
    out_ref[...] = jnp.concatenate([sums, jnp.zeros((group_count, width - 2 * rows), jnp.float32)], axis=1)


def pair_kernel(factor, sum_ref, other_ref, cross_ref, rest_ref, out_ref):
    out_ref[...] = (sum_ref[...] + other_ref[...] + cross_ref[...]) * factor


def add_kernel(*refs):
    *terms, _, out_ref = refs
    out_ref[...] = functools.reduce(jnp.add, [ref[...] for ref in terms])


def forward_kernel(far_ref, rest_ref, out_ref):
    half = out_ref.shape[1]
    out_ref[...] = lax.select(is_odd(), far_ref[:, half:], far_ref[:, :half])


def ready_kernel(
    tiles_ref, ready_ref, two_ref, query_ref, keys_ref, values_ref, sum_ref, rest_ref, one, other
):
    odd = is_odd()
    group_count, rows, _ = tiles_ref.shape
    group_width = two_ref.shape[1] // group_count
    half = group_count // 2
    for group in range(half):
        low, high = columns_of(group, group_width), columns_of(group + half, group_width)
        first = ready_ref[:, low] + DOT(tiles_ref[group, :, 2 * rows :], two_ref[:, low])
        second = ready_ref[:, high] + DOT(tiles_ref[group + half, :, 2 * rows :], two_ref[:, high])
        rest_ref[:, low] = lax.select(odd, first, second)
        known = lax.select(odd, second, first)
        one[:, low] = scaled(known, lax.select(odd, values_ref[:, high], query_ref[:, low]))
        other[:, low] = scaled(known, keys_ref[:, high])


def known_kernel(tiles_ref, late_ref, swap_ref, far_ref, query_ref, keys_ref, values_ref, one, other):
    odd = is_odd()
    group_count, rows, _ = tiles_ref.shape
    group_width = far_ref.shape[1] // group_count
    for group in range(group_count):
        columns = columns_of(group, group_width)
        arrived = jnp.concatenate([swap_ref[:, columns], far_ref[:, columns]], axis=0)
        late = late_ref[:, columns] + DOT(tiles_ref[group, :, rows:], arrived)
        one[:, columns] = scaled(late, lax.select(odd, query_ref[:, columns], values_ref[:, columns]))
        other[:, columns] = scaled(late, keys_ref[:, columns])


def last_kernel(
    tiles_ref, rest_ref, forwarded_ref, query_ref, keys_ref, values_ref,
    ready_one, ready_other, known_one, known_other,
    gated_out, key_out, value_out, mark_ref, one, other, sems,
):
    odd = is_odd()
    mark_ref[...] = jnp.zeros_like(mark_ref)
    group_count, rows, _ = tiles_ref.shape
    half = group_count // 2
    group_width = forwarded_ref.shape[1] // half
    step = max(1, half // PARTS)
    low_half, high_half = pl.ds(0, half * group_width), pl.ds(half * group_width, half * group_width)
    copies = launch(
        odd,
        [
            (0, known_one, key_out),
            (0, known_other, value_out),
            (0, ready_one, gated_out.at[:, low_half]),
            (1, known_one, gated_out),
            (1, ready_one, key_out.at[:, high_half]),
            (1, ready_other, value_out.at[:, high_half]),
        ],
        sems,
        0,
    )
    for group in range(half):
        low, high = columns_of(group, group_width), columns_of(group + half, group_width)
        tile = lax.select(
            odd, tiles_ref[group, :, rows : 2 * rows], tiles_ref[group + half, :, rows : 2 * rows]
        )
        ready = rest_ref[:, low] + DOT(tile, forwarded_ref[:, low])
        one[:, low] = scaled(ready, lax.select(odd, values_ref[:, low], query_ref[:, high]))
        other[:, low] = scaled(ready, keys_ref[:, low])
        if (group + 1) % step == 0:
            start, size = (group + 1 - step) * group_width, step * group_width
            part, place = pl.ds(start, size), pl.ds(start + half * group_width, size)
            moves = [
                (0, one.at[:, part], gated_out.at[:, place]),
                (1, one.at[:, part], key_out.at[:, part]),
                (1, other.at[:, part], value_out.at[:, part]),
            ]
            copies += launch(odd, moves, sems, len(copies))
    finish(odd, copies)


def shards(query, keys, values, cotangent, filter_taps):
    rows, local_width = query.shape
    group_count, taps = filter_taps.shape
    group_width = local_width // group_count
    half_width = local_width // 2
    factor = 1.0 / math.sqrt(rows * lax.axis_size("ctx") * group_width)

    def call(kernel, name, flops=10**6, **options):
        return pl.pallas_call(
            kernel,
            compiler_params=pltpu.CompilerParams(vmem_limit_bytes=VMEM_LIMIT),
            cost_estimate=pl.CostEstimate(flops=flops, bytes_accessed=10**5, transcendentals=0),
            name=name,
            **options,
        )

    bf16, f32 = jnp.bfloat16, jnp.float32
    block, half_block = pltpu.VMEM((rows, local_width), bf16), pltpu.VMEM((rows, half_width), bf16)
    wide, half_wide = pltpu.VMEM((rows, local_width), f32), pltpu.VMEM((rows, half_width), f32)
    tiles, sums = pltpu.VMEM((group_count, rows, taps), bf16), pltpu.VMEM((group_count, taps), f32)
    outs = [jax.ShapeDtypeStruct((rows, local_width), bf16)] * 3

    sent = call(
        diagonal_kernel,
        "diagonal",
        in_specs=[ANYWHERE] * 4,
        out_specs=WHOLE,
        out_shape=half_block,
        scratch_shapes=[half_block] * 2 + [pltpu.SemaphoreType.DMA((4,))],
    )(*in_hbm(query, keys, values, cotangent))
    diagonal = moved(sent, "ctx", (-1, 1))
    near, across = call(
        products_kernel,
        "products",
        in_specs=[WHOLE] * 4 + [ANYWHERE],
        out_specs=[WHOLE] * 2,
        out_shape=[block] * 2,
    )(*in_vmem(query, keys, values, cotangent), sent)
    two = moved(across, "ctx", (2, -2))
    far = moved(near, "ctx", (-2, 2))
    swap = moved(across, "ctx", (1, -1))

    ready_tiles, late_tiles = call(
        functools.partial(tiles_kernel, rows),
        "tiles",
        in_specs=[WHOLE],
        out_specs=[WHOLE] * 2,
        out_shape=[tiles] * 2,
    )(*in_vmem(filter_taps))
    partial, late, ready = call(
        functools.partial(own_kernel, rows),
        "own",
        flops=4 * 10**9,
        in_specs=[WHOLE] * 5,
        out_specs=[WHOLE] * 3,
        out_shape=[sums, wide, wide],
    )(*in_vmem(ready_tiles, late_tiles, near, across, diagonal))

    partial = call(
        functools.partial(two_kernel, rows),
        "two",
        in_specs=[WHOLE] * 3,
        out_specs=WHOLE,
        out_shape=sums,
    )(*in_vmem(partial, near, two))
    other = moved(partial, "ctx", (1, -1))

    rest, ready_one, ready_other = call(
        ready_kernel,
        "ready",
        in_specs=[WHOLE] * 6 + [ANYWHERE],
        out_specs=[WHOLE] * 3,
        out_shape=[half_wide, half_block, half_block],
    )(*in_vmem(ready_tiles, ready, two, query, keys, values), partial)

    forwarded = call(
        forward_kernel,
        "forward",
        in_specs=[WHOLE, ANYWHERE],
        out_specs=WHOLE,
        out_shape=half_block,
    )(*in_vmem(far), rest)
    forwarded = moved(forwarded, "ctx", (1, -1))

    cross = call(
        functools.partial(cross_kernel, rows),
        "cross",
        in_specs=[WHOLE] * 2,
        out_specs=WHOLE,
        out_shape=sums,
    )(*in_vmem(across, swap))
    pair_sum = call(
        functools.partial(pair_kernel, factor),
        "pair",
        in_specs=[WHOLE] * 3 + [ANYWHERE],
        out_specs=WHOLE,
        out_shape=sums,
    )(*in_vmem(partial, other, cross), rest)

    known_one, known_other = call(
        known_kernel,
        "known",
        flops=4 * 10**9,
        in_specs=[WHOLE] * 7,
        out_specs=[WHOLE] * 2,
        out_shape=[block] * 2,
    )(*in_vmem(late_tiles, late, swap, far, query, keys, values))

    def add(*terms, out_shape=sums, after=known_one):
        return call(
            add_kernel,
            "add",
            in_specs=[WHOLE] * len(terms) + [ANYWHERE],
            out_specs=WHOLE,
            out_shape=out_shape,
        )(*in_vmem(*terms), after)

    terms = sum_terms(pair_sum, "ctx", add)
    gated, key_grad, value_grad, mark = call(
        last_kernel,
        "last",
        in_specs=[WHOLE] * 10,
        out_specs=[ANYWHERE] * 3 + [WHOLE],
        out_shape=outs + [pltpu.VMEM((SUBLANES, group_width), f32)],
        scratch_shapes=[half_block] * 2 + [pltpu.SemaphoreType.DMA((6 + 3 * PARTS,))],
    )(
        *in_vmem(ready_tiles, rest, forwarded, query, keys, values),
        *in_vmem(ready_one, ready_other, known_one, known_other),
    )
    whole_sums = jax.ShapeDtypeStruct((group_count, taps), f32)
    return (gated, key_grad, value_grad, add(*terms, out_shape=whole_sums, after=mark))


def solution(mesh):
    in_specs = (P("ctx", "grp"), P("ctx", "grp"), P("ctx", "grp"), P("ctx", "grp"), P("grp", None))
    out_specs = (P("ctx", "grp"), P("ctx", "grp"), P("ctx", "grp"), P("grp", None))
    return jax.shard_map(shards, mesh=mesh, in_specs=in_specs, out_specs=out_specs, check_vma=False)
```

```python
import functools
import math

import jax
import jax.numpy as jnp
from jax import lax
from jax.experimental import pallas as pl
from jax.experimental.pallas import tpu as pltpu
from jax.sharding import PartitionSpec as P

SUBLANES = 8
PARTS = 2
VMEM_LIMIT = 16 * 1024 * 1024
WHOLE = pl.BlockSpec(memory_space=pltpu.VMEM)
ANYWHERE = pl.BlockSpec(memory_space=pl.ANY)
DOT_ROWS = functools.partial(
    lax.dot_general,
    dimension_numbers=(((1,), (1,)), ((), ())),
    preferred_element_type=jnp.float32,
)
DOT = functools.partial(jnp.dot, preferred_element_type=jnp.float32)


def in_vmem(*arrays):
    return [pltpu.with_memory_space_constraint(array, pltpu.VMEM) for array in arrays]


def in_hbm(*arrays):
    return [pltpu.with_memory_space_constraint(array, pltpu.HBM) for array in arrays]


def moved(block, axis, distances):
    size = lax.axis_size(axis)
    route = [(i, i + distances[i % 2]) for i in range(size)]
    return lax.ppermute(block, axis, [pair for pair in route if 0 <= pair[1] < size])


def sum_terms(pair_sum, axis, add):
    size = lax.axis_size(axis)
    if size & (size - 1):
        even = lax.axis_index(axis) % 2 == 0
        return [lax.psum(jnp.where(even, pair_sum, 0.0), axis)]
    terms = [pair_sum]
    stride = 2
    while stride < size:
        own = terms[0] if len(terms) == 1 else add(*terms)
        members = 4 if 4 * stride <= size else 2
        terms = [own]
        for turn in range(1, members):
            places = [(i, i // stride % members) for i in range(size)]
            route = [(i, i + ((place + turn) % members - place) * stride) for i, place in places]
            terms.append(lax.ppermute(own, axis, route))
        stride *= members
    return terms


def is_odd():
    return lax.rem(lax.axis_index("ctx"), 2) == 1


def product(left, right):
    return (left.astype(jnp.float32) * right.astype(jnp.float32)).astype(jnp.bfloat16)


def scaled(value, factor):
    return (value * factor.astype(jnp.float32)).astype(jnp.bfloat16)


def columns_of(group, width):
    return slice(group * width, (group + 1) * width)


def launch(odd, moves, sems, used):
    copies = [(*move, sems.at[used + place]) for place, move in enumerate(moves)]
    for parity, source, target, sem in copies:
        @pl.when(odd if parity else jnp.logical_not(odd))
        def _():
            pltpu.make_async_copy(source, target, sem).start()
    return copies


def finish(odd, copies):
    for parity, source, target, sem in copies:
        @pl.when(odd if parity else jnp.logical_not(odd))
        def _():
            pltpu.make_async_copy(source, target, sem).wait()


def lines_summed(total):
    line = lax.broadcasted_iota(jnp.int32, total.shape, 0)
    bit = 1
    while bit < SUBLANES:
        total = jnp.where((line & bit) == bit, pltpu.roll(total, total.shape[1] - bit, 1), total)
        bit *= 2
    return jnp.sum(total, axis=0, keepdims=True)


def skewed_sum(outer, rows):
    width = outer.shape[1]
    total = outer[:SUBLANES]
    for start in range(SUBLANES, rows, SUBLANES):
        total = total + pltpu.roll(outer[start : start + SUBLANES], width - start, 1)
    return lines_summed(total)


def skewed_pair(outer, rows):
    width = outer.shape[1]
    lane = lax.broadcasted_iota(jnp.int32, (SUBLANES, width), 1)
    high = outer[:SUBLANES]
    low = jnp.zeros_like(high)
    for start in range(SUBLANES, rows, SUBLANES):
        turned = pltpu.roll(outer[start : start + SUBLANES], width - start, 1)
        above = lane < width - start
        high = high + jnp.where(above, turned, 0.0)
        low = low + jnp.where(above, 0.0, turned)
    return lines_summed(jnp.concatenate([low, high], axis=1))


def diagonal_kernel(query_hbm, keys_hbm, values_hbm, cotangent_hbm, out_ref, left, right, sems):
    odd = is_odd()
    half = out_ref.shape[1]
    low, high = pl.ds(0, half), pl.ds(half, half)
    copies = launch(
        odd,
        [
            (1, keys_hbm.at[:, low], left),
            (1, values_hbm.at[:, low], right),
            (0, cotangent_hbm.at[:, high], left),
            (0, query_hbm.at[:, high], right),
        ],
        sems,
        0,
    )
    finish(odd, copies)
    out_ref[...] = product(left[...], right[...])


def products_kernel(
    query_ref, keys_ref, values_ref, cotangent_ref, sent_ref, near_ref, across_ref, low_ref, high_ref
):
    odd = is_odd()
    half = low_ref.shape[1]
    prod = product(keys_ref[...], values_ref[...])
    grad = product(cotangent_ref[...], query_ref[...])
    near_ref[...] = lax.select(odd, prod, grad)
    across = lax.select(odd, grad, prod)
    across_ref[...] = across
    low_ref[...] = across[:, :half]
    high_ref[...] = across[:, half:]


def tiles_kernel(rows, taps_ref, ready_tiles, late_tiles):
    odd = is_odd()
    group_count, width = taps_ref.shape
    for group in range(group_count):
        row = taps_ref[group : group + 1, :].astype(jnp.float32)
        spread = jnp.concatenate(
            [jnp.zeros((SUBLANES, rows), jnp.float32), jnp.broadcast_to(row, (SUBLANES, width))],
            axis=1,
        )
        spread = pltpu.roll(spread, 0, 1, stride=1, stride_axis=0)
        bands = [
            pltpu.roll(spread, start, 1)[:, rows:] if start else spread[:, rows:]
            for start in range(0, rows, SUBLANES)
        ]
        band = jnp.concatenate(bands, axis=0)
        turned = [band[:, start : start + rows].T for start in range(0, width, rows)]
        turned = jnp.concatenate(turned, axis=1)
        ready_tiles[group] = lax.select(odd, band, turned).astype(jnp.bfloat16)
        late_tiles[group] = lax.select(odd, turned, band).astype(jnp.bfloat16)


def own_kernel(
    rows, ready_tiles, late_tiles, near_ref, across_ref, diagonal_ref, sum_ref, late_ref, ready_ref
):
    odd = is_odd()
    group_count, width = sum_ref.shape
    group_width = near_ref.shape[1] // group_count
    half = group_count // 2
    blank = jnp.zeros((rows, rows), jnp.float32)
    for group in range(group_count):
        columns = columns_of(group, group_width)
        late_ref[:, columns] = DOT(late_tiles[group, :, :rows], near_ref[:, columns])
        ready_ref[:, columns] = DOT(ready_tiles[group, :, :rows], across_ref[:, columns])
    middles = []
    for group in range(half):
        low, high = columns_of(group, group_width), columns_of(group + half, group_width)
        arrived = diagonal_ref[:, low]
        own = lax.select(odd, near_ref[:, high], near_ref[:, low])
        middles.append(DOT_ROWS(lax.select(odd, own, arrived), lax.select(odd, arrived, own)))
        tile = lax.select(
            odd, ready_tiles[group + half, :, rows : 2 * rows], ready_tiles[group, :, rows : 2 * rows]
        )
        more = DOT(tile, arrived)
        ready_ref[:, low] += lax.select(odd, blank, more)
        ready_ref[:, high] += lax.select(odd, more, blank)
    sums = []
    for group in range(group_count):
        columns = columns_of(group, group_width)
        near, across = near_ref[:, columns], across_ref[:, columns]
        outer = DOT_ROWS(lax.select(odd, near, across), lax.select(odd, across, near))
        if group < half:
            middle = lax.select(odd, blank, middles[group])
        else:
            middle = lax.select(odd, middles[group - half], blank)
        sums.append(skewed_sum(jnp.concatenate([outer, middle, blank], axis=1), rows)[:, : 2 * rows])
    sums = jnp.concatenate(sums, axis=0)
    sum_ref[...] = jnp.concatenate([sums, jnp.zeros((group_count, width - 2 * rows), jnp.float32)], axis=1)


def two_kernel(rows, sum_ref, near_ref, two_ref, cross_ref, out_ref):
    odd = is_odd()
    group_count, width = out_ref.shape
    group_width = near_ref.shape[1] // group_count
    sums = []
    for group in range(group_count):
        columns = columns_of(group, group_width)
        near, two = near_ref[:, columns], two_ref[:, columns]
        outer = DOT_ROWS(lax.select(odd, near, two), lax.select(odd, two, near))
        sums.append(skewed_pair(outer, rows))
    sums = jnp.concatenate(sums, axis=0)
    out_ref[...] = sum_ref[...] + jnp.concatenate(
        [jnp.zeros((group_count, width - 2 * rows), jnp.float32), sums], axis=1
    )


def cross_kernel(rows, across_ref, swap_ref, after_ref, out_ref):
    odd = is_odd()
    group_count, width = out_ref.shape
    group_width = across_ref.shape[1] // group_count
    sums = []
    for group in range(group_count):
        columns = columns_of(group, group_width)
        across, swap = across_ref[:, columns], swap_ref[:, columns]
        outer = DOT_ROWS(lax.select(odd, swap, across), lax.select(odd, across, swap))
        sums.append(skewed_pair(outer, rows))
    sums = jnp.concatenate(sums, axis=0)
    out_ref[...] = jnp.concatenate([sums, jnp.zeros((group_count, width - 2 * rows), jnp.float32)], axis=1)


def pair_kernel(factor, sum_ref, other_ref, low_ref, high_ref, rest_ref, out_ref):
    half = low_ref.shape[0]
    out_ref[:half] = (sum_ref[:half] + other_ref[:half] + low_ref[...]) * factor
    out_ref[half:] = (sum_ref[half:] + other_ref[half:] + high_ref[...]) * factor


def add_kernel(*refs):
    *terms, _, out_ref = refs
    out_ref[...] = functools.reduce(jnp.add, [ref[...] for ref in terms])


def forward_kernel(far_ref, rest_ref, out_ref):
    half = out_ref.shape[1]
    out_ref[...] = lax.select(is_odd(), far_ref[:, half:], far_ref[:, :half])


def ready_kernel(
    tiles_ref, ready_ref, two_ref, query_ref, keys_ref, values_ref, sum_ref, rest_ref, one, other
):
    odd = is_odd()
    group_count, rows, _ = tiles_ref.shape
    group_width = two_ref.shape[1] // group_count
    half = group_count // 2
    for group in range(half):
        low, high = columns_of(group, group_width), columns_of(group + half, group_width)
        first = ready_ref[:, low] + DOT(tiles_ref[group, :, 2 * rows :], two_ref[:, low])
        second = ready_ref[:, high] + DOT(tiles_ref[group + half, :, 2 * rows :], two_ref[:, high])
        rest_ref[:, low] = lax.select(odd, first, second)
        known = lax.select(odd, second, first)
        one[:, low] = scaled(known, lax.select(odd, values_ref[:, high], query_ref[:, low]))
        other[:, low] = scaled(known, keys_ref[:, high])


def known_kernel(
    tiles_ref, late_ref, low_ref, high_ref, far_ref, query_ref, keys_ref, values_ref, one, other
):
    odd = is_odd()
    group_count, rows, _ = tiles_ref.shape
    group_width = far_ref.shape[1] // group_count
    half = group_count // 2
    for group in range(group_count):
        columns = columns_of(group, group_width)
        inner = columns_of(group % half, group_width)
        swap = (low_ref if group < half else high_ref)[:, inner]
        arrived = jnp.concatenate([swap, far_ref[:, columns]], axis=0)
        late = late_ref[:, columns] + DOT(tiles_ref[group, :, rows:], arrived)
        one[:, columns] = scaled(late, lax.select(odd, query_ref[:, columns], values_ref[:, columns]))
        other[:, columns] = scaled(late, keys_ref[:, columns])


def last_kernel(
    tiles_ref, rest_ref, forwarded_ref, query_ref, keys_ref, values_ref,
    ready_one, ready_other, known_one, known_other,
    gated_out, key_out, value_out, mark_ref, one, other, sems,
):
    odd = is_odd()
    mark_ref[...] = jnp.zeros_like(mark_ref)
    group_count, rows, _ = tiles_ref.shape
    half = group_count // 2
    group_width = forwarded_ref.shape[1] // half
    step = max(1, half // PARTS)
    low_half, high_half = pl.ds(0, half * group_width), pl.ds(half * group_width, half * group_width)
    copies = launch(
        odd,
        [
            (0, known_one, key_out),
            (0, known_other, value_out),
            (0, ready_one, gated_out.at[:, low_half]),
            (1, known_one, gated_out),
            (1, ready_one, key_out.at[:, high_half]),
            (1, ready_other, value_out.at[:, high_half]),
        ],
        sems,
        0,
    )
    for group in range(half):
        low, high = columns_of(group, group_width), columns_of(group + half, group_width)
        tile = lax.select(
            odd, tiles_ref[group, :, rows : 2 * rows], tiles_ref[group + half, :, rows : 2 * rows]
        )
        ready = rest_ref[:, low] + DOT(tile, forwarded_ref[:, low])
        one[:, low] = scaled(ready, lax.select(odd, values_ref[:, low], query_ref[:, high]))
        other[:, low] = scaled(ready, keys_ref[:, low])
        if (group + 1) % step == 0:
            start, size = (group + 1 - step) * group_width, step * group_width
            part, place = pl.ds(start, size), pl.ds(start + half * group_width, size)
            moves = [
                (0, one.at[:, part], gated_out.at[:, place]),
                (1, one.at[:, part], key_out.at[:, part]),
                (1, other.at[:, part], value_out.at[:, part]),
            ]
            copies += launch(odd, moves, sems, len(copies))
    finish(odd, copies)


def shards(query, keys, values, cotangent, filter_taps):
    rows, local_width = query.shape
    group_count, taps = filter_taps.shape
    group_width = local_width // group_count
    half_width = local_width // 2
    factor = 1.0 / math.sqrt(rows * lax.axis_size("ctx") * group_width)

    def call(kernel, name, flops=10**6, **options):
        return pl.pallas_call(
            kernel,
            compiler_params=pltpu.CompilerParams(vmem_limit_bytes=VMEM_LIMIT),
            cost_estimate=pl.CostEstimate(flops=flops, bytes_accessed=10**5, transcendentals=0),
            name=name,
            **options,
        )

    bf16, f32 = jnp.bfloat16, jnp.float32
    block, half_block = pltpu.VMEM((rows, local_width), bf16), pltpu.VMEM((rows, half_width), bf16)
    wide, half_wide = pltpu.VMEM((rows, local_width), f32), pltpu.VMEM((rows, half_width), f32)
    tiles, sums = pltpu.VMEM((group_count, rows, taps), bf16), pltpu.VMEM((group_count, taps), f32)
    half_sums = pltpu.VMEM((group_count // 2, taps), f32)
    outs = [jax.ShapeDtypeStruct((rows, local_width), bf16)] * 3

    sent = call(
        diagonal_kernel,
        "diagonal",
        in_specs=[ANYWHERE] * 4,
        out_specs=WHOLE,
        out_shape=half_block,
        scratch_shapes=[half_block] * 2 + [pltpu.SemaphoreType.DMA((4,))],
    )(*in_hbm(query, keys, values, cotangent))
    diagonal = moved(sent, "ctx", (-1, 1))
    near, across, across_low, across_high = call(
        products_kernel,
        "products",
        in_specs=[WHOLE] * 4 + [ANYWHERE],
        out_specs=[WHOLE] * 4,
        out_shape=[block, block, half_block, half_block],
    )(*in_vmem(query, keys, values, cotangent), sent)
    two = moved(across, "ctx", (2, -2))
    far = moved(near, "ctx", (-2, 2))
    swap_low = moved(across_low, "ctx", (1, -1))
    swap_high = moved(across_high, "ctx", (1, -1))

    ready_tiles, late_tiles = call(
        functools.partial(tiles_kernel, rows),
        "tiles",
        in_specs=[WHOLE],
        out_specs=[WHOLE] * 2,
        out_shape=[tiles] * 2,
    )(*in_vmem(filter_taps))
    partial, late, ready = call(
        functools.partial(own_kernel, rows),
        "own",
        flops=4 * 10**9,
        in_specs=[WHOLE] * 5,
        out_specs=[WHOLE] * 3,
        out_shape=[sums, wide, wide],
    )(*in_vmem(ready_tiles, late_tiles, near, across, diagonal))

    def cross_of(own, swap, after):
        return call(
            functools.partial(cross_kernel, rows),
            "cross",
            in_specs=[WHOLE] * 2 + [ANYWHERE],
            out_specs=WHOLE,
            out_shape=half_sums,
        )(*in_vmem(own, swap), after)

    cross_low = cross_of(across_low, swap_low, partial)
    partial = call(
        functools.partial(two_kernel, rows),
        "two",
        in_specs=[WHOLE] * 3 + [ANYWHERE],
        out_specs=WHOLE,
        out_shape=sums,
    )(*in_vmem(partial, near, two), cross_low)
    other = moved(partial, "ctx", (1, -1))

    rest, ready_one, ready_other = call(
        ready_kernel,
        "ready",
        in_specs=[WHOLE] * 6 + [ANYWHERE],
        out_specs=[WHOLE] * 3,
        out_shape=[half_wide, half_block, half_block],
    )(*in_vmem(ready_tiles, ready, two, query, keys, values), partial)

    sent_on = call(
        forward_kernel,
        "forward",
        in_specs=[WHOLE, ANYWHERE],
        out_specs=WHOLE,
        out_shape=half_block,
    )(*in_vmem(far), rest)
    forwarded = moved(sent_on, "ctx", (1, -1))

    pair_sum = call(
        functools.partial(pair_kernel, factor),
        "pair",
        in_specs=[WHOLE] * 4 + [ANYWHERE],
        out_specs=WHOLE,
        out_shape=sums,
    )(*in_vmem(partial, other, cross_low, cross_of(across_high, swap_high, sent_on)), rest)

    known_one, known_other = call(
        known_kernel,
        "known",
        flops=4 * 10**9,
        in_specs=[WHOLE] * 8,
        out_specs=[WHOLE] * 2,
        out_shape=[block] * 2,
    )(*in_vmem(late_tiles, late, swap_low, swap_high, far, query, keys, values))

    def add(*terms, out_shape=sums, after=known_one):
        return call(
            add_kernel,
            "add",
            in_specs=[WHOLE] * len(terms) + [ANYWHERE],
            out_specs=WHOLE,
            out_shape=out_shape,
        )(*in_vmem(*terms), after)

    terms = sum_terms(pair_sum, "ctx", add)
    gated, key_grad, value_grad, mark = call(
        last_kernel,
        "last",
        in_specs=[WHOLE] * 10,
        out_specs=[ANYWHERE] * 3 + [WHOLE],
        out_shape=outs + [pltpu.VMEM((SUBLANES, group_width), f32)],
        scratch_shapes=[half_block] * 2 + [pltpu.SemaphoreType.DMA((6 + 3 * PARTS,))],
    )(
        *in_vmem(ready_tiles, rest, forwarded, query, keys, values),
        *in_vmem(ready_one, ready_other, known_one, known_other),
    )
    whole_sums = jax.ShapeDtypeStruct((group_count, taps), f32)
    return (gated, key_grad, value_grad, add(*terms, out_shape=whole_sums, after=mark))


def solution(mesh):
    in_specs = (P("ctx", "grp"), P("ctx", "grp"), P("ctx", "grp"), P("ctx", "grp"), P("grp", None))
    out_specs = (P("ctx", "grp"), P("ctx", "grp"), P("ctx", "grp"), P("grp", None))
    return jax.shard_map(shards, mesh=mesh, in_specs=in_specs, out_specs=out_specs, check_vma=False)
```

```python
import functools
import math

import jax
import jax.numpy as jnp
from jax import lax
from jax.experimental import pallas as pl
from jax.experimental.pallas import tpu as pltpu
from jax.sharding import PartitionSpec as P

SUBLANES = 8
PARTS = 2
VMEM_LIMIT = 16 * 1024 * 1024
WHOLE = pl.BlockSpec(memory_space=pltpu.VMEM)
ANYWHERE = pl.BlockSpec(memory_space=pl.ANY)
DOT_ROWS = functools.partial(
    lax.dot_general,
    dimension_numbers=(((1,), (1,)), ((), ())),
    preferred_element_type=jnp.float32,
)
DOT = functools.partial(jnp.dot, preferred_element_type=jnp.float32)


def in_vmem(*arrays):
    return [pltpu.with_memory_space_constraint(array, pltpu.VMEM) for array in arrays]


def in_hbm(*arrays):
    return [pltpu.with_memory_space_constraint(array, pltpu.HBM) for array in arrays]


def moved(block, axis, distances):
    size = lax.axis_size(axis)
    route = [(i, i + distances[i % 2]) for i in range(size)]
    return lax.ppermute(block, axis, [pair for pair in route if 0 <= pair[1] < size])


def sum_terms(pair_sum, axis, add):
    size = lax.axis_size(axis)
    if size & (size - 1):
        even = lax.axis_index(axis) % 2 == 0
        return [lax.psum(jnp.where(even, pair_sum, 0.0), axis)]
    terms = [pair_sum]
    stride = 2
    while stride < size:
        own = terms[0] if len(terms) == 1 else add(*terms)
        members = 4 if 4 * stride <= size else 2
        terms = [own]
        for turn in range(1, members):
            places = [(i, i // stride % members) for i in range(size)]
            route = [(i, i + ((place + turn) % members - place) * stride) for i, place in places]
            terms.append(lax.ppermute(own, axis, route))
        stride *= members
    return terms


def is_odd():
    return lax.rem(lax.axis_index("ctx"), 2) == 1


def product(left, right):
    return (left.astype(jnp.float32) * right.astype(jnp.float32)).astype(jnp.bfloat16)


def scaled(value, factor):
    return (value * factor.astype(jnp.float32)).astype(jnp.bfloat16)


def columns_of(group, width):
    return slice(group * width, (group + 1) * width)


def launch(odd, moves, sems, used):
    copies = [(*move, sems.at[used + place]) for place, move in enumerate(moves)]
    for parity, source, target, sem in copies:
        @pl.when(odd if parity else jnp.logical_not(odd))
        def _():
            pltpu.make_async_copy(source, target, sem).start()
    return copies


def finish(odd, copies):
    for parity, source, target, sem in copies:
        @pl.when(odd if parity else jnp.logical_not(odd))
        def _():
            pltpu.make_async_copy(source, target, sem).wait()


def lines_summed(total):
    line = lax.broadcasted_iota(jnp.int32, total.shape, 0)
    bit = 1
    while bit < SUBLANES:
        total = jnp.where((line & bit) == bit, pltpu.roll(total, total.shape[1] - bit, 1), total)
        bit *= 2
    return jnp.sum(total, axis=0, keepdims=True)


def skewed_sum(outer, rows):
    width = outer.shape[1]
    total = outer[:SUBLANES]
    for start in range(SUBLANES, rows, SUBLANES):
        total = total + pltpu.roll(outer[start : start + SUBLANES], width - start, 1)
    return lines_summed(total)


def skewed_pairs(outer_ref):
    group_count, rows, width = outer_ref.shape

    def lines(start):
        return outer_ref[:, start : start + SUBLANES, :].reshape(group_count * SUBLANES, width)

    high = lines(0)
    low = jnp.zeros_like(high)
    lane = lax.broadcasted_iota(jnp.int32, high.shape, 1)
    for start in range(SUBLANES, rows, SUBLANES):
        turned = pltpu.roll(lines(start), width - start, 1)
        above = lane < width - start
        high = high + jnp.where(above, turned, 0.0)
        low = low + jnp.where(above, 0.0, turned)
    total = jnp.concatenate([low, high], axis=1)
    line = lax.broadcasted_iota(jnp.int32, total.shape, 0)
    bit = 1
    while bit < SUBLANES:
        total = jnp.where((line & bit) == bit, pltpu.roll(total, 2 * width - bit, 1), total)
        bit *= 2
    return jnp.sum(total.reshape(group_count, SUBLANES, 2 * width), axis=1)


def diagonal_kernel(query_hbm, keys_hbm, values_hbm, cotangent_hbm, out_ref, left, right, sems):
    odd = is_odd()
    half = out_ref.shape[1]
    low, high = pl.ds(0, half), pl.ds(half, half)
    copies = launch(
        odd,
        [
            (1, keys_hbm.at[:, low], left),
            (1, values_hbm.at[:, low], right),
            (0, cotangent_hbm.at[:, high], left),
            (0, query_hbm.at[:, high], right),
        ],
        sems,
        0,
    )
    finish(odd, copies)
    out_ref[...] = product(left[...], right[...])


def products_kernel(query_ref, keys_ref, values_ref, cotangent_ref, sent_ref, near_ref, across_ref):
    odd = is_odd()
    prod = product(keys_ref[...], values_ref[...])
    grad = product(cotangent_ref[...], query_ref[...])
    near_ref[...] = lax.select(odd, prod, grad)
    across_ref[...] = lax.select(odd, grad, prod)


def tiles_kernel(rows, taps_ref, ready_tiles, late_tiles):
    odd = is_odd()
    group_count, width = taps_ref.shape
    for group in range(group_count):
        row = taps_ref[group : group + 1, :].astype(jnp.float32)
        spread = jnp.concatenate(
            [jnp.zeros((SUBLANES, rows), jnp.float32), jnp.broadcast_to(row, (SUBLANES, width))],
            axis=1,
        )
        spread = pltpu.roll(spread, 0, 1, stride=1, stride_axis=0)
        bands = [
            pltpu.roll(spread, start, 1)[:, rows:] if start else spread[:, rows:]
            for start in range(0, rows, SUBLANES)
        ]
        band = jnp.concatenate(bands, axis=0)
        turned = [band[:, start : start + rows].T for start in range(0, width, rows)]
        turned = jnp.concatenate(turned, axis=1)
        ready_tiles[group] = lax.select(odd, band, turned).astype(jnp.bfloat16)
        late_tiles[group] = lax.select(odd, turned, band).astype(jnp.bfloat16)


def own_kernel(
    rows, ready_tiles, late_tiles, near_ref, across_ref, diagonal_ref, sum_ref, late_ref, ready_ref
):
    odd = is_odd()
    group_count, width = sum_ref.shape
    group_width = near_ref.shape[1] // group_count
    half = group_count // 2
    blank = jnp.zeros((rows, rows), jnp.float32)
    for group in range(group_count):
        columns = columns_of(group, group_width)
        late_ref[:, columns] = DOT(late_tiles[group, :, :rows], near_ref[:, columns])
        ready_ref[:, columns] = DOT(ready_tiles[group, :, :rows], across_ref[:, columns])
    middles = []
    for group in range(half):
        low, high = columns_of(group, group_width), columns_of(group + half, group_width)
        arrived = diagonal_ref[:, low]
        own = lax.select(odd, near_ref[:, high], near_ref[:, low])
        middles.append(DOT_ROWS(lax.select(odd, own, arrived), lax.select(odd, arrived, own)))
        tile = lax.select(
            odd, ready_tiles[group + half, :, rows : 2 * rows], ready_tiles[group, :, rows : 2 * rows]
        )
        more = DOT(tile, arrived)
        ready_ref[:, low] += lax.select(odd, blank, more)
        ready_ref[:, high] += lax.select(odd, more, blank)
    sums = []
    for group in range(group_count):
        columns = columns_of(group, group_width)
        near, across = near_ref[:, columns], across_ref[:, columns]
        outer = DOT_ROWS(lax.select(odd, near, across), lax.select(odd, across, near))
        if group < half:
            middle = lax.select(odd, blank, middles[group])
        else:
            middle = lax.select(odd, middles[group - half], blank)
        sums.append(skewed_sum(jnp.concatenate([outer, middle, blank], axis=1), rows)[:, : 2 * rows])
    sums = jnp.concatenate(sums, axis=0)
    sum_ref[...] = jnp.concatenate([sums, jnp.zeros((group_count, width - 2 * rows), jnp.float32)], axis=1)


def two_kernel(rows, sum_ref, near_ref, two_ref, out_ref, outer_ref):
    odd = is_odd()
    group_count, width = out_ref.shape
    group_width = near_ref.shape[1] // group_count
    for group in range(group_count):
        columns = columns_of(group, group_width)
        near, two = near_ref[:, columns], two_ref[:, columns]
        outer_ref[group] = DOT_ROWS(lax.select(odd, near, two), lax.select(odd, two, near))
    sums = skewed_pairs(outer_ref)
    out_ref[...] = sum_ref[...] + jnp.concatenate(
        [jnp.zeros((group_count, width - 2 * rows), jnp.float32), sums], axis=1
    )


def cross_kernel(rows, across_ref, swap_ref, out_ref, outer_ref):
    odd = is_odd()
    group_count, width = out_ref.shape
    group_width = across_ref.shape[1] // group_count
    for group in range(group_count):
        columns = columns_of(group, group_width)
        across, swap = across_ref[:, columns], swap_ref[:, columns]
        outer_ref[group] = DOT_ROWS(lax.select(odd, swap, across), lax.select(odd, across, swap))
    sums = skewed_pairs(outer_ref)
    out_ref[...] = jnp.concatenate([sums, jnp.zeros((group_count, width - 2 * rows), jnp.float32)], axis=1)


def pair_kernel(factor, sum_ref, other_ref, cross_ref, rest_ref, out_ref):
    out_ref[...] = (sum_ref[...] + other_ref[...] + cross_ref[...]) * factor


def add_kernel(*refs):
    *terms, _, out_ref = refs
    out_ref[...] = functools.reduce(jnp.add, [ref[...] for ref in terms])


def forward_kernel(far_ref, rest_ref, out_ref):
    half = out_ref.shape[1]
    out_ref[...] = lax.select(is_odd(), far_ref[:, half:], far_ref[:, :half])


def ready_kernel(
    tiles_ref, ready_ref, two_ref, query_ref, keys_ref, values_ref, sum_ref, rest_ref, one, other
):
    odd = is_odd()
    group_count, rows, _ = tiles_ref.shape
    group_width = two_ref.shape[1] // group_count
    half = group_count // 2
    for group in range(half):
        low, high = columns_of(group, group_width), columns_of(group + half, group_width)
        first = ready_ref[:, low] + DOT(tiles_ref[group, :, 2 * rows :], two_ref[:, low])
        second = ready_ref[:, high] + DOT(tiles_ref[group + half, :, 2 * rows :], two_ref[:, high])
        rest_ref[:, low] = lax.select(odd, first, second)
        known = lax.select(odd, second, first)
        one[:, low] = scaled(known, lax.select(odd, values_ref[:, high], query_ref[:, low]))
        other[:, low] = scaled(known, keys_ref[:, high])


def known_kernel(tiles_ref, late_ref, swap_ref, far_ref, query_ref, keys_ref, values_ref, one, other):
    odd = is_odd()
    group_count, rows, _ = tiles_ref.shape
    group_width = far_ref.shape[1] // group_count
    for group in range(group_count):
        columns = columns_of(group, group_width)
        arrived = jnp.concatenate([swap_ref[:, columns], far_ref[:, columns]], axis=0)
        late = late_ref[:, columns] + DOT(tiles_ref[group, :, rows:], arrived)
        one[:, columns] = scaled(late, lax.select(odd, query_ref[:, columns], values_ref[:, columns]))
        other[:, columns] = scaled(late, keys_ref[:, columns])


def last_kernel(
    tiles_ref, rest_ref, forwarded_ref, query_ref, keys_ref, values_ref,
    ready_one, ready_other, known_one, known_other,
    gated_out, key_out, value_out, mark_ref, one, other, sems,
):
    odd = is_odd()
    mark_ref[...] = jnp.zeros_like(mark_ref)
    group_count, rows, _ = tiles_ref.shape
    half = group_count // 2
    group_width = forwarded_ref.shape[1] // half
    step = max(1, half // PARTS)
    low_half, high_half = pl.ds(0, half * group_width), pl.ds(half * group_width, half * group_width)
    copies = launch(
        odd,
        [
            (0, known_one, key_out),
            (0, known_other, value_out),
            (0, ready_one, gated_out.at[:, low_half]),
            (1, known_one, gated_out),
            (1, ready_one, key_out.at[:, high_half]),
            (1, ready_other, value_out.at[:, high_half]),
        ],
        sems,
        0,
    )
    for group in range(half):
        low, high = columns_of(group, group_width), columns_of(group + half, group_width)
        tile = lax.select(
            odd, tiles_ref[group, :, rows : 2 * rows], tiles_ref[group + half, :, rows : 2 * rows]
        )
        ready = rest_ref[:, low] + DOT(tile, forwarded_ref[:, low])
        one[:, low] = scaled(ready, lax.select(odd, values_ref[:, low], query_ref[:, high]))
        other[:, low] = scaled(ready, keys_ref[:, low])
        if (group + 1) % step == 0:
            start, size = (group + 1 - step) * group_width, step * group_width
            part, place = pl.ds(start, size), pl.ds(start + half * group_width, size)
            moves = [
                (0, one.at[:, part], gated_out.at[:, place]),
                (1, one.at[:, part], key_out.at[:, part]),
                (1, other.at[:, part], value_out.at[:, part]),
            ]
            copies += launch(odd, moves, sems, len(copies))
    finish(odd, copies)


def shards(query, keys, values, cotangent, filter_taps):
    rows, local_width = query.shape
    group_count, taps = filter_taps.shape
    group_width = local_width // group_count
    half_width = local_width // 2
    factor = 1.0 / math.sqrt(rows * lax.axis_size("ctx") * group_width)

    def call(kernel, name, flops=10**6, **options):
        return pl.pallas_call(
            kernel,
            compiler_params=pltpu.CompilerParams(vmem_limit_bytes=VMEM_LIMIT),
            cost_estimate=pl.CostEstimate(flops=flops, bytes_accessed=10**5, transcendentals=0),
            name=name,
            **options,
        )

    bf16, f32 = jnp.bfloat16, jnp.float32
    block, half_block = pltpu.VMEM((rows, local_width), bf16), pltpu.VMEM((rows, half_width), bf16)
    wide, half_wide = pltpu.VMEM((rows, local_width), f32), pltpu.VMEM((rows, half_width), f32)
    tiles, sums = pltpu.VMEM((group_count, rows, taps), bf16), pltpu.VMEM((group_count, taps), f32)
    outs = [jax.ShapeDtypeStruct((rows, local_width), bf16)] * 3

    sent = call(
        diagonal_kernel,
        "diagonal",
        in_specs=[ANYWHERE] * 4,
        out_specs=WHOLE,
        out_shape=half_block,
        scratch_shapes=[half_block] * 2 + [pltpu.SemaphoreType.DMA((4,))],
    )(*in_hbm(query, keys, values, cotangent))
    diagonal = moved(sent, "ctx", (-1, 1))
    near, across = call(
        products_kernel,
        "products",
        in_specs=[WHOLE] * 4 + [ANYWHERE],
        out_specs=[WHOLE] * 2,
        out_shape=[block] * 2,
    )(*in_vmem(query, keys, values, cotangent), sent)
    two = moved(across, "ctx", (2, -2))
    far = moved(near, "ctx", (-2, 2))
    swap = moved(across, "ctx", (1, -1))

    ready_tiles, late_tiles = call(
        functools.partial(tiles_kernel, rows),
        "tiles",
        in_specs=[WHOLE],
        out_specs=[WHOLE] * 2,
        out_shape=[tiles] * 2,
    )(*in_vmem(filter_taps))
    partial, late, ready = call(
        functools.partial(own_kernel, rows),
        "own",
        flops=4 * 10**9,
        in_specs=[WHOLE] * 5,
        out_specs=[WHOLE] * 3,
        out_shape=[sums, wide, wide],
    )(*in_vmem(ready_tiles, late_tiles, near, across, diagonal))

    partial = call(
        functools.partial(two_kernel, rows),
        "two",
        in_specs=[WHOLE] * 3,
        out_specs=WHOLE,
        out_shape=sums,
        scratch_shapes=[pltpu.VMEM((group_count, rows, rows), f32)],
    )(*in_vmem(partial, near, two))
    other = moved(partial, "ctx", (1, -1))

    rest, ready_one, ready_other = call(
        ready_kernel,
        "ready",
        in_specs=[WHOLE] * 6 + [ANYWHERE],
        out_specs=[WHOLE] * 3,
        out_shape=[half_wide, half_block, half_block],
    )(*in_vmem(ready_tiles, ready, two, query, keys, values), partial)

    forwarded = call(
        forward_kernel,
        "forward",
        in_specs=[WHOLE, ANYWHERE],
        out_specs=WHOLE,
        out_shape=half_block,
    )(*in_vmem(far), rest)
    forwarded = moved(forwarded, "ctx", (1, -1))

    cross = call(
        functools.partial(cross_kernel, rows),
        "cross",
        in_specs=[WHOLE] * 2,
        out_specs=WHOLE,
        out_shape=sums,
        scratch_shapes=[pltpu.VMEM((group_count, rows, rows), f32)],
    )(*in_vmem(across, swap))
    pair_sum = call(
        functools.partial(pair_kernel, factor),
        "pair",
        in_specs=[WHOLE] * 3 + [ANYWHERE],
        out_specs=WHOLE,
        out_shape=sums,
    )(*in_vmem(partial, other, cross), rest)

    known_one, known_other = call(
        known_kernel,
        "known",
        flops=4 * 10**9,
        in_specs=[WHOLE] * 7,
        out_specs=[WHOLE] * 2,
        out_shape=[block] * 2,
    )(*in_vmem(late_tiles, late, swap, far, query, keys, values))

    def add(*terms, out_shape=sums, after=known_one):
        return call(
            add_kernel,
            "add",
            in_specs=[WHOLE] * len(terms) + [ANYWHERE],
            out_specs=WHOLE,
            out_shape=out_shape,
        )(*in_vmem(*terms), after)

    terms = sum_terms(pair_sum, "ctx", add)
    gated, key_grad, value_grad, mark = call(
        last_kernel,
        "last",
        in_specs=[WHOLE] * 10,
        out_specs=[ANYWHERE] * 3 + [WHOLE],
        out_shape=outs + [pltpu.VMEM((SUBLANES, group_width), f32)],
        scratch_shapes=[half_block] * 2 + [pltpu.SemaphoreType.DMA((6 + 3 * PARTS,))],
    )(
        *in_vmem(ready_tiles, rest, forwarded, query, keys, values),
        *in_vmem(ready_one, ready_other, known_one, known_other),
    )
    whole_sums = jax.ShapeDtypeStruct((group_count, taps), f32)
    return (gated, key_grad, value_grad, add(*terms, out_shape=whole_sums, after=mark))


def solution(mesh):
    in_specs = (P("ctx", "grp"), P("ctx", "grp"), P("ctx", "grp"), P("ctx", "grp"), P("grp", None))
    out_specs = (P("ctx", "grp"), P("ctx", "grp"), P("ctx", "grp"), P("grp", None))
    return jax.shard_map(shards, mesh=mesh, in_specs=in_specs, out_specs=out_specs, check_vma=False)
```

```python
import functools
import math

import jax
import jax.numpy as jnp
from jax import lax
from jax.experimental import pallas as pl
from jax.experimental.pallas import tpu as pltpu
from jax.sharding import PartitionSpec as P

SUBLANES = 8
PARTS = 2
VMEM_LIMIT = 16 * 1024 * 1024
WHOLE = pl.BlockSpec(memory_space=pltpu.VMEM)
ANYWHERE = pl.BlockSpec(memory_space=pl.ANY)
DOT_ROWS = functools.partial(
    lax.dot_general,
    dimension_numbers=(((1,), (1,)), ((), ())),
    preferred_element_type=jnp.float32,
)
DOT = functools.partial(jnp.dot, preferred_element_type=jnp.float32)


def in_vmem(*arrays):
    return [pltpu.with_memory_space_constraint(array, pltpu.VMEM) for array in arrays]


def in_hbm(*arrays):
    return [pltpu.with_memory_space_constraint(array, pltpu.HBM) for array in arrays]


def moved(block, axis, distances):
    size = lax.axis_size(axis)
    route = [(i, i + distances[i % 2]) for i in range(size)]
    return lax.ppermute(block, axis, [pair for pair in route if 0 <= pair[1] < size])


def sum_terms(pair_sum, axis, add):
    size = lax.axis_size(axis)
    if size & (size - 1):
        even = lax.axis_index(axis) % 2 == 0
        return [lax.psum(jnp.where(even, pair_sum, 0.0), axis)]
    terms = [pair_sum]
    stride = 2
    while stride < size:
        own = terms[0] if len(terms) == 1 else add(*terms)
        members = 4 if 4 * stride <= size else 2
        terms = [own]
        for turn in range(1, members):
            places = [(i, i // stride % members) for i in range(size)]
            route = [(i, i + ((place + turn) % members - place) * stride) for i, place in places]
            terms.append(lax.ppermute(own, axis, route))
        stride *= members
    return terms


def is_odd():
    return lax.rem(lax.axis_index("ctx"), 2) == 1


def product(left, right):
    return (left.astype(jnp.float32) * right.astype(jnp.float32)).astype(jnp.bfloat16)


def scaled(value, factor):
    return (value * factor.astype(jnp.float32)).astype(jnp.bfloat16)


def columns_of(group, width):
    return slice(group * width, (group + 1) * width)


def launch(odd, moves, sems, used):
    copies = [(*move, sems.at[used + place]) for place, move in enumerate(moves)]
    for parity, source, target, sem in copies:
        @pl.when(odd if parity else jnp.logical_not(odd))
        def _():
            pltpu.make_async_copy(source, target, sem).start()
    return copies


def finish(odd, copies):
    for parity, source, target, sem in copies:
        @pl.when(odd if parity else jnp.logical_not(odd))
        def _():
            pltpu.make_async_copy(source, target, sem).wait()


def lines_summed(total):
    line = lax.broadcasted_iota(jnp.int32, total.shape, 0)
    bit = 1
    while bit < SUBLANES:
        total = jnp.where((line & bit) == bit, pltpu.roll(total, total.shape[1] - bit, 1), total)
        bit *= 2
    return jnp.sum(total, axis=0, keepdims=True)


def skewed_sum(outer, rows):
    width = outer.shape[1]
    total = outer[:SUBLANES]
    for start in range(SUBLANES, rows, SUBLANES):
        total = total + pltpu.roll(outer[start : start + SUBLANES], width - start, 1)
    return lines_summed(total)


def skewed_pairs(outer_ref, right):
    group_count, rows, width = outer_ref.shape

    def lines(start):
        return outer_ref[:, start : start + SUBLANES, :].reshape(group_count * SUBLANES, width)

    first = lines(0)
    blank = jnp.zeros_like(first)
    high = lax.select(right, blank, first)
    low = lax.select(right, first, blank)
    lane = lax.broadcasted_iota(jnp.int32, first.shape, 1)
    for start in range(SUBLANES, rows, SUBLANES):
        shift = jnp.where(right, start, width - start)
        turned = pltpu.roll(lines(start), shift, 1)
        above = lane < shift
        high = high + jnp.where(above, turned, 0.0)
        low = low + jnp.where(above, 0.0, turned)
    total = jnp.concatenate([low, high], axis=1)
    line = lax.broadcasted_iota(jnp.int32, total.shape, 0)
    bit = 1
    while bit < SUBLANES:
        turned = pltpu.roll(total, jnp.where(right, bit, 2 * width - bit), 1)
        total = jnp.where((line & bit) == bit, turned, total)
        bit *= 2
    sums = jnp.sum(total.reshape(group_count, SUBLANES, 2 * width), axis=1)
    return lax.select(right, pltpu.roll(sums, 1, 1), sums)


def turned_columns(block, reverse):
    rows = block.shape[0]
    row = lax.broadcasted_iota(jnp.int32, (rows, rows), 0)
    column = lax.broadcasted_iota(jnp.int32, (rows, rows), 1)
    place = lax.select(reverse, rows - 1 - column, column)
    order = jnp.where(row == place, 1.0, 0.0).astype(block.dtype)
    moved_block = lax.dot_general(block, order, (((0,), (0,)), ((), ())), preferred_element_type=jnp.float32)
    return moved_block.astype(block.dtype)


def diagonal_kernel(query_hbm, keys_hbm, values_hbm, cotangent_hbm, out_ref, left, right, sems):
    odd = is_odd()
    half = out_ref.shape[1]
    low, high = pl.ds(0, half), pl.ds(half, half)
    copies = launch(
        odd,
        [
            (1, keys_hbm.at[:, low], left),
            (1, values_hbm.at[:, low], right),
            (0, cotangent_hbm.at[:, high], left),
            (0, query_hbm.at[:, high], right),
        ],
        sems,
        0,
    )
    finish(odd, copies)
    out_ref[...] = product(left[...], right[...])


def products_kernel(query_ref, keys_ref, values_ref, cotangent_ref, sent_ref, near_ref, across_ref):
    odd = is_odd()
    prod = product(keys_ref[...], values_ref[...])
    grad = product(cotangent_ref[...], query_ref[...])
    near_ref[...] = lax.select(odd, prod, grad)
    across_ref[...] = lax.select(odd, grad, prod)


def tiles_kernel(rows, taps_ref, ready_tiles, late_tiles):
    odd = is_odd()
    group_count, width = taps_ref.shape
    for group in range(group_count):
        row = taps_ref[group : group + 1, :].astype(jnp.float32)
        spread = jnp.concatenate(
            [jnp.zeros((SUBLANES, rows), jnp.float32), jnp.broadcast_to(row, (SUBLANES, width))],
            axis=1,
        )
        spread = pltpu.roll(spread, 0, 1, stride=1, stride_axis=0)
        bands = [
            pltpu.roll(spread, start, 1)[:, rows:] if start else spread[:, rows:]
            for start in range(0, rows, SUBLANES)
        ]
        band = jnp.concatenate(bands, axis=0)
        turned = [band[:, start : start + rows].T for start in range(0, width, rows)]
        turned = jnp.concatenate(turned, axis=1)
        ready_tiles[group] = lax.select(odd, band, turned).astype(jnp.bfloat16)
        late_tiles[group] = lax.select(odd, turned, band).astype(jnp.bfloat16)


def own_kernel(
    rows, ready_tiles, late_tiles, near_ref, across_ref, diagonal_ref, sum_ref, late_ref, ready_ref,
    near_turned, across_turned,
):
    odd = is_odd()
    group_count, width = sum_ref.shape
    group_width = near_ref.shape[1] // group_count
    half = group_count // 2
    blank = jnp.zeros((rows, rows), jnp.float32)
    for group in range(group_count):
        columns = columns_of(group, group_width)
        late_ref[:, columns] = DOT(late_tiles[group, :, :rows], near_ref[:, columns])
        ready_ref[:, columns] = DOT(ready_tiles[group, :, :rows], across_ref[:, columns])
    for group in range(group_count):
        columns, places = columns_of(group, group_width), columns_of(group, rows)
        near_turned[:, places] = turned_columns(near_ref[:, columns], odd)
        across_turned[:, places] = turned_columns(across_ref[:, columns], jnp.logical_not(odd))
    middles = []
    for group in range(half):
        low, high = columns_of(group, group_width), columns_of(group + half, group_width)
        arrived = diagonal_ref[:, low]
        own = lax.select(odd, near_ref[:, high], near_ref[:, low])
        middles.append(DOT_ROWS(lax.select(odd, own, arrived), lax.select(odd, arrived, own)))
        tile = lax.select(
            odd, ready_tiles[group + half, :, rows : 2 * rows], ready_tiles[group, :, rows : 2 * rows]
        )
        more = DOT(tile, arrived)
        ready_ref[:, low] += lax.select(odd, blank, more)
        ready_ref[:, high] += lax.select(odd, more, blank)
    sums = []
    for group in range(group_count):
        columns = columns_of(group, group_width)
        near, across = near_ref[:, columns], across_ref[:, columns]
        outer = DOT_ROWS(lax.select(odd, near, across), lax.select(odd, across, near))
        if group < half:
            middle = lax.select(odd, blank, middles[group])
        else:
            middle = lax.select(odd, middles[group - half], blank)
        sums.append(skewed_sum(jnp.concatenate([outer, middle, blank], axis=1), rows)[:, : 2 * rows])
    sums = jnp.concatenate(sums, axis=0)
    sum_ref[...] = jnp.concatenate([sums, jnp.zeros((group_count, width - 2 * rows), jnp.float32)], axis=1)


def two_kernel(rows, sum_ref, turned_ref, two_ref, out_ref, outer_ref):
    odd = is_odd()
    group_count, width = out_ref.shape
    group_width = two_ref.shape[1] // group_count
    for group in range(group_count):
        columns = columns_of(group, group_width)
        outer_ref[group] = DOT(two_ref[:, columns], turned_ref[:, columns_of(group, rows)])
    sums = skewed_pairs(outer_ref, odd)
    out_ref[...] = sum_ref[...] + jnp.concatenate(
        [jnp.zeros((group_count, width - 2 * rows), jnp.float32), sums], axis=1
    )


def cross_kernel(rows, turned_ref, swap_ref, out_ref, outer_ref):
    odd = is_odd()
    group_count, width = out_ref.shape
    group_width = swap_ref.shape[1] // group_count
    for group in range(group_count):
        columns = columns_of(group, group_width)
        outer_ref[group] = DOT(swap_ref[:, columns], turned_ref[:, columns_of(group, rows)])
    sums = skewed_pairs(outer_ref, jnp.logical_not(odd))
    out_ref[...] = jnp.concatenate([sums, jnp.zeros((group_count, width - 2 * rows), jnp.float32)], axis=1)


def pair_kernel(factor, sum_ref, other_ref, cross_ref, rest_ref, out_ref):
    out_ref[...] = (sum_ref[...] + other_ref[...] + cross_ref[...]) * factor


def add_kernel(*refs):
    *terms, _, out_ref = refs
    out_ref[...] = functools.reduce(jnp.add, [ref[...] for ref in terms])


def forward_kernel(far_ref, rest_ref, out_ref):
    half = out_ref.shape[1]
    out_ref[...] = lax.select(is_odd(), far_ref[:, half:], far_ref[:, :half])


def ready_kernel(
    tiles_ref, ready_ref, two_ref, query_ref, keys_ref, values_ref, sum_ref, rest_ref, one, other
):
    odd = is_odd()
    group_count, rows, _ = tiles_ref.shape
    group_width = two_ref.shape[1] // group_count
    half = group_count // 2
    for group in range(half):
        low, high = columns_of(group, group_width), columns_of(group + half, group_width)
        first = ready_ref[:, low] + DOT(tiles_ref[group, :, 2 * rows :], two_ref[:, low])
        second = ready_ref[:, high] + DOT(tiles_ref[group + half, :, 2 * rows :], two_ref[:, high])
        rest_ref[:, low] = lax.select(odd, first, second)
        known = lax.select(odd, second, first)
        one[:, low] = scaled(known, lax.select(odd, values_ref[:, high], query_ref[:, low]))
        other[:, low] = scaled(known, keys_ref[:, high])


def known_kernel(tiles_ref, late_ref, swap_ref, far_ref, query_ref, keys_ref, values_ref, one, other):
    odd = is_odd()
    group_count, rows, _ = tiles_ref.shape
    group_width = far_ref.shape[1] // group_count
    for group in range(group_count):
        columns = columns_of(group, group_width)
        arrived = jnp.concatenate([swap_ref[:, columns], far_ref[:, columns]], axis=0)
        late = late_ref[:, columns] + DOT(tiles_ref[group, :, rows:], arrived)
        one[:, columns] = scaled(late, lax.select(odd, query_ref[:, columns], values_ref[:, columns]))
        other[:, columns] = scaled(late, keys_ref[:, columns])


def last_kernel(
    tiles_ref, rest_ref, forwarded_ref, query_ref, keys_ref, values_ref,
    ready_one, ready_other, known_one, known_other,
    gated_out, key_out, value_out, mark_ref, one, other, sems,
):
    odd = is_odd()
    mark_ref[...] = jnp.zeros_like(mark_ref)
    group_count, rows, _ = tiles_ref.shape
    half = group_count // 2
    group_width = forwarded_ref.shape[1] // half
    step = max(1, half // PARTS)
    low_half, high_half = pl.ds(0, half * group_width), pl.ds(half * group_width, half * group_width)
    copies = launch(
        odd,
        [
            (0, known_one, key_out),
            (0, known_other, value_out),
            (0, ready_one, gated_out.at[:, low_half]),
            (1, known_one, gated_out),
            (1, ready_one, key_out.at[:, high_half]),
            (1, ready_other, value_out.at[:, high_half]),
        ],
        sems,
        0,
    )
    for group in range(half):
        low, high = columns_of(group, group_width), columns_of(group + half, group_width)
        tile = lax.select(
            odd, tiles_ref[group, :, rows : 2 * rows], tiles_ref[group + half, :, rows : 2 * rows]
        )
        ready = rest_ref[:, low] + DOT(tile, forwarded_ref[:, low])
        one[:, low] = scaled(ready, lax.select(odd, values_ref[:, low], query_ref[:, high]))
        other[:, low] = scaled(ready, keys_ref[:, low])
        if (group + 1) % step == 0:
            start, size = (group + 1 - step) * group_width, step * group_width
            part, place = pl.ds(start, size), pl.ds(start + half * group_width, size)
            moves = [
                (0, one.at[:, part], gated_out.at[:, place]),
                (1, one.at[:, part], key_out.at[:, part]),
                (1, other.at[:, part], value_out.at[:, part]),
            ]
            copies += launch(odd, moves, sems, len(copies))
    finish(odd, copies)


def shards(query, keys, values, cotangent, filter_taps):
    rows, local_width = query.shape
    group_count, taps = filter_taps.shape
    group_width = local_width // group_count
    half_width = local_width // 2
    factor = 1.0 / math.sqrt(rows * lax.axis_size("ctx") * group_width)

    def call(kernel, name, flops=10**6, **options):
        return pl.pallas_call(
            kernel,
            compiler_params=pltpu.CompilerParams(vmem_limit_bytes=VMEM_LIMIT),
            cost_estimate=pl.CostEstimate(flops=flops, bytes_accessed=10**5, transcendentals=0),
            name=name,
            **options,
        )

    bf16, f32 = jnp.bfloat16, jnp.float32
    block, half_block = pltpu.VMEM((rows, local_width), bf16), pltpu.VMEM((rows, half_width), bf16)
    wide, half_wide = pltpu.VMEM((rows, local_width), f32), pltpu.VMEM((rows, half_width), f32)
    tiles, sums = pltpu.VMEM((group_count, rows, taps), bf16), pltpu.VMEM((group_count, taps), f32)
    turned = pltpu.VMEM((group_width, group_count * rows), bf16)
    outs = [jax.ShapeDtypeStruct((rows, local_width), bf16)] * 3

    sent = call(
        diagonal_kernel,
        "diagonal",
        in_specs=[ANYWHERE] * 4,
        out_specs=WHOLE,
        out_shape=half_block,
        scratch_shapes=[half_block] * 2 + [pltpu.SemaphoreType.DMA((4,))],
    )(*in_hbm(query, keys, values, cotangent))
    diagonal = moved(sent, "ctx", (-1, 1))
    near, across = call(
        products_kernel,
        "products",
        in_specs=[WHOLE] * 4 + [ANYWHERE],
        out_specs=[WHOLE] * 2,
        out_shape=[block] * 2,
    )(*in_vmem(query, keys, values, cotangent), sent)
    two = moved(across, "ctx", (2, -2))
    far = moved(near, "ctx", (-2, 2))
    swap = moved(across, "ctx", (1, -1))

    ready_tiles, late_tiles = call(
        functools.partial(tiles_kernel, rows),
        "tiles",
        in_specs=[WHOLE],
        out_specs=[WHOLE] * 2,
        out_shape=[tiles] * 2,
    )(*in_vmem(filter_taps))
    partial, late, ready, near_turned, across_turned = call(
        functools.partial(own_kernel, rows),
        "own",
        flops=4 * 10**9,
        in_specs=[WHOLE] * 5,
        out_specs=[WHOLE] * 5,
        out_shape=[sums, wide, wide, turned, turned],
    )(*in_vmem(ready_tiles, late_tiles, near, across, diagonal))

    partial = call(
        functools.partial(two_kernel, rows),
        "two",
        in_specs=[WHOLE] * 3,
        out_specs=WHOLE,
        out_shape=sums,
        scratch_shapes=[pltpu.VMEM((group_count, rows, rows), f32)],
    )(*in_vmem(partial, near_turned, two))
    other = moved(partial, "ctx", (1, -1))

    rest, ready_one, ready_other = call(
        ready_kernel,
        "ready",
        in_specs=[WHOLE] * 6 + [ANYWHERE],
        out_specs=[WHOLE] * 3,
        out_shape=[half_wide, half_block, half_block],
    )(*in_vmem(ready_tiles, ready, two, query, keys, values), partial)

    forwarded = call(
        forward_kernel,
        "forward",
        in_specs=[WHOLE, ANYWHERE],
        out_specs=WHOLE,
        out_shape=half_block,
    )(*in_vmem(far), rest)
    forwarded = moved(forwarded, "ctx", (1, -1))

    cross = call(
        functools.partial(cross_kernel, rows),
        "cross",
        in_specs=[WHOLE] * 2,
        out_specs=WHOLE,
        out_shape=sums,
        scratch_shapes=[pltpu.VMEM((group_count, rows, rows), f32)],
    )(*in_vmem(across_turned, swap))
    pair_sum = call(
        functools.partial(pair_kernel, factor),
        "pair",
        in_specs=[WHOLE] * 3 + [ANYWHERE],
        out_specs=WHOLE,
        out_shape=sums,
    )(*in_vmem(partial, other, cross), rest)

    known_one, known_other = call(
        known_kernel,
        "known",
        flops=4 * 10**9,
        in_specs=[WHOLE] * 7,
        out_specs=[WHOLE] * 2,
        out_shape=[block] * 2,
    )(*in_vmem(late_tiles, late, swap, far, query, keys, values))

    def add(*terms, out_shape=sums, after=known_one):
        return call(
            add_kernel,
            "add",
            in_specs=[WHOLE] * len(terms) + [ANYWHERE],
            out_specs=WHOLE,
            out_shape=out_shape,
        )(*in_vmem(*terms), after)

    terms = sum_terms(pair_sum, "ctx", add)
    gated, key_grad, value_grad, mark = call(
        last_kernel,
        "last",
        in_specs=[WHOLE] * 10,
        out_specs=[ANYWHERE] * 3 + [WHOLE],
        out_shape=outs + [pltpu.VMEM((SUBLANES, group_width), f32)],
        scratch_shapes=[half_block] * 2 + [pltpu.SemaphoreType.DMA((6 + 3 * PARTS,))],
    )(
        *in_vmem(ready_tiles, rest, forwarded, query, keys, values),
        *in_vmem(ready_one, ready_other, known_one, known_other),
    )
    whole_sums = jax.ShapeDtypeStruct((group_count, taps), f32)
    return (gated, key_grad, value_grad, add(*terms, out_shape=whole_sums, after=mark))


def solution(mesh):
    in_specs = (P("ctx", "grp"), P("ctx", "grp"), P("ctx", "grp"), P("ctx", "grp"), P("grp", None))
    out_specs = (P("ctx", "grp"), P("ctx", "grp"), P("ctx", "grp"), P("grp", None))
    return jax.shard_map(shards, mesh=mesh, in_specs=in_specs, out_specs=out_specs, check_vma=False)
```

```python
import functools
import math

import jax
import jax.numpy as jnp
from jax import lax
from jax.experimental import pallas as pl
from jax.experimental.pallas import tpu as pltpu
from jax.sharding import PartitionSpec as P

SUBLANES = 8
PARTS = 2
VMEM_LIMIT = 16 * 1024 * 1024
WHOLE = pl.BlockSpec(memory_space=pltpu.VMEM)
ANYWHERE = pl.BlockSpec(memory_space=pl.ANY)
DOT_ROWS = functools.partial(
    lax.dot_general,
    dimension_numbers=(((1,), (1,)), ((), ())),
    preferred_element_type=jnp.float32,
)
DOT = functools.partial(jnp.dot, preferred_element_type=jnp.float32)


def in_vmem(*arrays):
    return [pltpu.with_memory_space_constraint(array, pltpu.VMEM) for array in arrays]


def in_hbm(*arrays):
    return [pltpu.with_memory_space_constraint(array, pltpu.HBM) for array in arrays]


def moved(block, axis, distances):
    size = lax.axis_size(axis)
    route = [(i, i + distances[i % 2]) for i in range(size)]
    return lax.ppermute(block, axis, [pair for pair in route if 0 <= pair[1] < size])


def sum_terms(pair_sum, axis, add):
    size = lax.axis_size(axis)
    if size & (size - 1):
        even = lax.axis_index(axis) % 2 == 0
        return [lax.psum(jnp.where(even, pair_sum, 0.0), axis)]
    terms = [pair_sum]
    stride = 2
    while stride < size:
        own = terms[0] if len(terms) == 1 else add(*terms)
        members = 4 if 4 * stride <= size else 2
        rounds = ((2, 3, 1, 0), (3, 2, 0, 1), (1, 0, 3, 2)) if members == 4 else ((1, 0),)
        terms = [own]
        for targets in rounds:
            places = [(i, i // stride % members) for i in range(size)]
            route = [(i, i + (targets[place] - place) * stride) for i, place in places]
            terms.append(lax.ppermute(own, axis, route))
        stride *= members
    return terms


def is_odd():
    return lax.rem(lax.axis_index("ctx"), 2) == 1


def product(left, right):
    return (left.astype(jnp.float32) * right.astype(jnp.float32)).astype(jnp.bfloat16)


def scaled(value, factor):
    return (value * factor.astype(jnp.float32)).astype(jnp.bfloat16)


def columns_of(group, width):
    return slice(group * width, (group + 1) * width)


def launch(odd, moves, sems, used):
    copies = [(*move, sems.at[used + place]) for place, move in enumerate(moves)]
    for parity, source, target, sem in copies:
        @pl.when(odd if parity else jnp.logical_not(odd))
        def _():
            pltpu.make_async_copy(source, target, sem).start()
    return copies


def finish(odd, copies):
    for parity, source, target, sem in copies:
        @pl.when(odd if parity else jnp.logical_not(odd))
        def _():
            pltpu.make_async_copy(source, target, sem).wait()


def lines_summed(total):
    line = lax.broadcasted_iota(jnp.int32, total.shape, 0)
    bit = 1
    while bit < SUBLANES:
        total = jnp.where((line & bit) == bit, pltpu.roll(total, total.shape[1] - bit, 1), total)
        bit *= 2
    return jnp.sum(total, axis=0, keepdims=True)


def skewed_sum(outer, rows):
    width = outer.shape[1]
    total = outer[:SUBLANES]
    for start in range(SUBLANES, rows, SUBLANES):
        total = total + pltpu.roll(outer[start : start + SUBLANES], width - start, 1)
    return lines_summed(total)


def skewed_pair(outer, rows):
    width = outer.shape[1]
    lane = lax.broadcasted_iota(jnp.int32, (SUBLANES, width), 1)
    high = outer[:SUBLANES]
    low = jnp.zeros_like(high)
    for start in range(SUBLANES, rows, SUBLANES):
        turned = pltpu.roll(outer[start : start + SUBLANES], width - start, 1)
        above = lane < width - start
        high = high + jnp.where(above, turned, 0.0)
        low = low + jnp.where(above, 0.0, turned)
    return lines_summed(jnp.concatenate([low, high], axis=1))


def diagonal_kernel(query_hbm, keys_hbm, values_hbm, cotangent_hbm, out_ref, left, right, sems):
    odd = is_odd()
    half = out_ref.shape[1]
    low, high = pl.ds(0, half), pl.ds(half, half)
    copies = launch(
        odd,
        [
            (1, keys_hbm.at[:, low], left),
            (1, values_hbm.at[:, low], right),
            (0, cotangent_hbm.at[:, high], left),
            (0, query_hbm.at[:, high], right),
        ],
        sems,
        0,
    )
    finish(odd, copies)
    out_ref[...] = product(left[...], right[...])


def products_kernel(query_ref, keys_ref, values_ref, cotangent_ref, sent_ref, near_ref, across_ref):
    odd = is_odd()
    prod = product(keys_ref[...], values_ref[...])
    grad = product(cotangent_ref[...], query_ref[...])
    near_ref[...] = lax.select(odd, prod, grad)
    across_ref[...] = lax.select(odd, grad, prod)


def tiles_kernel(rows, taps_ref, ready_tiles, late_tiles):
    odd = is_odd()
    group_count, width = taps_ref.shape
    for group in range(group_count):
        row = taps_ref[group : group + 1, :].astype(jnp.float32)
        spread = jnp.concatenate(
            [jnp.zeros((SUBLANES, rows), jnp.float32), jnp.broadcast_to(row, (SUBLANES, width))],
            axis=1,
        )
        spread = pltpu.roll(spread, 0, 1, stride=1, stride_axis=0)
        bands = [
            pltpu.roll(spread, start, 1)[:, rows:] if start else spread[:, rows:]
            for start in range(0, rows, SUBLANES)
        ]
        band = jnp.concatenate(bands, axis=0)
        turned = [band[:, start : start + rows].T for start in range(0, width, rows)]
        turned = jnp.concatenate(turned, axis=1)
        ready_tiles[group] = lax.select(odd, band, turned).astype(jnp.bfloat16)
        late_tiles[group] = lax.select(odd, turned, band).astype(jnp.bfloat16)


def own_kernel(
    rows, ready_tiles, late_tiles, near_ref, across_ref, diagonal_ref, sum_ref, late_ref, ready_ref
):
    odd = is_odd()
    group_count, width = sum_ref.shape
    group_width = near_ref.shape[1] // group_count
    half = group_count // 2
    blank = jnp.zeros((rows, rows), jnp.float32)
    for group in range(group_count):
        columns = columns_of(group, group_width)
        late_ref[:, columns] = DOT(late_tiles[group, :, :rows], near_ref[:, columns])
        ready_ref[:, columns] = DOT(ready_tiles[group, :, :rows], across_ref[:, columns])
    middles = []
    for group in range(half):
        low, high = columns_of(group, group_width), columns_of(group + half, group_width)
        arrived = diagonal_ref[:, low]
        own = lax.select(odd, near_ref[:, high], near_ref[:, low])
        middles.append(DOT_ROWS(lax.select(odd, own, arrived), lax.select(odd, arrived, own)))
        tile = lax.select(
            odd, ready_tiles[group + half, :, rows : 2 * rows], ready_tiles[group, :, rows : 2 * rows]
        )
        more = DOT(tile, arrived)
        ready_ref[:, low] += lax.select(odd, blank, more)
        ready_ref[:, high] += lax.select(odd, more, blank)
    sums = []
    for group in range(group_count):
        columns = columns_of(group, group_width)
        near, across = near_ref[:, columns], across_ref[:, columns]
        outer = DOT_ROWS(lax.select(odd, near, across), lax.select(odd, across, near))
        if group < half:
            middle = lax.select(odd, blank, middles[group])
        else:
            middle = lax.select(odd, middles[group - half], blank)
        sums.append(skewed_sum(jnp.concatenate([outer, middle, blank], axis=1), rows)[:, : 2 * rows])
    sums = jnp.concatenate(sums, axis=0)
    sum_ref[...] = jnp.concatenate([sums, jnp.zeros((group_count, width - 2 * rows), jnp.float32)], axis=1)


def two_kernel(rows, sum_ref, near_ref, two_ref, out_ref):
    odd = is_odd()
    group_count, width = out_ref.shape
    group_width = near_ref.shape[1] // group_count
    sums = []
    for group in range(group_count):
        columns = columns_of(group, group_width)
        near, two = near_ref[:, columns], two_ref[:, columns]
        outer = DOT_ROWS(lax.select(odd, near, two), lax.select(odd, two, near))
        sums.append(skewed_pair(outer, rows))
    sums = jnp.concatenate(sums, axis=0)
    out_ref[...] = sum_ref[...] + jnp.concatenate(
        [jnp.zeros((group_count, width - 2 * rows), jnp.float32), sums], axis=1
    )


def cross_kernel(rows, across_ref, swap_ref, out_ref):
    odd = is_odd()
    group_count, width = out_ref.shape
    group_width = across_ref.shape[1] // group_count
    sums = []
    for group in range(group_count):
        columns = columns_of(group, group_width)
        across, swap = across_ref[:, columns], swap_ref[:, columns]
        outer = DOT_ROWS(lax.select(odd, swap, across), lax.select(odd, across, swap))
        sums.append(skewed_pair(outer, rows))
    sums = jnp.concatenate(sums, axis=0)
    out_ref[...] = jnp.concatenate([sums, jnp.zeros((group_count, width - 2 * rows), jnp.float32)], axis=1)


def pair_kernel(factor, sum_ref, other_ref, cross_ref, rest_ref, out_ref):
    out_ref[...] = (sum_ref[...] + other_ref[...] + cross_ref[...]) * factor


def add_kernel(*refs):
    *terms, _, out_ref = refs
    out_ref[...] = functools.reduce(jnp.add, [ref[...] for ref in terms])


def forward_kernel(far_ref, rest_ref, out_ref):
    half = out_ref.shape[1]
    out_ref[...] = lax.select(is_odd(), far_ref[:, half:], far_ref[:, :half])


def ready_kernel(
    tiles_ref, ready_ref, two_ref, query_ref, keys_ref, values_ref, sum_ref, rest_ref, one, other
):
    odd = is_odd()
    group_count, rows, _ = tiles_ref.shape
    group_width = two_ref.shape[1] // group_count
    half = group_count // 2
    for group in range(half):
        low, high = columns_of(group, group_width), columns_of(group + half, group_width)
        first = ready_ref[:, low] + DOT(tiles_ref[group, :, 2 * rows :], two_ref[:, low])
        second = ready_ref[:, high] + DOT(tiles_ref[group + half, :, 2 * rows :], two_ref[:, high])
        rest_ref[:, low] = lax.select(odd, first, second)
        known = lax.select(odd, second, first)
        one[:, low] = scaled(known, lax.select(odd, values_ref[:, high], query_ref[:, low]))
        other[:, low] = scaled(known, keys_ref[:, high])


def known_kernel(tiles_ref, late_ref, swap_ref, far_ref, query_ref, keys_ref, values_ref, one, other):
    odd = is_odd()
    group_count, rows, _ = tiles_ref.shape
    group_width = far_ref.shape[1] // group_count
    for group in range(group_count):
        columns = columns_of(group, group_width)
        arrived = jnp.concatenate([swap_ref[:, columns], far_ref[:, columns]], axis=0)
        late = late_ref[:, columns] + DOT(tiles_ref[group, :, rows:], arrived)
        one[:, columns] = scaled(late, lax.select(odd, query_ref[:, columns], values_ref[:, columns]))
        other[:, columns] = scaled(late, keys_ref[:, columns])


def last_kernel(
    tiles_ref, rest_ref, forwarded_ref, query_ref, keys_ref, values_ref,
    ready_one, ready_other, known_one, known_other,
    gated_out, key_out, value_out, mark_ref, one, other, sems,
):
    odd = is_odd()
    mark_ref[...] = jnp.zeros_like(mark_ref)
    group_count, rows, _ = tiles_ref.shape
    half = group_count // 2
    group_width = forwarded_ref.shape[1] // half
    step = max(1, half // PARTS)
    low_half, high_half = pl.ds(0, half * group_width), pl.ds(half * group_width, half * group_width)
    copies = launch(
        odd,
        [
            (0, known_one, key_out),
            (0, known_other, value_out),
            (0, ready_one, gated_out.at[:, low_half]),
            (1, known_one, gated_out),
            (1, ready_one, key_out.at[:, high_half]),
            (1, ready_other, value_out.at[:, high_half]),
        ],
        sems,
        0,
    )
    for group in range(half):
        low, high = columns_of(group, group_width), columns_of(group + half, group_width)
        tile = lax.select(
            odd, tiles_ref[group, :, rows : 2 * rows], tiles_ref[group + half, :, rows : 2 * rows]
        )
        ready = rest_ref[:, low] + DOT(tile, forwarded_ref[:, low])
        one[:, low] = scaled(ready, lax.select(odd, values_ref[:, low], query_ref[:, high]))
        other[:, low] = scaled(ready, keys_ref[:, low])
        if (group + 1) % step == 0:
            start, size = (group + 1 - step) * group_width, step * group_width
            part, place = pl.ds(start, size), pl.ds(start + half * group_width, size)
            moves = [
                (0, one.at[:, part], gated_out.at[:, place]),
                (1, one.at[:, part], key_out.at[:, part]),
                (1, other.at[:, part], value_out.at[:, part]),
            ]
            copies += launch(odd, moves, sems, len(copies))
    finish(odd, copies)


def shards(query, keys, values, cotangent, filter_taps):
    rows, local_width = query.shape
    group_count, taps = filter_taps.shape
    group_width = local_width // group_count
    half_width = local_width // 2
    factor = 1.0 / math.sqrt(rows * lax.axis_size("ctx") * group_width)

    def call(kernel, name, flops=10**6, **options):
        return pl.pallas_call(
            kernel,
            compiler_params=pltpu.CompilerParams(vmem_limit_bytes=VMEM_LIMIT),
            cost_estimate=pl.CostEstimate(flops=flops, bytes_accessed=10**5, transcendentals=0),
            name=name,
            **options,
        )

    bf16, f32 = jnp.bfloat16, jnp.float32
    block, half_block = pltpu.VMEM((rows, local_width), bf16), pltpu.VMEM((rows, half_width), bf16)
    wide, half_wide = pltpu.VMEM((rows, local_width), f32), pltpu.VMEM((rows, half_width), f32)
    tiles, sums = pltpu.VMEM((group_count, rows, taps), bf16), pltpu.VMEM((group_count, taps), f32)
    outs = [jax.ShapeDtypeStruct((rows, local_width), bf16)] * 3

    sent = call(
        diagonal_kernel,
        "diagonal",
        in_specs=[ANYWHERE] * 4,
        out_specs=WHOLE,
        out_shape=half_block,
        scratch_shapes=[half_block] * 2 + [pltpu.SemaphoreType.DMA((4,))],
    )(*in_hbm(query, keys, values, cotangent))
    diagonal = moved(sent, "ctx", (-1, 1))
    near, across = call(
        products_kernel,
        "products",
        in_specs=[WHOLE] * 4 + [ANYWHERE],
        out_specs=[WHOLE] * 2,
        out_shape=[block] * 2,
    )(*in_vmem(query, keys, values, cotangent), sent)
    two = moved(across, "ctx", (2, -2))
    far = moved(near, "ctx", (-2, 2))
    swap = moved(across, "ctx", (1, -1))

    ready_tiles, late_tiles = call(
        functools.partial(tiles_kernel, rows),
        "tiles",
        in_specs=[WHOLE],
        out_specs=[WHOLE] * 2,
        out_shape=[tiles] * 2,
    )(*in_vmem(filter_taps))
    partial, late, ready = call(
        functools.partial(own_kernel, rows),
        "own",
        flops=4 * 10**9,
        in_specs=[WHOLE] * 5,
        out_specs=[WHOLE] * 3,
        out_shape=[sums, wide, wide],
    )(*in_vmem(ready_tiles, late_tiles, near, across, diagonal))

    partial = call(
        functools.partial(two_kernel, rows),
        "two",
        in_specs=[WHOLE] * 3,
        out_specs=WHOLE,
        out_shape=sums,
    )(*in_vmem(partial, near, two))
    other = moved(partial, "ctx", (1, -1))

    rest, ready_one, ready_other = call(
        ready_kernel,
        "ready",
        in_specs=[WHOLE] * 6 + [ANYWHERE],
        out_specs=[WHOLE] * 3,
        out_shape=[half_wide, half_block, half_block],
    )(*in_vmem(ready_tiles, ready, two, query, keys, values), partial)

    forwarded = call(
        forward_kernel,
        "forward",
        in_specs=[WHOLE, ANYWHERE],
        out_specs=WHOLE,
        out_shape=half_block,
    )(*in_vmem(far), rest)
    forwarded = moved(forwarded, "ctx", (1, -1))

    cross = call(
        functools.partial(cross_kernel, rows),
        "cross",
        in_specs=[WHOLE] * 2,
        out_specs=WHOLE,
        out_shape=sums,
    )(*in_vmem(across, swap))
    pair_sum = call(
        functools.partial(pair_kernel, factor),
        "pair",
        in_specs=[WHOLE] * 3 + [ANYWHERE],
        out_specs=WHOLE,
        out_shape=sums,
    )(*in_vmem(partial, other, cross), rest)

    known_one, known_other = call(
        known_kernel,
        "known",
        flops=4 * 10**9,
        in_specs=[WHOLE] * 7,
        out_specs=[WHOLE] * 2,
        out_shape=[block] * 2,
    )(*in_vmem(late_tiles, late, swap, far, query, keys, values))

    def add(*terms, out_shape=sums, after=known_one):
        return call(
            add_kernel,
            "add",
            in_specs=[WHOLE] * len(terms) + [ANYWHERE],
            out_specs=WHOLE,
            out_shape=out_shape,
        )(*in_vmem(*terms), after)

    terms = sum_terms(pair_sum, "ctx", add)
    gated, key_grad, value_grad, mark = call(
        last_kernel,
        "last",
        in_specs=[WHOLE] * 10,
        out_specs=[ANYWHERE] * 3 + [WHOLE],
        out_shape=outs + [pltpu.VMEM((SUBLANES, group_width), f32)],
        scratch_shapes=[half_block] * 2 + [pltpu.SemaphoreType.DMA((6 + 3 * PARTS,))],
    )(
        *in_vmem(ready_tiles, rest, forwarded, query, keys, values),
        *in_vmem(ready_one, ready_other, known_one, known_other),
    )
    whole_sums = jax.ShapeDtypeStruct((group_count, taps), f32)
    return (gated, key_grad, value_grad, add(*terms, out_shape=whole_sums, after=mark))


def solution(mesh):
    in_specs = (P("ctx", "grp"), P("ctx", "grp"), P("ctx", "grp"), P("ctx", "grp"), P("grp", None))
    out_specs = (P("ctx", "grp"), P("ctx", "grp"), P("ctx", "grp"), P("grp", None))
    return jax.shard_map(shards, mesh=mesh, in_specs=in_specs, out_specs=out_specs, check_vma=False)
```

```python
import functools
import math

import jax
import jax.numpy as jnp
from jax import lax
from jax.experimental import pallas as pl
from jax.experimental.pallas import tpu as pltpu
from jax.sharding import PartitionSpec as P

SUBLANES = 8
PARTS = 2
VMEM_LIMIT = 16 * 1024 * 1024
WHOLE = pl.BlockSpec(memory_space=pltpu.VMEM)
ANYWHERE = pl.BlockSpec(memory_space=pl.ANY)
DOT_ROWS = functools.partial(
    lax.dot_general,
    dimension_numbers=(((1,), (1,)), ((), ())),
    preferred_element_type=jnp.float32,
)
DOT = functools.partial(jnp.dot, preferred_element_type=jnp.float32)


def in_vmem(*arrays):
    return [pltpu.with_memory_space_constraint(array, pltpu.VMEM) for array in arrays]


def in_hbm(*arrays):
    return [pltpu.with_memory_space_constraint(array, pltpu.HBM) for array in arrays]


def moved(block, axis, distances):
    size = lax.axis_size(axis)
    route = [(i, i + distances[i % 2]) for i in range(size)]
    return lax.ppermute(block, axis, [pair for pair in route if 0 <= pair[1] < size])


def sum_terms(pair_sum, axis, add):
    size = lax.axis_size(axis)
    if size & (size - 1):
        even = lax.axis_index(axis) % 2 == 0
        return [lax.psum(jnp.where(even, pair_sum, 0.0), axis)]
    terms = [pair_sum]
    stride = 2
    while stride < size:
        own = terms[0] if len(terms) == 1 else add(*terms)
        members = 4 if 4 * stride <= size else 2
        rounds = ((2, 3, 1, 0), (3, 2, 0, 1), (1, 0, 3, 2)) if members == 4 else ((1, 0),)
        terms = [own]
        for targets in rounds:
            places = [(i, i // stride % members) for i in range(size)]
            route = [(i, i + (targets[place] - place) * stride) for i, place in places]
            terms.append(lax.ppermute(own, axis, route))
        stride *= members
    return terms


def is_odd():
    return lax.rem(lax.axis_index("ctx"), 2) == 1


def product(left, right):
    return (left.astype(jnp.float32) * right.astype(jnp.float32)).astype(jnp.bfloat16)


def scaled(value, factor):
    return (value * factor.astype(jnp.float32)).astype(jnp.bfloat16)


def columns_of(group, width):
    return slice(group * width, (group + 1) * width)


def launch(odd, moves, sems, used):
    copies = [(*move, sems.at[used + place]) for place, move in enumerate(moves)]
    for parity, source, target, sem in copies:
        @pl.when(odd if parity else jnp.logical_not(odd))
        def _():
            pltpu.make_async_copy(source, target, sem).start()
    return copies


def finish(odd, copies):
    for parity, source, target, sem in copies:
        @pl.when(odd if parity else jnp.logical_not(odd))
        def _():
            pltpu.make_async_copy(source, target, sem).wait()


def lines_summed(total):
    line = lax.broadcasted_iota(jnp.int32, total.shape, 0)
    bit = 1
    while bit < SUBLANES:
        total = jnp.where((line & bit) == bit, pltpu.roll(total, total.shape[1] - bit, 1), total)
        bit *= 2
    return jnp.sum(total, axis=0, keepdims=True)


def skewed_sum(outer, rows):
    width = outer.shape[1]
    total = outer[:SUBLANES]
    for start in range(SUBLANES, rows, SUBLANES):
        total = total + pltpu.roll(outer[start : start + SUBLANES], width - start, 1)
    return lines_summed(total)


def skewed_pairs(outer_ref, right):
    group_count, rows, width = outer_ref.shape

    def lines(start):
        return outer_ref[:, start : start + SUBLANES, :].reshape(group_count * SUBLANES, width)

    first = lines(0)
    blank = jnp.zeros_like(first)
    high = lax.select(right, blank, first)
    low = lax.select(right, first, blank)
    lane = lax.broadcasted_iota(jnp.int32, first.shape, 1)
    for start in range(SUBLANES, rows, SUBLANES):
        shift = jnp.where(right, start, width - start)
        turned = pltpu.roll(lines(start), shift, 1)
        above = lane < shift
        high = high + jnp.where(above, turned, 0.0)
        low = low + jnp.where(above, 0.0, turned)
    total = jnp.concatenate([low, high], axis=1)
    line = lax.broadcasted_iota(jnp.int32, total.shape, 0)
    bit = 1
    while bit < SUBLANES:
        turned = pltpu.roll(total, jnp.where(right, bit, 2 * width - bit), 1)
        total = jnp.where((line & bit) == bit, turned, total)
        bit *= 2
    sums = jnp.sum(total.reshape(group_count, SUBLANES, 2 * width), axis=1)
    return lax.select(right, pltpu.roll(sums, 1, 1), sums)


def turned_columns(block, reverse):
    rows = block.shape[0]
    row = lax.broadcasted_iota(jnp.int32, (rows, rows), 0)
    column = lax.broadcasted_iota(jnp.int32, (rows, rows), 1)
    place = lax.select(reverse, rows - 1 - column, column)
    order = jnp.where(row == place, 1.0, 0.0).astype(block.dtype)
    moved_block = lax.dot_general(block, order, (((0,), (0,)), ((), ())), preferred_element_type=jnp.float32)
    return moved_block.astype(block.dtype)


def diagonal_kernel(query_hbm, keys_hbm, values_hbm, cotangent_hbm, out_ref, left, right, sems):
    odd = is_odd()
    half = out_ref.shape[1]
    low, high = pl.ds(0, half), pl.ds(half, half)
    copies = launch(
        odd,
        [
            (1, keys_hbm.at[:, low], left),
            (1, values_hbm.at[:, low], right),
            (0, cotangent_hbm.at[:, high], left),
            (0, query_hbm.at[:, high], right),
        ],
        sems,
        0,
    )
    finish(odd, copies)
    out_ref[...] = product(left[...], right[...])


def products_kernel(query_ref, keys_ref, values_ref, cotangent_ref, sent_ref, near_ref, across_ref):
    odd = is_odd()
    prod = product(keys_ref[...], values_ref[...])
    grad = product(cotangent_ref[...], query_ref[...])
    near_ref[...] = lax.select(odd, prod, grad)
    across_ref[...] = lax.select(odd, grad, prod)


def tiles_kernel(rows, taps_ref, ready_tiles, late_tiles):
    odd = is_odd()
    group_count, width = taps_ref.shape
    for group in range(group_count):
        row = taps_ref[group : group + 1, :].astype(jnp.float32)
        spread = jnp.concatenate(
            [jnp.zeros((SUBLANES, rows), jnp.float32), jnp.broadcast_to(row, (SUBLANES, width))],
            axis=1,
        )
        spread = pltpu.roll(spread, 0, 1, stride=1, stride_axis=0)
        bands = [
            pltpu.roll(spread, start, 1)[:, rows:] if start else spread[:, rows:]
            for start in range(0, rows, SUBLANES)
        ]
        band = jnp.concatenate(bands, axis=0)
        turned = [band[:, start : start + rows].T for start in range(0, width, rows)]
        turned = jnp.concatenate(turned, axis=1)
        ready_tiles[group] = lax.select(odd, band, turned).astype(jnp.bfloat16)
        late_tiles[group] = lax.select(odd, turned, band).astype(jnp.bfloat16)


def own_kernel(
    rows, ready_tiles, late_tiles, near_ref, across_ref, diagonal_ref, sum_ref, late_ref, ready_ref,
    near_turned, across_turned,
):
    odd = is_odd()
    group_count, width = sum_ref.shape
    group_width = near_ref.shape[1] // group_count
    half = group_count // 2
    blank = jnp.zeros((rows, rows), jnp.float32)
    for group in range(group_count):
        columns = columns_of(group, group_width)
        late_ref[:, columns] = DOT(late_tiles[group, :, :rows], near_ref[:, columns])
        ready_ref[:, columns] = DOT(ready_tiles[group, :, :rows], across_ref[:, columns])
    for group in range(group_count):
        columns, places = columns_of(group, group_width), columns_of(group, rows)
        near_turned[:, places] = turned_columns(near_ref[:, columns], odd)
        across_turned[:, places] = turned_columns(across_ref[:, columns], jnp.logical_not(odd))
    middles = []
    for group in range(half):
        low, high = columns_of(group, group_width), columns_of(group + half, group_width)
        arrived = diagonal_ref[:, low]
        own = lax.select(odd, near_ref[:, high], near_ref[:, low])
        middles.append(DOT_ROWS(lax.select(odd, own, arrived), lax.select(odd, arrived, own)))
        tile = lax.select(
            odd, ready_tiles[group + half, :, rows : 2 * rows], ready_tiles[group, :, rows : 2 * rows]
        )
        more = DOT(tile, arrived)
        ready_ref[:, low] += lax.select(odd, blank, more)
        ready_ref[:, high] += lax.select(odd, more, blank)
    sums = []
    for group in range(group_count):
        columns = columns_of(group, group_width)
        near, across = near_ref[:, columns], across_ref[:, columns]
        outer = DOT_ROWS(lax.select(odd, near, across), lax.select(odd, across, near))
        if group < half:
            middle = lax.select(odd, blank, middles[group])
        else:
            middle = lax.select(odd, middles[group - half], blank)
        sums.append(skewed_sum(jnp.concatenate([outer, middle, blank], axis=1), rows)[:, : 2 * rows])
    sums = jnp.concatenate(sums, axis=0)
    sum_ref[...] = jnp.concatenate([sums, jnp.zeros((group_count, width - 2 * rows), jnp.float32)], axis=1)


def two_kernel(rows, sum_ref, turned_ref, two_ref, out_ref, outer_ref):
    odd = is_odd()
    group_count, width = out_ref.shape
    group_width = two_ref.shape[1] // group_count
    for group in range(group_count):
        columns = columns_of(group, group_width)
        outer_ref[group] = DOT(two_ref[:, columns], turned_ref[:, columns_of(group, rows)])
    sums = skewed_pairs(outer_ref, odd)
    out_ref[...] = sum_ref[...] + jnp.concatenate(
        [jnp.zeros((group_count, width - 2 * rows), jnp.float32), sums], axis=1
    )


def cross_kernel(rows, turned_ref, swap_ref, out_ref, outer_ref):
    odd = is_odd()
    group_count, width = out_ref.shape
    group_width = swap_ref.shape[1] // group_count
    for group in range(group_count):
        columns = columns_of(group, group_width)
        outer_ref[group] = DOT(swap_ref[:, columns], turned_ref[:, columns_of(group, rows)])
    sums = skewed_pairs(outer_ref, jnp.logical_not(odd))
    out_ref[...] = jnp.concatenate([sums, jnp.zeros((group_count, width - 2 * rows), jnp.float32)], axis=1)


def pair_kernel(factor, sum_ref, other_ref, cross_ref, rest_ref, out_ref):
    out_ref[...] = (sum_ref[...] + other_ref[...] + cross_ref[...]) * factor


def add_kernel(*refs):
    *terms, _, out_ref = refs
    out_ref[...] = functools.reduce(jnp.add, [ref[...] for ref in terms])


def forward_kernel(far_ref, rest_ref, out_ref):
    half = out_ref.shape[1]
    out_ref[...] = lax.select(is_odd(), far_ref[:, half:], far_ref[:, :half])


def ready_kernel(
    tiles_ref, ready_ref, two_ref, query_ref, keys_ref, values_ref, sum_ref, rest_ref, one, other
):
    odd = is_odd()
    group_count, rows, _ = tiles_ref.shape
    group_width = two_ref.shape[1] // group_count
    half = group_count // 2
    for group in range(half):
        low, high = columns_of(group, group_width), columns_of(group + half, group_width)
        first = ready_ref[:, low] + DOT(tiles_ref[group, :, 2 * rows :], two_ref[:, low])
        second = ready_ref[:, high] + DOT(tiles_ref[group + half, :, 2 * rows :], two_ref[:, high])
        rest_ref[:, low] = lax.select(odd, first, second)
        known = lax.select(odd, second, first)
        one[:, low] = scaled(known, lax.select(odd, values_ref[:, high], query_ref[:, low]))
        other[:, low] = scaled(known, keys_ref[:, high])


def known_kernel(tiles_ref, late_ref, swap_ref, far_ref, query_ref, keys_ref, values_ref, one, other):
    odd = is_odd()
    group_count, rows, _ = tiles_ref.shape
    group_width = far_ref.shape[1] // group_count
    for group in range(group_count):
        columns = columns_of(group, group_width)
        arrived = jnp.concatenate([swap_ref[:, columns], far_ref[:, columns]], axis=0)
        late = late_ref[:, columns] + DOT(tiles_ref[group, :, rows:], arrived)
        one[:, columns] = scaled(late, lax.select(odd, query_ref[:, columns], values_ref[:, columns]))
        other[:, columns] = scaled(late, keys_ref[:, columns])


def last_kernel(
    tiles_ref, rest_ref, forwarded_ref, query_ref, keys_ref, values_ref,
    ready_one, ready_other, known_one, known_other,
    gated_out, key_out, value_out, mark_ref, one, other, sems,
):
    odd = is_odd()
    mark_ref[...] = jnp.zeros_like(mark_ref)
    group_count, rows, _ = tiles_ref.shape
    half = group_count // 2
    group_width = forwarded_ref.shape[1] // half
    step = max(1, half // PARTS)
    low_half, high_half = pl.ds(0, half * group_width), pl.ds(half * group_width, half * group_width)
    copies = launch(
        odd,
        [
            (0, known_one, key_out),
            (0, known_other, value_out),
            (0, ready_one, gated_out.at[:, low_half]),
            (1, known_one, gated_out),
            (1, ready_one, key_out.at[:, high_half]),
            (1, ready_other, value_out.at[:, high_half]),
        ],
        sems,
        0,
    )
    for group in range(half):
        low, high = columns_of(group, group_width), columns_of(group + half, group_width)
        tile = lax.select(
            odd, tiles_ref[group, :, rows : 2 * rows], tiles_ref[group + half, :, rows : 2 * rows]
        )
        ready = rest_ref[:, low] + DOT(tile, forwarded_ref[:, low])
        one[:, low] = scaled(ready, lax.select(odd, values_ref[:, low], query_ref[:, high]))
        other[:, low] = scaled(ready, keys_ref[:, low])
        if (group + 1) % step == 0:
            start, size = (group + 1 - step) * group_width, step * group_width
            part, place = pl.ds(start, size), pl.ds(start + half * group_width, size)
            moves = [
                (0, one.at[:, part], gated_out.at[:, place]),
                (1, one.at[:, part], key_out.at[:, part]),
                (1, other.at[:, part], value_out.at[:, part]),
            ]
            copies += launch(odd, moves, sems, len(copies))
    finish(odd, copies)


def shards(query, keys, values, cotangent, filter_taps):
    rows, local_width = query.shape
    group_count, taps = filter_taps.shape
    group_width = local_width // group_count
    half_width = local_width // 2
    factor = 1.0 / math.sqrt(rows * lax.axis_size("ctx") * group_width)

    def call(kernel, name, flops=10**6, **options):
        return pl.pallas_call(
            kernel,
            compiler_params=pltpu.CompilerParams(vmem_limit_bytes=VMEM_LIMIT),
            cost_estimate=pl.CostEstimate(flops=flops, bytes_accessed=10**5, transcendentals=0),
            name=name,
            **options,
        )

    bf16, f32 = jnp.bfloat16, jnp.float32
    block, half_block = pltpu.VMEM((rows, local_width), bf16), pltpu.VMEM((rows, half_width), bf16)
    wide, half_wide = pltpu.VMEM((rows, local_width), f32), pltpu.VMEM((rows, half_width), f32)
    tiles, sums = pltpu.VMEM((group_count, rows, taps), bf16), pltpu.VMEM((group_count, taps), f32)
    turned = pltpu.VMEM((group_width, group_count * rows), bf16)
    outs = [jax.ShapeDtypeStruct((rows, local_width), bf16)] * 3

    sent = call(
        diagonal_kernel,
        "diagonal",
        in_specs=[ANYWHERE] * 4,
        out_specs=WHOLE,
        out_shape=half_block,
        scratch_shapes=[half_block] * 2 + [pltpu.SemaphoreType.DMA((4,))],
    )(*in_hbm(query, keys, values, cotangent))
    diagonal = moved(sent, "ctx", (-1, 1))
    near, across = call(
        products_kernel,
        "products",
        in_specs=[WHOLE] * 4 + [ANYWHERE],
        out_specs=[WHOLE] * 2,
        out_shape=[block] * 2,
    )(*in_vmem(query, keys, values, cotangent), sent)
    two = moved(across, "ctx", (2, -2))
    far = moved(near, "ctx", (-2, 2))
    swap = moved(across, "ctx", (1, -1))

    ready_tiles, late_tiles = call(
        functools.partial(tiles_kernel, rows),
        "tiles",
        in_specs=[WHOLE],
        out_specs=[WHOLE] * 2,
        out_shape=[tiles] * 2,
    )(*in_vmem(filter_taps))
    partial, late, ready, near_turned, across_turned = call(
        functools.partial(own_kernel, rows),
        "own",
        flops=4 * 10**9,
        in_specs=[WHOLE] * 5,
        out_specs=[WHOLE] * 5,
        out_shape=[sums, wide, wide, turned, turned],
    )(*in_vmem(ready_tiles, late_tiles, near, across, diagonal))

    partial = call(
        functools.partial(two_kernel, rows),
        "two",
        in_specs=[WHOLE] * 3,
        out_specs=WHOLE,
        out_shape=sums,
        scratch_shapes=[pltpu.VMEM((group_count, rows, rows), f32)],
    )(*in_vmem(partial, near_turned, two))
    other = moved(partial, "ctx", (1, -1))

    rest, ready_one, ready_other = call(
        ready_kernel,
        "ready",
        in_specs=[WHOLE] * 6 + [ANYWHERE],
        out_specs=[WHOLE] * 3,
        out_shape=[half_wide, half_block, half_block],
    )(*in_vmem(ready_tiles, ready, two, query, keys, values), partial)

    forwarded = call(
        forward_kernel,
        "forward",
        in_specs=[WHOLE, ANYWHERE],
        out_specs=WHOLE,
        out_shape=half_block,
    )(*in_vmem(far), rest)
    forwarded = moved(forwarded, "ctx", (1, -1))

    cross = call(
        functools.partial(cross_kernel, rows),
        "cross",
        in_specs=[WHOLE] * 2,
        out_specs=WHOLE,
        out_shape=sums,
        scratch_shapes=[pltpu.VMEM((group_count, rows, rows), f32)],
    )(*in_vmem(across_turned, swap))
    pair_sum = call(
        functools.partial(pair_kernel, factor),
        "pair",
        in_specs=[WHOLE] * 3 + [ANYWHERE],
        out_specs=WHOLE,
        out_shape=sums,
    )(*in_vmem(partial, other, cross), rest)

    known_one, known_other = call(
        known_kernel,
        "known",
        flops=4 * 10**9,
        in_specs=[WHOLE] * 7,
        out_specs=[WHOLE] * 2,
        out_shape=[block] * 2,
    )(*in_vmem(late_tiles, late, swap, far, query, keys, values))

    def add(*terms, out_shape=sums, after=known_one):
        return call(
            add_kernel,
            "add",
            in_specs=[WHOLE] * len(terms) + [ANYWHERE],
            out_specs=WHOLE,
            out_shape=out_shape,
        )(*in_vmem(*terms), after)

    terms = sum_terms(pair_sum, "ctx", add)
    gated, key_grad, value_grad, mark = call(
        last_kernel,
        "last",
        in_specs=[WHOLE] * 10,
        out_specs=[ANYWHERE] * 3 + [WHOLE],
        out_shape=outs + [pltpu.VMEM((SUBLANES, group_width), f32)],
        scratch_shapes=[half_block] * 2 + [pltpu.SemaphoreType.DMA((6 + 3 * PARTS,))],
    )(
        *in_vmem(ready_tiles, rest, forwarded, query, keys, values),
        *in_vmem(ready_one, ready_other, known_one, known_other),
    )
    whole_sums = jax.ShapeDtypeStruct((group_count, taps), f32)
    return (gated, key_grad, value_grad, add(*terms, out_shape=whole_sums, after=mark))


def solution(mesh):
    in_specs = (P("ctx", "grp"), P("ctx", "grp"), P("ctx", "grp"), P("ctx", "grp"), P("grp", None))
    out_specs = (P("ctx", "grp"), P("ctx", "grp"), P("ctx", "grp"), P("grp", None))
    return jax.shard_map(shards, mesh=mesh, in_specs=in_specs, out_specs=out_specs, check_vma=False)
```

```python
import functools
import math

import jax
import jax.numpy as jnp
from jax import lax
from jax.experimental import pallas as pl
from jax.experimental.pallas import tpu as pltpu
from jax.sharding import PartitionSpec as P

SUBLANES = 8
PARTS = 2
VMEM_LIMIT = 16 * 1024 * 1024
WHOLE = pl.BlockSpec(memory_space=pltpu.VMEM)
ANYWHERE = pl.BlockSpec(memory_space=pl.ANY)
DOT_ROWS = functools.partial(
    lax.dot_general,
    dimension_numbers=(((1,), (1,)), ((), ())),
    preferred_element_type=jnp.float32,
)
DOT = functools.partial(jnp.dot, preferred_element_type=jnp.float32)


def in_vmem(*arrays):
    return [pltpu.with_memory_space_constraint(array, pltpu.VMEM) for array in arrays]


def in_hbm(*arrays):
    return [pltpu.with_memory_space_constraint(array, pltpu.HBM) for array in arrays]


def moved(block, axis, distances):
    size = lax.axis_size(axis)
    route = [(i, i + distances[i % 2]) for i in range(size)]
    return lax.ppermute(block, axis, [pair for pair in route if 0 <= pair[1] < size])


def sum_terms(pair_sum, axis, add):
    size = lax.axis_size(axis)
    if size & (size - 1):
        even = lax.axis_index(axis) % 2 == 0
        return [lax.psum(jnp.where(even, pair_sum, 0.0), axis)]
    terms = [pair_sum]
    stride = 2
    while stride < size:
        own = terms[0] if len(terms) == 1 else add(*terms)
        members = 4 if 4 * stride <= size else 2
        rounds = ((1, 3, 0, 2), (3, 2, 1, 0), (2, 0, 3, 1)) if members == 4 else ((1, 0),)
        terms = [own]
        for targets in rounds:
            places = [(i, i // stride % members) for i in range(size)]
            route = [(i, i + (targets[place] - place) * stride) for i, place in places]
            terms.append(lax.ppermute(own, axis, route))
        stride *= members
    return terms


def is_odd():
    return lax.rem(lax.axis_index("ctx"), 2) == 1


def product(left, right):
    return (left.astype(jnp.float32) * right.astype(jnp.float32)).astype(jnp.bfloat16)


def scaled(value, factor):
    return (value * factor.astype(jnp.float32)).astype(jnp.bfloat16)


def columns_of(group, width):
    return slice(group * width, (group + 1) * width)


def launch(odd, moves, sems, used):
    copies = [(*move, sems.at[used + place]) for place, move in enumerate(moves)]
    for parity, source, target, sem in copies:
        @pl.when(odd if parity else jnp.logical_not(odd))
        def _():
            pltpu.make_async_copy(source, target, sem).start()
    return copies


def finish(odd, copies):
    for parity, source, target, sem in copies:
        @pl.when(odd if parity else jnp.logical_not(odd))
        def _():
            pltpu.make_async_copy(source, target, sem).wait()


def lines_summed(total):
    line = lax.broadcasted_iota(jnp.int32, total.shape, 0)
    bit = 1
    while bit < SUBLANES:
        total = jnp.where((line & bit) == bit, pltpu.roll(total, total.shape[1] - bit, 1), total)
        bit *= 2
    return jnp.sum(total, axis=0, keepdims=True)


def skewed_sum(outer, rows):
    width = outer.shape[1]
    total = outer[:SUBLANES]
    for start in range(SUBLANES, rows, SUBLANES):
        total = total + pltpu.roll(outer[start : start + SUBLANES], width - start, 1)
    return lines_summed(total)


def skewed_pairs(outer_ref, right):
    group_count, rows, width = outer_ref.shape

    def lines(start):
        return outer_ref[:, start : start + SUBLANES, :].reshape(group_count * SUBLANES, width)

    first = lines(0)
    blank = jnp.zeros_like(first)
    high = lax.select(right, blank, first)
    low = lax.select(right, first, blank)
    lane = lax.broadcasted_iota(jnp.int32, first.shape, 1)
    for start in range(SUBLANES, rows, SUBLANES):
        shift = jnp.where(right, start, width - start)
        turned = pltpu.roll(lines(start), shift, 1)
        above = lane < shift
        high = high + jnp.where(above, turned, 0.0)
        low = low + jnp.where(above, 0.0, turned)
    total = jnp.concatenate([low, high], axis=1)
    line = lax.broadcasted_iota(jnp.int32, total.shape, 0)
    bit = 1
    while bit < SUBLANES:
        turned = pltpu.roll(total, jnp.where(right, bit, 2 * width - bit), 1)
        total = jnp.where((line & bit) == bit, turned, total)
        bit *= 2
    sums = jnp.sum(total.reshape(group_count, SUBLANES, 2 * width), axis=1)
    return lax.select(right, pltpu.roll(sums, 1, 1), sums)


def turned_columns(block, reverse):
    rows = block.shape[0]
    row = lax.broadcasted_iota(jnp.int32, (rows, rows), 0)
    column = lax.broadcasted_iota(jnp.int32, (rows, rows), 1)
    place = lax.select(reverse, rows - 1 - column, column)
    order = jnp.where(row == place, 1.0, 0.0).astype(block.dtype)
    moved_block = lax.dot_general(block, order, (((0,), (0,)), ((), ())), preferred_element_type=jnp.float32)
    return moved_block.astype(block.dtype)


def diagonal_kernel(query_hbm, keys_hbm, values_hbm, cotangent_hbm, out_ref, left, right, sems):
    odd = is_odd()
    half = out_ref.shape[1]
    low, high = pl.ds(0, half), pl.ds(half, half)
    copies = launch(
        odd,
        [
            (1, keys_hbm.at[:, low], left),
            (1, values_hbm.at[:, low], right),
            (0, cotangent_hbm.at[:, high], left),
            (0, query_hbm.at[:, high], right),
        ],
        sems,
        0,
    )
    finish(odd, copies)
    out_ref[...] = product(left[...], right[...])


def products_kernel(query_ref, keys_ref, values_ref, cotangent_ref, sent_ref, near_ref, across_ref):
    odd = is_odd()
    prod = product(keys_ref[...], values_ref[...])
    grad = product(cotangent_ref[...], query_ref[...])
    near_ref[...] = lax.select(odd, prod, grad)
    across_ref[...] = lax.select(odd, grad, prod)


def tiles_kernel(rows, taps_ref, ready_tiles, late_tiles):
    odd = is_odd()
    group_count, width = taps_ref.shape
    for group in range(group_count):
        row = taps_ref[group : group + 1, :].astype(jnp.float32)
        spread = jnp.concatenate(
            [jnp.zeros((SUBLANES, rows), jnp.float32), jnp.broadcast_to(row, (SUBLANES, width))],
            axis=1,
        )
        spread = pltpu.roll(spread, 0, 1, stride=1, stride_axis=0)
        bands = [
            pltpu.roll(spread, start, 1)[:, rows:] if start else spread[:, rows:]
            for start in range(0, rows, SUBLANES)
        ]
        band = jnp.concatenate(bands, axis=0)
        turned = [band[:, start : start + rows].T for start in range(0, width, rows)]
        turned = jnp.concatenate(turned, axis=1)
        ready_tiles[group] = lax.select(odd, band, turned).astype(jnp.bfloat16)
        late_tiles[group] = lax.select(odd, turned, band).astype(jnp.bfloat16)


def own_kernel(
    rows, ready_tiles, late_tiles, near_ref, across_ref, diagonal_ref, sum_ref, late_ref, ready_ref,
    near_turned, across_turned,
):
    odd = is_odd()
    group_count, width = sum_ref.shape
    group_width = near_ref.shape[1] // group_count
    half = group_count // 2
    blank = jnp.zeros((rows, rows), jnp.float32)
    for group in range(group_count):
        columns = columns_of(group, group_width)
        late_ref[:, columns] = DOT(late_tiles[group, :, :rows], near_ref[:, columns])
        ready_ref[:, columns] = DOT(ready_tiles[group, :, :rows], across_ref[:, columns])
    for group in range(group_count):
        columns, places = columns_of(group, group_width), columns_of(group, rows)
        near_turned[:, places] = turned_columns(near_ref[:, columns], odd)
        across_turned[:, places] = turned_columns(across_ref[:, columns], jnp.logical_not(odd))
    middles = []
    for group in range(half):
        low, high = columns_of(group, group_width), columns_of(group + half, group_width)
        arrived = diagonal_ref[:, low]
        own = lax.select(odd, near_ref[:, high], near_ref[:, low])
        middles.append(DOT_ROWS(lax.select(odd, own, arrived), lax.select(odd, arrived, own)))
        tile = lax.select(
            odd, ready_tiles[group + half, :, rows : 2 * rows], ready_tiles[group, :, rows : 2 * rows]
        )
        more = DOT(tile, arrived)
        ready_ref[:, low] += lax.select(odd, blank, more)
        ready_ref[:, high] += lax.select(odd, more, blank)
    sums = []
    for group in range(group_count):
        columns = columns_of(group, group_width)
        near, across = near_ref[:, columns], across_ref[:, columns]
        outer = DOT_ROWS(lax.select(odd, near, across), lax.select(odd, across, near))
        if group < half:
            middle = lax.select(odd, blank, middles[group])
        else:
            middle = lax.select(odd, middles[group - half], blank)
        sums.append(skewed_sum(jnp.concatenate([outer, middle, blank], axis=1), rows)[:, : 2 * rows])
    sums = jnp.concatenate(sums, axis=0)
    sum_ref[...] = jnp.concatenate([sums, jnp.zeros((group_count, width - 2 * rows), jnp.float32)], axis=1)


def two_kernel(rows, sum_ref, turned_ref, two_ref, out_ref, outer_ref):
    odd = is_odd()
    group_count, width = out_ref.shape
    group_width = two_ref.shape[1] // group_count
    for group in range(group_count):
        columns = columns_of(group, group_width)
        outer_ref[group] = DOT(two_ref[:, columns], turned_ref[:, columns_of(group, rows)])
    sums = skewed_pairs(outer_ref, odd)
    out_ref[...] = sum_ref[...] + jnp.concatenate(
        [jnp.zeros((group_count, width - 2 * rows), jnp.float32), sums], axis=1
    )


def cross_kernel(rows, turned_ref, swap_ref, out_ref, outer_ref):
    odd = is_odd()
    group_count, width = out_ref.shape
    group_width = swap_ref.shape[1] // group_count
    for group in range(group_count):
        columns = columns_of(group, group_width)
        outer_ref[group] = DOT(swap_ref[:, columns], turned_ref[:, columns_of(group, rows)])
    sums = skewed_pairs(outer_ref, jnp.logical_not(odd))
    out_ref[...] = jnp.concatenate([sums, jnp.zeros((group_count, width - 2 * rows), jnp.float32)], axis=1)


def pair_kernel(factor, sum_ref, other_ref, cross_ref, rest_ref, out_ref):
    out_ref[...] = (sum_ref[...] + other_ref[...] + cross_ref[...]) * factor


def add_kernel(*refs):
    *terms, _, out_ref = refs
    out_ref[...] = functools.reduce(jnp.add, [ref[...] for ref in terms])


def forward_kernel(far_ref, rest_ref, out_ref):
    half = out_ref.shape[1]
    out_ref[...] = lax.select(is_odd(), far_ref[:, half:], far_ref[:, :half])


def ready_kernel(
    tiles_ref, ready_ref, two_ref, query_ref, keys_ref, values_ref, sum_ref, rest_ref, one, other
):
    odd = is_odd()
    group_count, rows, _ = tiles_ref.shape
    group_width = two_ref.shape[1] // group_count
    half = group_count // 2
    for group in range(half):
        low, high = columns_of(group, group_width), columns_of(group + half, group_width)
        first = ready_ref[:, low] + DOT(tiles_ref[group, :, 2 * rows :], two_ref[:, low])
        second = ready_ref[:, high] + DOT(tiles_ref[group + half, :, 2 * rows :], two_ref[:, high])
        rest_ref[:, low] = lax.select(odd, first, second)
        known = lax.select(odd, second, first)
        one[:, low] = scaled(known, lax.select(odd, values_ref[:, high], query_ref[:, low]))
        other[:, low] = scaled(known, keys_ref[:, high])


def known_kernel(tiles_ref, late_ref, swap_ref, far_ref, query_ref, keys_ref, values_ref, one, other):
    odd = is_odd()
    group_count, rows, _ = tiles_ref.shape
    group_width = far_ref.shape[1] // group_count
    for group in range(group_count):
        columns = columns_of(group, group_width)
        arrived = jnp.concatenate([swap_ref[:, columns], far_ref[:, columns]], axis=0)
        late = late_ref[:, columns] + DOT(tiles_ref[group, :, rows:], arrived)
        one[:, columns] = scaled(late, lax.select(odd, query_ref[:, columns], values_ref[:, columns]))
        other[:, columns] = scaled(late, keys_ref[:, columns])


def last_kernel(
    tiles_ref, rest_ref, forwarded_ref, query_ref, keys_ref, values_ref,
    ready_one, ready_other, known_one, known_other,
    gated_out, key_out, value_out, mark_ref, one, other, sems,
):
    odd = is_odd()
    mark_ref[...] = jnp.zeros_like(mark_ref)
    group_count, rows, _ = tiles_ref.shape
    half = group_count // 2
    group_width = forwarded_ref.shape[1] // half
    step = max(1, half // PARTS)
    low_half, high_half = pl.ds(0, half * group_width), pl.ds(half * group_width, half * group_width)
    copies = launch(
        odd,
        [
            (0, known_one, key_out),
            (0, known_other, value_out),
            (0, ready_one, gated_out.at[:, low_half]),
            (1, known_one, gated_out),
            (1, ready_one, key_out.at[:, high_half]),
            (1, ready_other, value_out.at[:, high_half]),
        ],
        sems,
        0,
    )
    for group in range(half):
        low, high = columns_of(group, group_width), columns_of(group + half, group_width)
        tile = lax.select(
            odd, tiles_ref[group, :, rows : 2 * rows], tiles_ref[group + half, :, rows : 2 * rows]
        )
        ready = rest_ref[:, low] + DOT(tile, forwarded_ref[:, low])
        one[:, low] = scaled(ready, lax.select(odd, values_ref[:, low], query_ref[:, high]))
        other[:, low] = scaled(ready, keys_ref[:, low])
        if (group + 1) % step == 0:
            start, size = (group + 1 - step) * group_width, step * group_width
            part, place = pl.ds(start, size), pl.ds(start + half * group_width, size)
            moves = [
                (0, one.at[:, part], gated_out.at[:, place]),
                (1, one.at[:, part], key_out.at[:, part]),
                (1, other.at[:, part], value_out.at[:, part]),
            ]
            copies += launch(odd, moves, sems, len(copies))
    finish(odd, copies)


def shards(query, keys, values, cotangent, filter_taps):
    rows, local_width = query.shape
    group_count, taps = filter_taps.shape
    group_width = local_width // group_count
    half_width = local_width // 2
    factor = 1.0 / math.sqrt(rows * lax.axis_size("ctx") * group_width)

    def call(kernel, name, flops=10**6, **options):
        return pl.pallas_call(
            kernel,
            compiler_params=pltpu.CompilerParams(vmem_limit_bytes=VMEM_LIMIT),
            cost_estimate=pl.CostEstimate(flops=flops, bytes_accessed=10**5, transcendentals=0),
            name=name,
            **options,
        )

    bf16, f32 = jnp.bfloat16, jnp.float32
    block, half_block = pltpu.VMEM((rows, local_width), bf16), pltpu.VMEM((rows, half_width), bf16)
    wide, half_wide = pltpu.VMEM((rows, local_width), f32), pltpu.VMEM((rows, half_width), f32)
    tiles, sums = pltpu.VMEM((group_count, rows, taps), bf16), pltpu.VMEM((group_count, taps), f32)
    turned = pltpu.VMEM((group_width, group_count * rows), bf16)
    outs = [jax.ShapeDtypeStruct((rows, local_width), bf16)] * 3

    sent = call(
        diagonal_kernel,
        "diagonal",
        in_specs=[ANYWHERE] * 4,
        out_specs=WHOLE,
        out_shape=half_block,
        scratch_shapes=[half_block] * 2 + [pltpu.SemaphoreType.DMA((4,))],
    )(*in_hbm(query, keys, values, cotangent))
    diagonal = moved(sent, "ctx", (-1, 1))
    near, across = call(
        products_kernel,
        "products",
        in_specs=[WHOLE] * 4 + [ANYWHERE],
        out_specs=[WHOLE] * 2,
        out_shape=[block] * 2,
    )(*in_vmem(query, keys, values, cotangent), sent)
    two = moved(across, "ctx", (2, -2))
    far = moved(near, "ctx", (-2, 2))
    swap = moved(across, "ctx", (1, -1))

    ready_tiles, late_tiles = call(
        functools.partial(tiles_kernel, rows),
        "tiles",
        in_specs=[WHOLE],
        out_specs=[WHOLE] * 2,
        out_shape=[tiles] * 2,
    )(*in_vmem(filter_taps))
    partial, late, ready, near_turned, across_turned = call(
        functools.partial(own_kernel, rows),
        "own",
        flops=4 * 10**9,
        in_specs=[WHOLE] * 5,
        out_specs=[WHOLE] * 5,
        out_shape=[sums, wide, wide, turned, turned],
    )(*in_vmem(ready_tiles, late_tiles, near, across, diagonal))

    partial = call(
        functools.partial(two_kernel, rows),
        "two",
        in_specs=[WHOLE] * 3,
        out_specs=WHOLE,
        out_shape=sums,
        scratch_shapes=[pltpu.VMEM((group_count, rows, rows), f32)],
    )(*in_vmem(partial, near_turned, two))
    other = moved(partial, "ctx", (1, -1))

    rest, ready_one, ready_other = call(
        ready_kernel,
        "ready",
        in_specs=[WHOLE] * 6 + [ANYWHERE],
        out_specs=[WHOLE] * 3,
        out_shape=[half_wide, half_block, half_block],
    )(*in_vmem(ready_tiles, ready, two, query, keys, values), partial)

    forwarded = call(
        forward_kernel,
        "forward",
        in_specs=[WHOLE, ANYWHERE],
        out_specs=WHOLE,
        out_shape=half_block,
    )(*in_vmem(far), rest)
    forwarded = moved(forwarded, "ctx", (1, -1))

    cross = call(
        functools.partial(cross_kernel, rows),
        "cross",
        in_specs=[WHOLE] * 2,
        out_specs=WHOLE,
        out_shape=sums,
        scratch_shapes=[pltpu.VMEM((group_count, rows, rows), f32)],
    )(*in_vmem(across_turned, swap))
    pair_sum = call(
        functools.partial(pair_kernel, factor),
        "pair",
        in_specs=[WHOLE] * 3 + [ANYWHERE],
        out_specs=WHOLE,
        out_shape=sums,
    )(*in_vmem(partial, other, cross), rest)

    known_one, known_other = call(
        known_kernel,
        "known",
        flops=4 * 10**9,
        in_specs=[WHOLE] * 7,
        out_specs=[WHOLE] * 2,
        out_shape=[block] * 2,
    )(*in_vmem(late_tiles, late, swap, far, query, keys, values))

    def add(*terms, out_shape=sums, after=known_one):
        return call(
            add_kernel,
            "add",
            in_specs=[WHOLE] * len(terms) + [ANYWHERE],
            out_specs=WHOLE,
            out_shape=out_shape,
        )(*in_vmem(*terms), after)

    terms = sum_terms(pair_sum, "ctx", add)
    gated, key_grad, value_grad, mark = call(
        last_kernel,
        "last",
        in_specs=[WHOLE] * 10,
        out_specs=[ANYWHERE] * 3 + [WHOLE],
        out_shape=outs + [pltpu.VMEM((SUBLANES, group_width), f32)],
        scratch_shapes=[half_block] * 2 + [pltpu.SemaphoreType.DMA((6 + 3 * PARTS,))],
    )(
        *in_vmem(ready_tiles, rest, forwarded, query, keys, values),
        *in_vmem(ready_one, ready_other, known_one, known_other),
    )
    whole_sums = jax.ShapeDtypeStruct((group_count, taps), f32)
    return (gated, key_grad, value_grad, add(*terms, out_shape=whole_sums, after=mark))


def solution(mesh):
    in_specs = (P("ctx", "grp"), P("ctx", "grp"), P("ctx", "grp"), P("ctx", "grp"), P("grp", None))
    out_specs = (P("ctx", "grp"), P("ctx", "grp"), P("ctx", "grp"), P("grp", None))
    return jax.shard_map(shards, mesh=mesh, in_specs=in_specs, out_specs=out_specs, check_vma=False)
```

```python
import functools
import math

import jax
import jax.numpy as jnp
from jax import lax
from jax.experimental import pallas as pl
from jax.experimental.pallas import tpu as pltpu
from jax.sharding import PartitionSpec as P

SUBLANES = 8
PARTS = 4
VMEM_LIMIT = 16 * 1024 * 1024
WHOLE = pl.BlockSpec(memory_space=pltpu.VMEM)
ANYWHERE = pl.BlockSpec(memory_space=pl.ANY)
DOT_ROWS = functools.partial(
    lax.dot_general,
    dimension_numbers=(((1,), (1,)), ((), ())),
    preferred_element_type=jnp.float32,
)
DOT = functools.partial(jnp.dot, preferred_element_type=jnp.float32)


def in_vmem(*arrays):
    return [pltpu.with_memory_space_constraint(array, pltpu.VMEM) for array in arrays]


def in_hbm(*arrays):
    return [pltpu.with_memory_space_constraint(array, pltpu.HBM) for array in arrays]


def moved(block, axis, distances):
    size = lax.axis_size(axis)
    route = [(i, i + distances[i % 2]) for i in range(size)]
    return lax.ppermute(block, axis, [pair for pair in route if 0 <= pair[1] < size])


def sum_terms(pair_sum, axis, add):
    size = lax.axis_size(axis)
    if size & (size - 1):
        even = lax.axis_index(axis) % 2 == 0
        return [lax.psum(jnp.where(even, pair_sum, 0.0), axis)]
    terms = [pair_sum]
    stride = 2
    while stride < size:
        own = terms[0] if len(terms) == 1 else add(*terms)
        members = 4 if 4 * stride <= size else 2
        rounds = ((1, 3, 0, 2), (3, 2, 1, 0), (2, 0, 3, 1)) if members == 4 else ((1, 0),)
        terms = [own]
        for targets in rounds:
            places = [(i, i // stride % members) for i in range(size)]
            route = [(i, i + (targets[place] - place) * stride) for i, place in places]
            terms.append(lax.ppermute(own, axis, route))
        stride *= members
    return terms


def is_odd():
    return lax.rem(lax.axis_index("ctx"), 2) == 1


def product(left, right):
    return (left.astype(jnp.float32) * right.astype(jnp.float32)).astype(jnp.bfloat16)


def scaled(value, factor):
    return (value * factor.astype(jnp.float32)).astype(jnp.bfloat16)


def columns_of(group, width):
    return slice(group * width, (group + 1) * width)


def launch(odd, moves, sems, used):
    copies = [(*move, sems.at[used + place]) for place, move in enumerate(moves)]
    for parity, source, target, sem in copies:
        @pl.when(odd if parity else jnp.logical_not(odd))
        def _():
            pltpu.make_async_copy(source, target, sem).start()
    return copies


def finish(odd, copies):
    for parity, source, target, sem in copies:
        @pl.when(odd if parity else jnp.logical_not(odd))
        def _():
            pltpu.make_async_copy(source, target, sem).wait()


def lines_summed(total):
    line = lax.broadcasted_iota(jnp.int32, total.shape, 0)
    bit = 1
    while bit < SUBLANES:
        total = jnp.where((line & bit) == bit, pltpu.roll(total, total.shape[1] - bit, 1), total)
        bit *= 2
    return jnp.sum(total, axis=0, keepdims=True)


def skewed_sum(outer, rows):
    width = outer.shape[1]
    total = outer[:SUBLANES]
    for start in range(SUBLANES, rows, SUBLANES):
        total = total + pltpu.roll(outer[start : start + SUBLANES], width - start, 1)
    return lines_summed(total)


def skewed_pairs(outer_ref, right):
    group_count, rows, width = outer_ref.shape

    def lines(start):
        return outer_ref[:, start : start + SUBLANES, :].reshape(group_count * SUBLANES, width)

    first = lines(0)
    blank = jnp.zeros_like(first)
    high = lax.select(right, blank, first)
    low = lax.select(right, first, blank)
    lane = lax.broadcasted_iota(jnp.int32, first.shape, 1)
    for start in range(SUBLANES, rows, SUBLANES):
        shift = jnp.where(right, start, width - start)
        turned = pltpu.roll(lines(start), shift, 1)
        above = lane < shift
        high = high + jnp.where(above, turned, 0.0)
        low = low + jnp.where(above, 0.0, turned)
    total = jnp.concatenate([low, high], axis=1)
    line = lax.broadcasted_iota(jnp.int32, total.shape, 0)
    bit = 1
    while bit < SUBLANES:
        turned = pltpu.roll(total, jnp.where(right, bit, 2 * width - bit), 1)
        total = jnp.where((line & bit) == bit, turned, total)
        bit *= 2
    sums = jnp.sum(total.reshape(group_count, SUBLANES, 2 * width), axis=1)
    return lax.select(right, pltpu.roll(sums, 1, 1), sums)


def turned_columns(block, reverse):
    rows = block.shape[0]
    row = lax.broadcasted_iota(jnp.int32, (rows, rows), 0)
    column = lax.broadcasted_iota(jnp.int32, (rows, rows), 1)
    place = lax.select(reverse, rows - 1 - column, column)
    order = jnp.where(row == place, 1.0, 0.0).astype(block.dtype)
    moved_block = lax.dot_general(block, order, (((0,), (0,)), ((), ())), preferred_element_type=jnp.float32)
    return moved_block.astype(block.dtype)


def diagonal_kernel(query_hbm, keys_hbm, values_hbm, cotangent_hbm, out_ref, left, right, sems):
    odd = is_odd()
    half = out_ref.shape[1]
    low, high = pl.ds(0, half), pl.ds(half, half)
    copies = launch(
        odd,
        [
            (1, keys_hbm.at[:, low], left),
            (1, values_hbm.at[:, low], right),
            (0, cotangent_hbm.at[:, high], left),
            (0, query_hbm.at[:, high], right),
        ],
        sems,
        0,
    )
    finish(odd, copies)
    out_ref[...] = product(left[...], right[...])


def products_kernel(query_ref, keys_ref, values_ref, cotangent_ref, sent_ref, near_ref, across_ref):
    odd = is_odd()
    prod = product(keys_ref[...], values_ref[...])
    grad = product(cotangent_ref[...], query_ref[...])
    near_ref[...] = lax.select(odd, prod, grad)
    across_ref[...] = lax.select(odd, grad, prod)


def tiles_kernel(rows, taps_ref, ready_tiles, late_tiles):
    odd = is_odd()
    group_count, width = taps_ref.shape
    for group in range(group_count):
        row = taps_ref[group : group + 1, :].astype(jnp.float32)
        spread = jnp.concatenate(
            [jnp.zeros((SUBLANES, rows), jnp.float32), jnp.broadcast_to(row, (SUBLANES, width))],
            axis=1,
        )
        spread = pltpu.roll(spread, 0, 1, stride=1, stride_axis=0)
        bands = [
            pltpu.roll(spread, start, 1)[:, rows:] if start else spread[:, rows:]
            for start in range(0, rows, SUBLANES)
        ]
        band = jnp.concatenate(bands, axis=0)
        turned = [band[:, start : start + rows].T for start in range(0, width, rows)]
        turned = jnp.concatenate(turned, axis=1)
        ready_tiles[group] = lax.select(odd, band, turned).astype(jnp.bfloat16)
        late_tiles[group] = lax.select(odd, turned, band).astype(jnp.bfloat16)


def own_kernel(
    rows, ready_tiles, late_tiles, near_ref, across_ref, diagonal_ref, sum_ref, late_ref, ready_ref,
    near_turned, across_turned,
):
    odd = is_odd()
    group_count, width = sum_ref.shape
    group_width = near_ref.shape[1] // group_count
    half = group_count // 2
    blank = jnp.zeros((rows, rows), jnp.float32)
    for group in range(group_count):
        columns = columns_of(group, group_width)
        late_ref[:, columns] = DOT(late_tiles[group, :, :rows], near_ref[:, columns])
        ready_ref[:, columns] = DOT(ready_tiles[group, :, :rows], across_ref[:, columns])
    for group in range(group_count):
        columns, places = columns_of(group, group_width), columns_of(group, rows)
        near_turned[:, places] = turned_columns(near_ref[:, columns], odd)
        across_turned[:, places] = turned_columns(across_ref[:, columns], jnp.logical_not(odd))
    middles = []
    for group in range(half):
        low, high = columns_of(group, group_width), columns_of(group + half, group_width)
        arrived = diagonal_ref[:, low]
        own = lax.select(odd, near_ref[:, high], near_ref[:, low])
        middles.append(DOT_ROWS(lax.select(odd, own, arrived), lax.select(odd, arrived, own)))
        tile = lax.select(
            odd, ready_tiles[group + half, :, rows : 2 * rows], ready_tiles[group, :, rows : 2 * rows]
        )
        more = DOT(tile, arrived)
        ready_ref[:, low] += lax.select(odd, blank, more)
        ready_ref[:, high] += lax.select(odd, more, blank)
    sums = []
    for group in range(group_count):
        columns = columns_of(group, group_width)
        near, across = near_ref[:, columns], across_ref[:, columns]
        outer = DOT_ROWS(lax.select(odd, near, across), lax.select(odd, across, near))
        if group < half:
            middle = lax.select(odd, blank, middles[group])
        else:
            middle = lax.select(odd, middles[group - half], blank)
        sums.append(skewed_sum(jnp.concatenate([outer, middle, blank], axis=1), rows)[:, : 2 * rows])
    sums = jnp.concatenate(sums, axis=0)
    sum_ref[...] = jnp.concatenate([sums, jnp.zeros((group_count, width - 2 * rows), jnp.float32)], axis=1)


def two_kernel(rows, sum_ref, turned_ref, two_ref, out_ref, outer_ref):
    odd = is_odd()
    group_count, width = out_ref.shape
    group_width = two_ref.shape[1] // group_count
    for group in range(group_count):
        columns = columns_of(group, group_width)
        outer_ref[group] = DOT(two_ref[:, columns], turned_ref[:, columns_of(group, rows)])
    sums = skewed_pairs(outer_ref, odd)
    out_ref[...] = sum_ref[...] + jnp.concatenate(
        [jnp.zeros((group_count, width - 2 * rows), jnp.float32), sums], axis=1
    )


def cross_kernel(rows, turned_ref, swap_ref, out_ref, outer_ref):
    odd = is_odd()
    group_count, width = out_ref.shape
    group_width = swap_ref.shape[1] // group_count
    for group in range(group_count):
        columns = columns_of(group, group_width)
        outer_ref[group] = DOT(swap_ref[:, columns], turned_ref[:, columns_of(group, rows)])
    sums = skewed_pairs(outer_ref, jnp.logical_not(odd))
    out_ref[...] = jnp.concatenate([sums, jnp.zeros((group_count, width - 2 * rows), jnp.float32)], axis=1)


def pair_kernel(factor, sum_ref, other_ref, cross_ref, rest_ref, out_ref):
    out_ref[...] = (sum_ref[...] + other_ref[...] + cross_ref[...]) * factor


def add_kernel(*refs):
    *terms, _, out_ref = refs
    out_ref[...] = functools.reduce(jnp.add, [ref[...] for ref in terms])


def forward_kernel(far_ref, rest_ref, out_ref):
    half = out_ref.shape[1]
    out_ref[...] = lax.select(is_odd(), far_ref[:, half:], far_ref[:, :half])


def ready_kernel(
    tiles_ref, ready_ref, two_ref, query_ref, keys_ref, values_ref, sum_ref, rest_ref, one, other
):
    odd = is_odd()
    group_count, rows, _ = tiles_ref.shape
    group_width = two_ref.shape[1] // group_count
    half = group_count // 2
    for group in range(half):
        low, high = columns_of(group, group_width), columns_of(group + half, group_width)
        first = ready_ref[:, low] + DOT(tiles_ref[group, :, 2 * rows :], two_ref[:, low])
        second = ready_ref[:, high] + DOT(tiles_ref[group + half, :, 2 * rows :], two_ref[:, high])
        rest_ref[:, low] = lax.select(odd, first, second)
        known = lax.select(odd, second, first)
        one[:, low] = scaled(known, lax.select(odd, values_ref[:, high], query_ref[:, low]))
        other[:, low] = scaled(known, keys_ref[:, high])


def known_kernel(tiles_ref, late_ref, swap_ref, far_ref, query_ref, keys_ref, values_ref, one, other):
    odd = is_odd()
    group_count, rows, _ = tiles_ref.shape
    group_width = far_ref.shape[1] // group_count
    for group in range(group_count):
        columns = columns_of(group, group_width)
        arrived = jnp.concatenate([swap_ref[:, columns], far_ref[:, columns]], axis=0)
        late = late_ref[:, columns] + DOT(tiles_ref[group, :, rows:], arrived)
        one[:, columns] = scaled(late, lax.select(odd, query_ref[:, columns], values_ref[:, columns]))
        other[:, columns] = scaled(late, keys_ref[:, columns])


def last_kernel(
    tiles_ref, rest_ref, forwarded_ref, query_ref, keys_ref, values_ref,
    ready_one, ready_other, known_one, known_other,
    gated_out, key_out, value_out, mark_ref, one, other, sems,
):
    odd = is_odd()
    mark_ref[...] = jnp.zeros_like(mark_ref)
    group_count, rows, _ = tiles_ref.shape
    half = group_count // 2
    group_width = forwarded_ref.shape[1] // half
    step = max(1, half // PARTS)
    low_half, high_half = pl.ds(0, half * group_width), pl.ds(half * group_width, half * group_width)
    copies = launch(
        odd,
        [
            (0, known_one, key_out),
            (0, known_other, value_out),
            (0, ready_one, gated_out.at[:, low_half]),
            (1, known_one, gated_out),
            (1, ready_one, key_out.at[:, high_half]),
            (1, ready_other, value_out.at[:, high_half]),
        ],
        sems,
        0,
    )
    for group in range(half):
        low, high = columns_of(group, group_width), columns_of(group + half, group_width)
        tile = lax.select(
            odd, tiles_ref[group, :, rows : 2 * rows], tiles_ref[group + half, :, rows : 2 * rows]
        )
        ready = rest_ref[:, low] + DOT(tile, forwarded_ref[:, low])
        one[:, low] = scaled(ready, lax.select(odd, values_ref[:, low], query_ref[:, high]))
        other[:, low] = scaled(ready, keys_ref[:, low])
        if (group + 1) % step == 0:
            start, size = (group + 1 - step) * group_width, step * group_width
            part, place = pl.ds(start, size), pl.ds(start + half * group_width, size)
            moves = [
                (0, one.at[:, part], gated_out.at[:, place]),
                (1, one.at[:, part], key_out.at[:, part]),
                (1, other.at[:, part], value_out.at[:, part]),
            ]
            copies += launch(odd, moves, sems, len(copies))
    finish(odd, copies)


def shards(query, keys, values, cotangent, filter_taps):
    rows, local_width = query.shape
    group_count, taps = filter_taps.shape
    group_width = local_width // group_count
    half_width = local_width // 2
    factor = 1.0 / math.sqrt(rows * lax.axis_size("ctx") * group_width)

    def call(kernel, name, flops=10**6, **options):
        return pl.pallas_call(
            kernel,
            compiler_params=pltpu.CompilerParams(vmem_limit_bytes=VMEM_LIMIT),
            cost_estimate=pl.CostEstimate(flops=flops, bytes_accessed=10**5, transcendentals=0),
            name=name,
            **options,
        )

    bf16, f32 = jnp.bfloat16, jnp.float32
    block, half_block = pltpu.VMEM((rows, local_width), bf16), pltpu.VMEM((rows, half_width), bf16)
    wide, half_wide = pltpu.VMEM((rows, local_width), f32), pltpu.VMEM((rows, half_width), f32)
    tiles, sums = pltpu.VMEM((group_count, rows, taps), bf16), pltpu.VMEM((group_count, taps), f32)
    turned = pltpu.VMEM((group_width, group_count * rows), bf16)
    outs = [jax.ShapeDtypeStruct((rows, local_width), bf16)] * 3

    sent = call(
        diagonal_kernel,
        "diagonal",
        in_specs=[ANYWHERE] * 4,
        out_specs=WHOLE,
        out_shape=half_block,
        scratch_shapes=[half_block] * 2 + [pltpu.SemaphoreType.DMA((4,))],
    )(*in_hbm(query, keys, values, cotangent))
    diagonal = moved(sent, "ctx", (-1, 1))
    near, across = call(
        products_kernel,
        "products",
        in_specs=[WHOLE] * 4 + [ANYWHERE],
        out_specs=[WHOLE] * 2,
        out_shape=[block] * 2,
    )(*in_vmem(query, keys, values, cotangent), sent)
    two = moved(across, "ctx", (2, -2))
    far = moved(near, "ctx", (-2, 2))
    swap = moved(across, "ctx", (1, -1))

    ready_tiles, late_tiles = call(
        functools.partial(tiles_kernel, rows),
        "tiles",
        in_specs=[WHOLE],
        out_specs=[WHOLE] * 2,
        out_shape=[tiles] * 2,
    )(*in_vmem(filter_taps))
    partial, late, ready, near_turned, across_turned = call(
        functools.partial(own_kernel, rows),
        "own",
        flops=4 * 10**9,
        in_specs=[WHOLE] * 5,
        out_specs=[WHOLE] * 5,
        out_shape=[sums, wide, wide, turned, turned],
    )(*in_vmem(ready_tiles, late_tiles, near, across, diagonal))

    partial = call(
        functools.partial(two_kernel, rows),
        "two",
        in_specs=[WHOLE] * 3,
        out_specs=WHOLE,
        out_shape=sums,
        scratch_shapes=[pltpu.VMEM((group_count, rows, rows), f32)],
    )(*in_vmem(partial, near_turned, two))
    other = moved(partial, "ctx", (1, -1))

    rest, ready_one, ready_other = call(
        ready_kernel,
        "ready",
        in_specs=[WHOLE] * 6 + [ANYWHERE],
        out_specs=[WHOLE] * 3,
        out_shape=[half_wide, half_block, half_block],
    )(*in_vmem(ready_tiles, ready, two, query, keys, values), partial)

    forwarded = call(
        forward_kernel,
        "forward",
        in_specs=[WHOLE, ANYWHERE],
        out_specs=WHOLE,
        out_shape=half_block,
    )(*in_vmem(far), rest)
    forwarded = moved(forwarded, "ctx", (1, -1))

    cross = call(
        functools.partial(cross_kernel, rows),
        "cross",
        in_specs=[WHOLE] * 2,
        out_specs=WHOLE,
        out_shape=sums,
        scratch_shapes=[pltpu.VMEM((group_count, rows, rows), f32)],
    )(*in_vmem(across_turned, swap))
    pair_sum = call(
        functools.partial(pair_kernel, factor),
        "pair",
        in_specs=[WHOLE] * 3 + [ANYWHERE],
        out_specs=WHOLE,
        out_shape=sums,
    )(*in_vmem(partial, other, cross), rest)

    known_one, known_other = call(
        known_kernel,
        "known",
        flops=4 * 10**9,
        in_specs=[WHOLE] * 7,
        out_specs=[WHOLE] * 2,
        out_shape=[block] * 2,
    )(*in_vmem(late_tiles, late, swap, far, query, keys, values))

    def add(*terms, out_shape=sums, after=known_one):
        return call(
            add_kernel,
            "add",
            in_specs=[WHOLE] * len(terms) + [ANYWHERE],
            out_specs=WHOLE,
            out_shape=out_shape,
        )(*in_vmem(*terms), after)

    terms = sum_terms(pair_sum, "ctx", add)
    gated, key_grad, value_grad, mark = call(
        last_kernel,
        "last",
        in_specs=[WHOLE] * 10,
        out_specs=[ANYWHERE] * 3 + [WHOLE],
        out_shape=outs + [pltpu.VMEM((SUBLANES, group_width), f32)],
        scratch_shapes=[half_block] * 2 + [pltpu.SemaphoreType.DMA((6 + 3 * PARTS,))],
    )(
        *in_vmem(ready_tiles, rest, forwarded, query, keys, values),
        *in_vmem(ready_one, ready_other, known_one, known_other),
    )
    whole_sums = jax.ShapeDtypeStruct((group_count, taps), f32)
    return (gated, key_grad, value_grad, add(*terms, out_shape=whole_sums, after=mark))


def solution(mesh):
    in_specs = (P("ctx", "grp"), P("ctx", "grp"), P("ctx", "grp"), P("ctx", "grp"), P("grp", None))
    out_specs = (P("ctx", "grp"), P("ctx", "grp"), P("ctx", "grp"), P("grp", None))
    return jax.shard_map(shards, mesh=mesh, in_specs=in_specs, out_specs=out_specs, check_vma=False)
```
